32 devices in a mesh: batch: 16 (over z, x, core), tensor: 2 (over y).
Axes of the slice: x: 2, y: 2, z: 4, core: 2. Of those that a mesh axis runs over, the one named last changes fastest.
Arguments:
- tokens: bfloat16 [32768, 768], P(('batch', 'tensor')), may hold values from -6 to 6
- lengths: int32 [64], P(('batch', 'tensor')), may hold values from 1 to 512, as said below
- w_query: bfloat16 [768, 768], P(None, 'tensor'), may hold values from -0.21875 to 0.21875
- b_query: bfloat16 [768], P('tensor'), may hold values from -1.796875 to 1.796875
- w_key: bfloat16 [768, 768], P(None, 'tensor'), may hold values from -0.21875 to 0.21875
- w_value: bfloat16 [768, 768], P(None, 'tensor'), may hold values from -0.21875 to 0.21875
- b_value: bfloat16 [768], P('tensor'), may hold values from -1.796875 to 1.796875
- w_out: bfloat16 [768, 768], P('tensor'), may hold values from -0.875 to 0.875
- b_out: bfloat16 [768], replicated, may hold values from -1.796875 to 1.796875
- gain_one: bfloat16 [768], replicated, may hold values from 0.25 to 1.75
- shift_one: bfloat16 [768], replicated, may hold values from -1.796875 to 1.796875
- w_up: bfloat16 [768, 3072], P(None, 'tensor'), may hold values from -0.21875 to 0.21875
- b_up: bfloat16 [3072], P('tensor'), may hold values from -3 to 3
- w_down: bfloat16 [3072, 768], P('tensor'), may hold values from -0.109375 to 0.109375
- b_down: bfloat16 [768], replicated, may hold values from -1.796875 to 1.796875
- gain_two: bfloat16 [768], replicated, may hold values from 0.25 to 1.75
- shift_two: bfloat16 [768], replicated, may hold values from -1.796875 to 1.796875
- out_grad: bfloat16 [32768, 768], P(('batch', 'tensor')), may hold values from -6 to 6
- pool_grad: float32 [64, 768], P(('batch', 'tensor')), may hold values from -6 to 6
Outputs:
- output: bfloat16 [32768, 768], P(('batch', 'tensor'))
- pooled: float32 [64, 768], P(('batch', 'tensor'))
- d_tokens: float32 [32768, 768], P(('batch', 'tensor'))
- g_query: float32 [768, 768], P(None, 'tensor')
- g_bias_query: float32 [768], P('tensor')
- g_key: float32 [768, 768], P(None, 'tensor')
- g_value: float32 [768, 768], P(None, 'tensor')
- g_bias_value: float32 [768], P('tensor')
- g_out: float32 [768, 768], P('tensor')
- g_bias_out: float32 [768], replicated
- g_gain_one: float32 [768], replicated
- g_shift_one: float32 [768], replicated
- g_up: float32 [768, 3072], P(None, 'tensor')
- g_bias_up: float32 [3072], P('tensor')
- g_down: float32 [3072, 768], P('tensor')
- g_bias_down: float32 [768], replicated
- g_gain_two: float32 [768], replicated
- g_shift_two: float32 [768], replicated
The draws below stay inside these ranges and needn't reach their ends.
Inputs may be any that keep to these rules, and one draw needn't show every extreme that they name: `lengths`: tokens at or beyond a slot's length are padding; some slot has exactly 512 tokens.
All inputs are finite; a program needn't handle non-finite values.
Results may differ from the reference program's by a relative error of at most 0.013.
The reference program's roundings to bfloat16 on the way count: a program that leaves them out, or rounds other values in their place, can miss the bound.
Values may be sent and summed in bfloat16 or wider, within the bound.
No kernel may reach another device: no remote copies, remote signals or barrier semaphores. Data moves between devices by JAX's collectives and lax.ppermute only.
A program may use at most 192 MiB of HBM per device.

```python
import jax
import jax.numpy as jnp
from jax import lax

D = 768
HEADS = 12
HD = 64
FF = 3072
LEN = 512
SEQ_DEV = 2
SEQS = 64
TOKENS = 32768
N_TENSOR = 2


def draw_lengths(key, part):
    key = jax.random.fold_in(key, 11)
    key_kind, key_short, key_long, key_place = jax.random.split(key, 4)
    kinds = jax.random.randint(key_kind, (SEQS,), 0, 2)
    short_len = jax.random.randint(key_short, (SEQS,), max(1, LEN // 64), LEN // 8 + 1)
    long_len = jax.random.randint(key_long, (SEQS,), max(1, LEN // 8), LEN + 1)
    seq_len = jnp.where(kinds == 1, long_len, short_len)
    place = jax.random.randint(key_place, (), 0, SEQS)
    seq_len = seq_len.at[place].set(LEN)
    return seq_len.astype(jnp.int32)


def steps_of(stream_key, extent, cuts, least, top_value):
    loudness, own = 1.0, jax.random.fold_in(stream_key, 6)
    for axis_at, blocks in cuts:
        heights = jnp.exp(jax.random.uniform(jax.random.fold_in(own, axis_at), (blocks,), jnp.float32, least / len(cuts), top_value / len(cuts)))
        loudness = loudness * jnp.repeat(heights, extent[axis_at] // blocks).reshape([-1 if axis == axis_at else 1 for axis in range(len(extent))])
    return loudness


def scatter_about(stream_key, extent, deviation, bound, cuts=(), kind=jnp.bfloat16):
    entries = deviation * jax.random.normal(stream_key, extent, jnp.float32)
    if cuts:
        entries = entries * steps_of(stream_key, extent, cuts, -0.22, 0.18)
    return jnp.clip(entries, -bound, bound).astype(kind)


def setup_inputs(seed: int = 0) -> dict:
    seeds = jax.random.split(jax.random.key(seed), 20)
    tokens = scatter_about(seeds[0], (TOKENS, D), 1.0, 6.0, ((0, 32),))
    lengths = draw_lengths(jax.random.fold_in(seeds[19], 71), 0)
    w_query = scatter_about(seeds[2], (D, D), D ** -0.5, 0.21875, ((1, 2),))
    b_query = scatter_about(seeds[3], (D,), 0.3, 1.796875, ((0, 2),))
    w_key = scatter_about(seeds[4], (D, D), D ** -0.5, 0.21875, ((1, 2),))
    w_value = scatter_about(seeds[5], (D, D), D ** -0.5, 0.21875, ((1, 2),))
    b_value = scatter_about(seeds[6], (D,), 0.3, 1.796875, ((0, 2),))
    w_out = scatter_about(seeds[7], (D, D), (D // 16) ** -0.5, 0.875, ((0, 2),))
    b_out = scatter_about(seeds[8], (D,), 0.3, 1.796875)
    gain_one = jnp.clip(1.0 + 0.15 * jax.random.normal(seeds[9], (D,), jnp.float32), 0.25, 1.75).astype(jnp.bfloat16)
    shift_one = scatter_about(seeds[10], (D,), 0.3, 1.796875)
    w_up = scatter_about(seeds[11], (D, FF), D ** -0.5, 0.21875, ((1, 2),))
    b_up = scatter_about(seeds[12], (FF,), 0.5, 3.0, ((0, 2),))
    w_down = scatter_about(seeds[13], (FF, D), FF ** -0.5, 0.109375, ((0, 2),))
    b_down = scatter_about(seeds[14], (D,), 0.3, 1.796875)
    gain_two = jnp.clip(1.0 + 0.15 * jax.random.normal(seeds[15], (D,), jnp.float32), 0.25, 1.75).astype(jnp.bfloat16)
    shift_two = scatter_about(seeds[16], (D,), 0.3, 1.796875)
    out_grad = scatter_about(seeds[17], (TOKENS, D), 1.0, 6.0, ((0, 32),))
    pool_grad = scatter_about(seeds[18], (SEQS, D), 1.0, 6.0, ((0, 32),), jnp.float32)
    return {"tokens": tokens, "lengths": lengths, "w_query": w_query, "b_query": b_query, "w_key": w_key, "w_value": w_value, "b_value": b_value, "w_out": w_out, "b_out": b_out, "gain_one": gain_one, "shift_one": shift_one, "w_up": w_up, "b_up": b_up, "w_down": w_down, "b_down": b_down, "gain_two": gain_two, "shift_two": shift_two, "out_grad": out_grad, "pool_grad": pool_grad}


EPSILON = 1e-12
NEG_FILL = -1e+30
HIGH = lax.Precision.HIGHEST

@jax.custom_vjp
def low(v):
    return lax.optimization_barrier(v.astype(jnp.bfloat16)).astype(jnp.float32)

@jax.custom_vjp
def low_back(v):
    return v

def low_keep(v):
    return (low(v), None)

def low_pass(kept, grad):
    return (grad,)

def back_keep(v):
    return (v, None)

def back_low(kept, grad):
    return (low(grad),)
low.defvjp(low_keep, low_pass)
low_back.defvjp(back_keep, back_low)

def matmul(left, right):
    return jnp.dot(left, right, precision=HIGH)

def layer_norm(residue, norm_gain, norm_shift):
    center = residue - lax.optimization_barrier(jnp.mean(residue, -1, keepdims=True))
    spread = lax.optimization_barrier(jnp.mean(center * center, -1, keepdims=True))
    return center * lax.rsqrt(spread + EPSILON) * norm_gain + norm_shift

def block_forward(params, block_tokens, block_lengths):
    w_query, b_query, w_key, w_value, b_value, w_out, b_out, gain_one, shift_one, w_up, b_up, w_down, b_down, gain_two, shift_two = params
    seq_block = block_tokens.shape[0]
    flat_rows = block_tokens.reshape(seq_block * LEN, D)

    def heads_of(values):
        return values.reshape(seq_block, LEN, HEADS, HD)
    query_h = heads_of(low_back(low(matmul(flat_rows, w_query) + b_query)))
    key_h = heads_of(low_back(low(matmul(flat_rows, w_key))))
    value_h = heads_of(low_back(low(matmul(flat_rows, w_value) + b_value)))
    scores = low_back(jnp.einsum('bqhd,bkhd->bhqk', query_h, key_h, precision=HIGH) * HD ** (-0.5))
    key_valid = jnp.arange(LEN)[None, :] < block_lengths[:, None]
    scores = jnp.where(key_valid[:, None, None, :], scores, NEG_FILL)
    probs = jax.nn.softmax(scores, axis=-1)
    mixed = jnp.einsum('bhqk,bkhd->bqhd', low(probs), value_h, precision=HIGH)
    mixed = low_back(low(mixed)).reshape(seq_block * LEN, D)
    attn = low_back(matmul(mixed, w_out))
    hidden_one = layer_norm(flat_rows + attn + b_out, gain_one, shift_one)
    pre_act = low_back(matmul(low(hidden_one), w_up) + b_up)
    act_low = low(jax.nn.gelu(pre_act, approximate=False))
    ffn = low_back(matmul(act_low, w_down))
    output = layer_norm(hidden_one + ffn + b_down, gain_two, shift_two)
    shaped = output.reshape(seq_block, LEN, D)
    pooled = lax.optimization_barrier(jnp.sum(jnp.where(key_valid[:, :, None], shaped, 0.0), 1)) / block_lengths[:, None].astype(output.dtype)
    return (output, pooled)

def reference(tokens, lengths, w_query, b_query, w_key, w_value, b_value, w_out, b_out, gain_one, shift_one, w_up, b_up, w_down, b_down, gain_two, shift_two, out_grad, pool_grad):
    params = tuple((weight.astype(jnp.float32) for weight in (w_query, b_query, w_key, w_value, b_value, w_out, b_out, gain_one, shift_one, w_up, b_up, w_down, b_down, gain_two, shift_two)))
    block_seqs = SEQ_DEV * N_TENSOR
    block_count = SEQS // block_seqs
    len_blocks = lengths.reshape(block_count, block_seqs)

    def whole(params_in, tokens_in):

        def scan_step(carry, inputs):
            block_tokens, block_lengths = inputs
            result = jax.checkpoint(block_forward)(params_in, block_tokens, block_lengths)
            return (carry, result)
        blocks = tokens_in.reshape(block_count, block_seqs, LEN, D)
        unused, (outs_all, pools_all) = lax.scan(scan_step, None, (blocks, len_blocks))
        return (outs_all.reshape(TOKENS, D), pools_all.reshape(SEQS, D))
    (output, pooled), pull_back = jax.vjp(whole, params, tokens.astype(jnp.float32))
    grads, d_tokens = pull_back((out_grad.astype(jnp.float32), pool_grad.astype(jnp.float32)))
    return (output.astype(jnp.bfloat16), pooled, d_tokens, grads[0], grads[1], grads[2], grads[3], grads[4], grads[5], grads[6], grads[7], grads[8], grads[9], grads[10], grads[11], grads[12], grads[13], grads[14])
```

```python
import functools

import jax
import jax.numpy as jnp
from jax import lax
from jax.experimental import pallas as pl
from jax.experimental.pallas import tpu as pltpu
from jax.sharding import PartitionSpec as P

HD = 64
EPSILON = 1e-12
NEG_FILL = -1e30
F32 = jnp.float32
BF16 = jnp.bfloat16
VMEM_LIMIT = 56 * 1024 * 1024
SQRT_HALF = 0.7071067811865476
INV_SQRT_2PI = 0.3989422804014327


def dot(left, right):
    return lax.dot_general(left, right, (((1,), (0,)), ((), ())), preferred_element_type=F32)


def dot_nt(left, right):
    return lax.dot_general(left, right, (((1,), (1,)), ((), ())), preferred_element_type=F32)


def dot_tn(left, right):
    return lax.dot_general(left, right, (((0,), (0,)), ((), ())), preferred_element_type=F32)


def call(body, name, grid, ins, outs, scratch=(), scalars=(), aliases=None, flops=0, trans=0):
    n_scalar = len(scalars)
    in_bytes = sum(a.size * a.dtype.itemsize for a, _, _ in ins)
    out_bytes = 0
    for shape, dtype, _, _ in outs:
        size = jnp.dtype(dtype).itemsize
        for extent in shape:
            size *= extent
        out_bytes += size
    return pl.pallas_call(
        body,
        name=name,
        grid_spec=pltpu.PrefetchScalarGridSpec(
            num_scalar_prefetch=n_scalar,
            grid=grid,
            in_specs=[pl.BlockSpec(b, m) for _, b, m in ins],
            out_specs=[pl.BlockSpec(b, m) for _, _, b, m in outs],
            scratch_shapes=list(scratch),
        ),
        out_shape=[jax.ShapeDtypeStruct(s, d) for s, d, _, _ in outs],
        input_output_aliases={k + n_scalar: v for k, v in (aliases or {}).items()},
        compiler_params=pltpu.CompilerParams(
            vmem_limit_bytes=VMEM_LIMIT, dimension_semantics=("arbitrary",) * len(grid)
        ),
        cost_estimate=pl.CostEstimate(
            flops=int(flops), bytes_accessed=int(in_bytes + out_bytes), transcendentals=int(trans)
        ),
    )(*scalars, *[a for a, _, _ in ins])


def whole(array):
    zeros = (0,) * array.ndim
    return (array, array.shape, lambda *_: zeros)


def whole_out(shape, dtype):
    zeros = (0,) * len(shape)
    return (shape, dtype, shape, lambda *_: zeros)


def attn_fwd_body(
    heads, first, len_ref, x_ref, wq_ref, wk_ref, wv_ref, wo_ref, bias_ref, *refs
):
    if first:
        q_ref, kt_ref, v_ref, p_ref, mt_ref, out_ref, xt_ref, vt_scr = refs
    else:
        part_ref, q_ref, kt_ref, v_ref, p_ref, mt_ref, out_ref, vt_scr = refs
    seq = pl.program_id(0)
    x = x_ref[...]
    if first:
        xt_ref[...] = x.T
    query = (dot(x, wq_ref[...]) + bias_ref[0:1, :].astype(F32)).astype(BF16)
    key = dot(x, wk_ref[...]).astype(BF16)
    value = (dot(x, wv_ref[...]) + bias_ref[1:2, :].astype(F32)).astype(BF16)
    query = query * jnp.asarray(HD**-0.5, BF16)
    q_ref[...] = query
    v_ref[...] = value
    kt_ref[...] = key.T
    vt_scr[...] = value.T
    span = x.shape[0]
    valid = lax.broadcasted_iota(jnp.int32, (span, span), 0) < len_ref[seq]
    for head in range(heads):
        cols = slice(head * HD, (head + 1) * HD)
        scores = dot_nt(key[:, cols], query[:, cols])
        scores = jnp.where(valid, scores, NEG_FILL)
        top = jnp.max(scores, axis=0, keepdims=True)
        weight = jnp.exp(scores - top)
        total = jnp.sum(weight, axis=0, keepdims=True)
        probs = (weight * (1.0 / total)).astype(BF16)
        p_ref[0, head] = probs
        mt_ref[cols, :] = dot(vt_scr[cols, :], probs).astype(BF16)
    share = dot_tn(mt_ref[...], wo_ref[...])
    if not first:
        share = share + part_ref[...]
    out_ref[...] = share


def attn_fwd(lengths, x, wq, wk, wv, wo, bias, part):
    rows, width = x.shape
    seqs = lengths.shape[0]
    span = rows // seqs
    local = wq.shape[1]
    heads = local // HD
    first = part is None
    row_blk = lambda s, *_: (s, 0)
    col_blk = lambda s, *_: (0, s)
    ins = [
        (x, (span, width), row_blk),
        whole(wq),
        whole(wk),
        whole(wv),
        whole(wo),
        whole(bias),
    ]
    outs = [
        ((rows, local), BF16, (span, local), row_blk),
        ((local, rows), BF16, (local, span), col_blk),
        ((rows, local), BF16, (span, local), row_blk),
        ((seqs, heads, span, span), BF16, (1, heads, span, span), lambda s, *_: (s, 0, 0, 0)),
        ((local, rows), BF16, (local, span), col_blk),
        ((rows, width), F32, (span, width), row_blk),
    ]
    if first:
        outs.append(((width, rows), BF16, (width, span), col_blk))
    else:
        ins.append((part, (span, width), row_blk))
    return call(
        functools.partial(attn_fwd_body, heads, first),
        "attn_fwd",
        (seqs,),
        ins,
        outs,
        scratch=[pltpu.VMEM((local, span), BF16)],
        scalars=(lengths,),
        flops=8 * rows * width * local + 16 * rows * span * local,
        trans=rows * span * heads,
    )


def norm_parts(resid):
    center = resid - jnp.mean(resid, -1, keepdims=True)
    spread = jnp.mean(center * center, -1, keepdims=True)
    rstd = lax.rsqrt(spread + EPSILON)
    return center * rstd, rstd


def norm_back(unit, rstd, gain, grad):
    scaled = grad * gain
    return rstd * (
        scaled
        - jnp.mean(scaled, -1, keepdims=True)
        - unit * jnp.mean(scaled * unit, -1, keepdims=True)
    )


def ln1_body(x_ref, attn_ref, small_ref, resid_ref, hid_ref, low_ref, lowt_ref):
    resid = x_ref[...].astype(F32) + attn_ref[...] + small_ref[0:1, :]
    unit, _ = norm_parts(resid)
    hidden = unit * small_ref[1:2, :] + small_ref[2:3, :]
    resid_ref[...] = resid
    hid_ref[...] = hidden
    low = hidden.astype(BF16)
    low_ref[...] = low
    lowt_ref[...] = low.T


def ln1(x, attn, small, blk):
    rows, width = x.shape
    row_blk = lambda s, *_: (s, 0)
    col_blk = lambda s, *_: (0, s)
    return call(
        ln1_body,
        "ln1",
        (rows // blk,),
        [(x, (blk, width), row_blk), (attn, (blk, width), row_blk), whole(small)],
        [
            ((rows, width), F32, (blk, width), row_blk),
            ((rows, width), F32, (blk, width), row_blk),
            ((rows, width), BF16, (blk, width), row_blk),
            ((width, rows), BF16, (width, blk), col_blk),
        ],
        flops=20 * rows * width,
    )


def ln2_body(
    len_ref,
    hid_ref,
    ffn_ref,
    small_ref,
    og_ref,
    pg_ref,
    out_ref,
    pool_ref,
    dres_ref,
    dlow_ref,
    dlowt_ref,
    sums_ref,
):
    seq = pl.program_id(0)
    resid = hid_ref[...] + ffn_ref[...] + small_ref[3:4, :]
    unit, rstd = norm_parts(resid)
    gain = small_ref[4:5, :]
    out = unit * gain + small_ref[5:6, :]
    out_ref[...] = out.astype(BF16)
    length = len_ref[seq]
    count = length.astype(F32)
    valid = lax.broadcasted_iota(jnp.int32, resid.shape, 0) < length
    pool_ref[0] = jnp.sum(jnp.where(valid, out, 0.0), 0, keepdims=True) / count
    spread = jnp.where(valid, pg_ref[0] / count, 0.0)
    d_out = og_ref[...].astype(F32) + spread
    d_resid = norm_back(unit, rstd, gain, d_out)
    dres_ref[...] = d_resid
    low = d_resid.astype(BF16)
    dlow_ref[...] = low
    dlowt_ref[...] = low.T

    @pl.when(seq == 0)
    def _():
        sums_ref[...] = jnp.zeros_like(sums_ref)

    sums_ref[0:1, :] += jnp.sum(d_resid, 0, keepdims=True)
    sums_ref[1:2, :] += jnp.sum(d_out * unit, 0, keepdims=True)
    sums_ref[2:3, :] += jnp.sum(d_out, 0, keepdims=True)


def ln2(lengths, hid, ffn, small, out_grad, pool_grad):
    rows, width = hid.shape
    seqs = lengths.shape[0]
    blk = rows // seqs
    row_blk = lambda s, *_: (s, 0)
    col_blk = lambda s, *_: (0, s)
    seq_blk = lambda s, *_: (s, 0, 0)
    return call(
        ln2_body,
        "ln2",
        (seqs,),
        [
            (hid, (blk, width), row_blk),
            (ffn, (blk, width), row_blk),
            whole(small),
            (out_grad, (blk, width), row_blk),
            (pool_grad.reshape(seqs, 1, width), (1, 1, width), seq_blk),
        ],
        [
            ((rows, width), BF16, (blk, width), row_blk),
            ((seqs, 1, width), F32, (1, 1, width), seq_blk),
            ((rows, width), F32, (blk, width), row_blk),
            ((rows, width), BF16, (blk, width), row_blk),
            ((width, rows), BF16, (width, blk), col_blk),
            whole_out((8, width), F32),
        ],
        scalars=(lengths,),
        flops=40 * rows * width,
    )


def ln1_back_body(resid_ref, dhid_ref, dres2_ref, small_ref, dres_ref, dlow_ref, sums_ref):
    step = pl.program_id(0)
    unit, rstd = norm_parts(resid_ref[...])
    d_hidden = dhid_ref[...] + dres2_ref[...]
    d_resid = norm_back(unit, rstd, small_ref[1:2, :], d_hidden)
    dres_ref[...] = d_resid
    dlow_ref[...] = d_resid.astype(BF16)

    @pl.when(step == 0)
    def _():
        sums_ref[...] = jnp.zeros_like(sums_ref)

    sums_ref[0:1, :] += jnp.sum(d_resid, 0, keepdims=True)
    sums_ref[1:2, :] += jnp.sum(d_hidden * unit, 0, keepdims=True)
    sums_ref[2:3, :] += jnp.sum(d_hidden, 0, keepdims=True)


def ln1_back(resid, d_hid, d_res2, small, blk):
    rows, width = resid.shape
    row_blk = lambda s, *_: (s, 0)
    return call(
        ln1_back_body,
        "ln1_back",
        (rows // blk,),
        [(a, (blk, width), row_blk) for a in (resid, d_hid, d_res2)] + [whole(small)],
        [
            ((rows, width), F32, (blk, width), row_blk),
            ((rows, width), BF16, (blk, width), row_blk),
            whole_out((8, width), F32),
        ],
        flops=30 * rows * width,
    )


def gelu_pair(pre):
    bell = jnp.exp(pre * pre * -0.5)
    t = 1.0 / (1.0 + (0.3275911 * SQRT_HALF) * jnp.abs(pre))
    poly = 0.5 * 1.061405429
    poly = poly * t + 0.5 * -1.453152027
    poly = poly * t + 0.5 * 1.421413741
    poly = poly * t + 0.5 * -0.284496736
    poly = poly * t + 0.5 * 0.254829592
    tail = poly * t * bell
    phi = jnp.where(pre >= 0.0, 1.0 - tail, tail)
    return pre * phi, phi + pre * bell * INV_SQRT_2PI


ROW_TILE = 256


def load_piece(own, step, wrefs, wu_scr, wd_scr):
    if own:
        wu_scr[...] = wrefs[0][...]
        wd_scr[...] = wrefs[1][...]
        return
    units = wu_scr.shape[1]
    width = wu_scr.shape[0]
    for at, ref in enumerate(wrefs):

        @pl.when(step == at)
        def _(ref=ref):
            wu_scr[...] = ref[0:width, :]
            for part in range(width // units):
                wd_scr[:, part * units : (part + 1) * units] = ref[
                    width + part * units : width + (part + 1) * units, :
                ]


def ffn_fwd_body(own, n_w, order, spot_ref, *refs):
    h_ref, bias_ref, *refs = refs
    wrefs = refs[:n_w]
    refs = refs[n_w:]
    if own:
        act_ref, der_ref, acc_ref, wu_scr, wd_scr = refs
    else:
        part_ref, act_ref, der_ref, acc_ref, wu_scr, wd_scr = refs
    step = pl.program_id(0)
    load_piece(own, step, wrefs, wu_scr, wd_scr)
    spot = spot_ref[0] ^ order(step)
    bias = bias_ref[pl.ds(2 + spot, 1), :]
    rows = h_ref.shape[0]

    @pl.when(step == 0)
    def _():
        if own:
            acc_ref[...] = jnp.zeros_like(acc_ref)
        else:
            acc_ref[...] = part_ref[...]

    for at in range(rows // ROW_TILE):
        rs = slice(at * ROW_TILE, (at + 1) * ROW_TILE)
        pre = dot(h_ref[rs, :], wu_scr[...]) + bias
        act, der = gelu_pair(pre)
        act = act.astype(BF16)
        act_ref[0, rs, :] = act
        der_ref[0, rs, :] = der.astype(BF16)
        acc_ref[rs, :] += dot(act, wd_scr[...])


def piece_inputs(own, spot_order, wu, wd, packs, units, width):
    if own:
        return [
            (wu, (width, units), lambda i, spot: (0, spot[0] ^ spot_order(i))),
            (wd, (units, width), lambda i, spot: (spot[0] ^ spot_order(i), 0)),
        ]
    return [whole(p) for p in packs]


def ffn_fwd(spot, h, bias, wu=None, wd=None, packs=(), order=lambda i: i, part=None):
    rows, width = h.shape
    own = wu is not None
    units = (wu.shape[1] // 4) if own else packs[0].shape[1]
    steps = 4 if own else len(packs)
    ws = piece_inputs(own, order, wu, wd, packs, units, width)
    ins = [whole(h), whole(bias)] + ws
    if not own:
        ins.append(whole(part))
    piece_blk = lambda i, *_: (i, 0, 0)
    return call(
        functools.partial(ffn_fwd_body, own, len(ws), order),
        "ffn_fwd",
        (steps,),
        ins,
        [
            ((steps, rows, units), BF16, (1, rows, units), piece_blk),
            ((steps, rows, units), BF16, (1, rows, units), piece_blk),
            whole_out((rows, width), F32),
        ],
        scratch=[pltpu.VMEM((width, units), BF16), pltpu.VMEM((units, width), BF16)],
        scalars=(spot,),
        flops=4 * rows * width * units * steps,
        trans=2 * rows * units * steps,
    )


def ffn_bwd_body(own, n_w, n_recv, order, base, spot_ref, *refs):
    (df_ref, dft_ref, ht_ref, act_ref, der_ref, dh_in, bs_in, *refs) = refs
    wrefs, refs = refs[:n_w], refs[n_w:]
    recv, refs = refs[:n_recv], refs[n_recv:]
    up_ref, down_ref, dh_ref, bs_ref, wu_scr, wd_scr, dpre_scr = refs
    step = pl.program_id(0)
    load_piece(own, step, wrefs, wu_scr, wd_scr)
    spot = spot_ref[0] ^ order(step)
    rows = df_ref.shape[0]

    @pl.when(step == 0)
    def _():
        dh_ref[...] = dh_in[...]
        bs_ref[...] = bs_in[...]

    bias = jnp.zeros((1, wu_scr.shape[1]), F32)
    for at in range(rows // ROW_TILE):
        rs = slice(at * ROW_TILE, (at + 1) * ROW_TILE)
        d_act = dot_nt(df_ref[rs, :], wd_scr[...])
        d_pre = (der_ref[0, rs, :].astype(F32) * d_act).astype(BF16)
        dpre_scr[rs, :] = d_pre
        bias = bias + jnp.sum(d_pre.astype(F32), 0, keepdims=True)
        dh_ref[rs, :] += dot_nt(d_pre, wu_scr[...])
    bs_ref[pl.ds(base + spot, 1), :] = bias
    up = dot(ht_ref[...], dpre_scr[...])
    down = dot(dft_ref[...], act_ref[0])
    if n_recv:
        up = up + recv[0][0].astype(F32)
        down = down + recv[1][0].astype(F32)
    up_ref[0] = up.astype(BF16)
    down_ref[0] = down.astype(BF16)


def ffn_bwd(spot, df, dft, ht, act, der, dh, bs, base, order, wu=None, wd=None, packs=(), recv=(), at=0):
    rows, width = df.shape
    own = wu is not None
    units = act.shape[2]
    steps = 2
    ws = piece_inputs(own, order, wu, wd, packs, units, width)
    act_blk = lambda i, *_: (at(i), 0, 0)
    piece_blk = lambda i, *_: (i, 0, 0)
    ins = [
        whole(df),
        whole(dft),
        whole(ht),
        (act, (1, rows, units), act_blk),
        (der, (1, rows, units), act_blk),
        whole(dh),
        whole(bs),
    ]
    ins += ws
    ins += [(r, (1, width, units), piece_blk) for r in recv]
    return call(
        functools.partial(ffn_bwd_body, own, len(ws), len(recv), order, base),
        "ffn_bwd",
        (steps,),
        ins,
        [
            ((steps, width, units), BF16, (1, width, units), piece_blk),
            ((steps, width, units), BF16, (1, width, units), piece_blk),
            whole_out((rows, width), F32),
            whole_out(bs.shape, F32),
        ],
        scratch=[
            pltpu.VMEM((width, units), BF16),
            pltpu.VMEM((units, width), BF16),
            pltpu.VMEM((rows, units), BF16),
        ],
        scalars=(spot,),
        aliases={5: 2, 6: 3},
        flops=8 * rows * width * units * steps,
    )


def attn_bwd_body(
    heads,
    spot_ref,
    da_ref,
    xt_ref,
    wq_ref,
    wk_ref,
    wv_ref,
    wo_ref,
    q_ref,
    kt_ref,
    v_ref,
    p_ref,
    mt_ref,
    dx_in,
    keep_ref,
    send_ref,
    dx_ref,
    sums_ref,
    g_scr,
    dqt_scr,
    dk_scr,
    dv_scr,
):
    seq = pl.program_id(0)
    last = pl.num_programs(0) - 1
    scale = HD**-0.5

    @pl.when(seq == 0)
    def _():
        g_scr[...] = jnp.zeros_like(g_scr)
        sums_ref[...] = jnp.zeros_like(sums_ref)

    d_attn = da_ref[...]
    d_mixed = dot_nt(d_attn, wo_ref[...]).astype(BF16)
    local = d_mixed.shape[1]
    width = d_attn.shape[1]
    g_out = dot(mt_ref[...], d_attn)
    for part in range(width // local):
        g_scr[3, part * local : (part + 1) * local, :] += g_out[:, part * local : (part + 1) * local]
    for head in range(heads):
        cols = slice(head * HD, (head + 1) * HD)
        d_mixed_h = d_mixed[:, cols]
        d_probs = dot_nt(v_ref[:, cols], d_mixed_h)
        low_probs = p_ref[0, head]
        probs = low_probs.astype(F32)
        inner = jnp.sum(d_probs * probs, axis=0, keepdims=True)
        d_scores = (probs * (d_probs - inner)).astype(BF16)
        dv_scr[:, cols] = dot(low_probs, d_mixed_h).astype(BF16)
        dk_scr[:, cols] = dot(d_scores, q_ref[:, cols]).astype(BF16)
        dqt_scr[cols, :] = (dot(kt_ref[cols, :], d_scores) * scale).astype(BF16)
    d_query = dqt_scr[...].T
    d_key = dk_scr[...]
    d_value = dv_scr[...]
    xt = xt_ref[...]
    g_scr[0] += dot(xt, d_query)
    g_scr[1] += dot(xt, d_key)
    g_scr[2] += dot(xt, d_value)
    sums_ref[0:1, :] += jnp.sum(d_query.astype(F32), 0, keepdims=True)
    sums_ref[1:2, :] += jnp.sum(d_value.astype(F32), 0, keepdims=True)
    dx_ref[...] = (
        dx_in[...]
        + dot_nt(d_query, wq_ref[...])
        + dot_nt(d_key, wk_ref[...])
        + dot_nt(d_value, wv_ref[...])
    )

    @pl.when(seq == last)
    def _():
        spot = spot_ref[0]
        for mat in range(4):
            rel = spot ^ mat

            @pl.when((rel & 1) == 0)
            def _(mat=mat, rel=rel):
                keep_ref[rel >> 1] = g_scr[mat].astype(BF16)

            @pl.when((rel & 1) == 1)
            def _(mat=mat, rel=rel):
                send_ref[rel >> 1] = g_scr[mat].astype(BF16)


def attn_bwd(spot, seqs, d_attn, xt, wq, wk, wv, wo, saved, dx):
    q, kt, v, probs, mt = saved
    rows, width = d_attn.shape
    span = rows // seqs
    local = wq.shape[1]
    heads = local // HD
    row_blk = lambda s, *_: (s, 0)
    col_blk = lambda s, *_: (0, s)
    ins = [
        (d_attn, (span, width), row_blk),
        (xt, (width, span), col_blk),
        whole(wq),
        whole(wk),
        whole(wv),
        whole(wo),
        (q, (span, local), row_blk),
        (kt, (local, span), col_blk),
        (v, (span, local), row_blk),
        (probs, (1, heads, span, span), lambda s, *_: (s, 0, 0, 0)),
        (mt, (local, span), col_blk),
        (dx, (span, width), row_blk),
    ]
    return call(
        functools.partial(attn_bwd_body, heads),
        "attn_bwd",
        (seqs,),
        ins,
        [
            whole_out((2, width, local), BF16),
            whole_out((2, width, local), BF16),
            ((rows, width), F32, (span, width), row_blk),
            whole_out((8, local), F32),
        ],
        scratch=[
            pltpu.VMEM((4, width, local), F32),
            pltpu.VMEM((local, span), BF16),
            pltpu.VMEM((span, local), BF16),
            pltpu.VMEM((span, local), BF16),
        ],
        scalars=(spot,),
        flops=16 * rows * width * local + 40 * rows * span * local,
    )


def assemble_body(spot_ref, p0, p1, p2, p3, wq_ref, wk_ref, wv_ref, wo_ref, bias_ref):
    local = wq_ref.shape[1]
    rows = wq_ref.shape[0] // 4
    outs = wo_ref.shape[0] // 4
    for rel, piece in enumerate((p0, p1, p2, p3)):
        spot = spot_ref[0] ^ rel
        at = pl.ds(pl.multiple_of(spot * rows, rows), rows)
        wq_ref[at, :] = piece[0:rows, :]
        wk_ref[at, :] = piece[rows : 2 * rows, :]
        wv_ref[at, :] = piece[2 * rows : 3 * rows, :]
        out_at = pl.ds(pl.multiple_of(spot * outs, outs), outs)
        for part in range(wo_ref.shape[1] // local):
            begin = 3 * rows + part * outs
            wo_ref[out_at, part * local : (part + 1) * local] = piece[begin : begin + outs, :]
    tail = 3 * rows + (wo_ref.shape[1] // local) * outs
    bias_ref[...] = p0[tail : tail + bias_ref.shape[0], :].astype(F32)


def assemble(spot, pieces, width, local):
    return call(
        assemble_body,
        "assemble",
        (1,),
        [whole(p) for p in pieces],
        [
            whole_out((width, local), BF16),
            whole_out((width, local), BF16),
            whole_out((width, local), BF16),
            whole_out((local, width), BF16),
            whole_out((16, local), F32),
        ],
        scalars=(spot,),
    )


def finish_ffn_body(spot_ref, u0, u1, u2, u3, d0, d1, d2, d3, up_ref, down_ref):
    step = pl.program_id(0)
    for at, (up, down) in enumerate(((u0, d0), (u1, d1), (u2, d2), (u3, d3))):

        @pl.when(step == at)
        def _(up=up, down=down):
            up_ref[...] = up[...].astype(F32)
            down_ref[...] = down[...].astype(F32).T


def finish_ffn(spot, ups, downs):
    width, units = ups[0].shape
    return call(
        finish_ffn_body,
        "finish_ffn",
        (4,),
        [whole(a) for a in (*ups, *downs)],
        [
            ((width, 4 * units), F32, (width, units), lambda i, spot: (0, spot[0] ^ i)),
            ((4 * units, width), F32, (units, width), lambda i, spot: (spot[0] ^ i, 0)),
        ],
        scalars=(spot,),
    )


def finish_attn_body(spot_ref, p0, p1, p2, p3, gq_ref, gk_ref, gv_ref, go_ref):
    local = gq_ref.shape[1]
    for rel, piece in enumerate((p0, p1, p2, p3)):
        spot = spot_ref[0] ^ rel
        for mat, ref in enumerate((gq_ref, gk_ref, gv_ref)):

            @pl.when(spot == mat)
            def _(piece=piece, ref=ref):
                ref[...] = piece[...].astype(F32)

        @pl.when(spot == 3)
        def _(piece=piece):
            for part in range(go_ref.shape[1] // local):
                cols = slice(part * local, (part + 1) * local)
                go_ref[:, cols] = piece[cols, :].astype(F32)


def finish_attn(spot, pieces):
    width, local = pieces[0].shape
    return call(
        finish_attn_body,
        "finish_attn",
        (1,),
        [whole(p) for p in pieces],
        [
            whole_out((width, local), F32),
            whole_out((width, local), F32),
            whole_out((width, local), F32),
            whole_out((local, width), F32),
        ],
        scalars=(spot,),
    )


def local(
    n_batch,
    tokens,
    lengths,
    w_query,
    b_query,
    w_key,
    w_value,
    b_value,
    w_out,
    b_out,
    gain_one,
    shift_one,
    w_up,
    b_up,
    w_down,
    b_down,
    gain_two,
    shift_two,
    out_grad,
    pool_grad,
):
    rows, width = tokens.shape
    seqs = lengths.shape[0]
    span = rows // seqs
    half = w_query.shape[1]
    place = lax.axis_index("batch")
    quarter = place & 3
    spot = quarter.astype(jnp.int32).reshape(1)
    z_low = (place >> 2) & 1
    z_high = (place >> 3) & 1

    def swap(array, bit):
        return lax.ppermute(array, "batch", [(i, i ^ bit) for i in range(n_batch)])

    def swap_core(array):
        return swap(array, 1)

    def swap_x(array):
        return swap(array, 2)

    def swap_y(array):
        return lax.ppermute(array, "tensor", [(0, 1), (1, 0)])

    def quarter_rows(array):
        extent = array.shape[0] // 4
        return lax.dynamic_slice_in_dim(array, quarter * extent, extent, 0)

    def fold(array):
        return [array[:, at : at + half] for at in range(0, array.shape[1], half)]

    bias_rows = jnp.concatenate([b_query, b_value, b_up]).reshape(-1, half)
    bias_rows = jnp.pad(bias_rows, ((0, 16 - bias_rows.shape[0]), (0, 0)))
    attn_pack = jnp.concatenate(
        [quarter_rows(w_query), quarter_rows(w_key), quarter_rows(w_value)]
        + fold(quarter_rows(w_out))
        + [bias_rows],
        axis=0,
    )
    ffn_pack = jnp.concatenate(
        [lax.dynamic_slice_in_dim(w_up, quarter * half, half, 1)] + fold(quarter_rows(w_down)),
        axis=0,
    )
    attn_0 = swap_y(attn_pack)
    ffn_0 = swap_y(ffn_pack)
    attn_2 = swap_x(attn_0)
    attn_1 = swap_core(attn_0)
    attn_3 = swap_core(attn_2)
    ffn_2 = swap_x(ffn_0)
    ffn_1 = swap_core(ffn_0)
    ffn_3 = swap_core(ffn_2)

    small = jnp.stack([b_out, gain_one, shift_one, b_down, gain_two, shift_two]).astype(F32)
    own_bias = bias_rows.astype(F32)

    *own_saved, attn_part, xt = attn_fwd(
        lengths, tokens, w_query, w_key, w_value, w_out, own_bias, None
    )
    far_q, far_k, far_v, far_o, far_bias = assemble(
        spot, (attn_0, attn_1, attn_2, attn_3), width, half
    )
    *far_saved, attn_sum = attn_fwd(lengths, tokens, far_q, far_k, far_v, far_o, far_bias, attn_part)
    resid_one, hidden, hidden_low, hidden_t = ln1(tokens, attn_sum, small, span)

    own_act, own_der, ffn_part = ffn_fwd(spot, hidden_low, own_bias, wu=w_up, wd=w_down)
    far_act, far_der, ffn_sum = ffn_fwd(
        spot, hidden_low, far_bias, packs=(ffn_0, ffn_1, ffn_2, ffn_3), part=ffn_part
    )
    output, pooled, d_resid_two, d_ffn, d_ffn_t, sums_two = ln2(
        lengths, hidden, ffn_sum, small, out_grad, pool_grad
    )

    d_hidden = jnp.zeros((rows, width), F32)
    bias_sums = jnp.zeros((8, half), F32)
    common = (d_ffn, d_ffn_t, hidden_t)
    send = lambda i: 2 * i + 1
    keep = lambda i: 2 * i
    fu, fd, d_hidden, bias_sums = ffn_bwd(
        spot, *common, far_act, far_der, d_hidden, bias_sums, 4, send, packs=(ffn_1, ffn_3), at=send
    )
    fu, fd = swap_core(fu), swap_core(fd)
    ou, od, d_hidden, bias_sums = ffn_bwd(
        spot, *common, own_act, own_der, d_hidden, bias_sums, 0, send, wu=w_up, wd=w_down, at=send
    )
    ou, od = swap_core(ou), swap_core(od)
    fu, fd, d_hidden, bias_sums = ffn_bwd(
        spot,
        *common,
        far_act,
        far_der,
        d_hidden,
        bias_sums,
        4,
        keep,
        packs=(ffn_0, ffn_2),
        recv=(fu, fd),
        at=keep,
    )
    ou, od, d_hidden, bias_sums = ffn_bwd(
        spot,
        *common,
        own_act,
        own_der,
        d_hidden,
        bias_sums,
        0,
        keep,
        wu=w_up,
        wd=w_down,
        recv=(ou, od),
        at=keep,
    )

    def add(*terms):
        total = terms[0].astype(F32)
        for term in terms[1:]:
            total = total + term.astype(F32)
        return total.astype(BF16)

    def over_z(piece):
        extent = piece.shape[0] // 4
        parts = piece.reshape(2, 2, extent, half)
        take = lambda a, axis, at: lax.dynamic_index_in_dim(a, at, axis, keepdims=False)
        got = swap(take(parts, 1, 1 - z_low), 4)
        parts = add(take(parts, 1, z_low), got)
        got = swap(take(parts, 0, 1 - z_high), 8)
        part = add(take(parts, 0, z_high), got)
        bit = 16
        while bit < n_batch:
            part = add(part, swap(part, bit))
            bit *= 2
        got = swap(part, 8)
        both = jnp.where(z_high == 0, jnp.stack([part, got]), jnp.stack([got, part]))
        got = swap(both, 4)
        full = jnp.where(z_low == 0, jnp.stack([both, got], 1), jnp.stack([got, both], 1))
        return full.reshape(piece.shape)

    def gather_back(piece_0):
        piece_2 = swap_x(piece_0)
        piece_1 = swap_core(piece_0)
        piece_3 = swap_core(piece_2)
        return piece_0, piece_1, piece_2, piece_3

    def reduce_y_first(own, far):
        own = add(own, swap_y(far))
        return gather_back(over_z(add(own[0], swap_x(own[1]))))

    def reduce_x_first(own, far):
        far = add(far[0], swap_x(far[1]))
        own = add(own[0], swap_x(own[1]))
        return gather_back(over_z(add(own, swap_y(far))))

    ups = reduce_y_first(ou, fu)
    downs = reduce_x_first(od, fd)
    g_up, g_down = finish_ffn(spot, ups, downs)

    d_resid_one, d_attn, sums_one = ln1_back(resid_one, d_hidden, d_resid_two, small, span)
    far_keep, far_send, dx, far_sums = attn_bwd(
        spot, seqs, d_attn, xt, far_q, far_k, far_v, far_o, far_saved, d_resid_one
    )
    far = add(far_keep, swap_core(far_send))
    own_keep, own_send, d_tokens, own_sums = attn_bwd(
        spot, seqs, d_attn, xt, w_query, w_key, w_value, w_out, own_saved, dx
    )
    own = add(own_keep, swap_core(own_send))
    g_query, g_key, g_value, g_out = finish_attn(spot, reduce_y_first(own, far))

    shared = jnp.concatenate([sums_one[:3].reshape(-1), sums_two[:3].reshape(-1)])
    own_vec = jnp.concatenate([bias_sums[:4].reshape(-1), own_sums[:2].reshape(-1)])
    far_vec = jnp.concatenate([bias_sums[4:].reshape(-1), far_sums[:2].reshape(-1)])
    vec = jnp.concatenate([own_vec, shared]) + swap_y(jnp.concatenate([far_vec, shared]))
    bit = 1
    while bit < n_batch:
        vec = vec + swap(vec, bit)
        bit *= 2
    cuts = [4 * half, 5 * half, 6 * half] + [6 * half + width * i for i in range(1, 6)]
    (
        g_bias_up,
        g_bias_query,
        g_bias_value,
        d_bias_out,
        d_gain_one,
        d_shift_one,
        d_bias_down,
        d_gain_two,
        d_shift_two,
    ) = jnp.split(vec, cuts)
    return (
        output,
        pooled.reshape(seqs, width),
        d_tokens,
        g_query,
        g_bias_query,
        g_key,
        g_value,
        g_bias_value,
        g_out,
        d_bias_out,
        d_gain_one,
        d_shift_one,
        g_up,
        g_bias_up,
        g_down,
        d_bias_down,
        d_gain_two,
        d_shift_two,
    )


def solution(mesh):
    return jax.shard_map(
        functools.partial(local, mesh.shape["batch"]),
        mesh=mesh,
        in_specs=(
            P(("batch", "tensor"), None),
            P(("batch", "tensor")),
            P(None, "tensor"),
            P("tensor"),
            P(None, "tensor"),
            P(None, "tensor"),
            P("tensor"),
            P("tensor", None),
            P(),
            P(),
            P(),
            P(None, "tensor"),
            P("tensor"),
            P("tensor", None),
            P(),
            P(),
            P(),
            P(("batch", "tensor"), None),
            P(("batch", "tensor"), None),
        ),
        out_specs=(
            P(("batch", "tensor"), None),
            P(("batch", "tensor"), None),
            P(("batch", "tensor"), None),
            P(None, "tensor"),
            P("tensor"),
            P(None, "tensor"),
            P(None, "tensor"),
            P("tensor"),
            P("tensor", None),
            P(),
            P(),
            P(),
            P(None, "tensor"),
            P("tensor"),
            P("tensor", None),
            P(),
            P(),
            P(),
        ),
        check_vma=False,
    )
```

```python
import functools

import jax
import jax.numpy as jnp
from jax import lax
from jax.experimental import pallas as pl
from jax.experimental.pallas import tpu as pltpu
from jax.sharding import PartitionSpec as P

HD = 64
EPSILON = 1e-12
NEG_FILL = -1e30
F32 = jnp.float32
BF16 = jnp.bfloat16
MIB = 1024 * 1024
SQRT_HALF = 0.7071067811865476
INV_SQRT_2PI = 0.3989422804014327


def dot(left, right):
    return lax.dot_general(left, right, (((1,), (0,)), ((), ())), preferred_element_type=F32)


def dot_nt(left, right):
    return lax.dot_general(left, right, (((1,), (1,)), ((), ())), preferred_element_type=F32)


def dot_tn(left, right):
    return lax.dot_general(left, right, (((0,), (0,)), ((), ())), preferred_element_type=F32)


class Part:
    def __init__(self, buf):
        self.buf = buf

    def __call__(self, part=None):
        return self.buf

    def send(self, part=0):
        pass


def hbm(shape, dtype):
    return (shape, dtype, pltpu.HBM)


def resident_call(body, name, ins, outs, scalars=(), scratch=(), aliases=None, limit=12, flops=0, trans=0):
    spaces = [entry[1] if isinstance(entry, tuple) else pltpu.VMEM for entry in ins]
    arrays = [entry[0] if isinstance(entry, tuple) else entry for entry in ins]
    out_spaces = [entry[2] if len(entry) == 3 else pltpu.VMEM for entry in outs]
    moved = sum(a.size * a.dtype.itemsize for a in arrays) // 4
    spec = lambda space: pl.BlockSpec(memory_space=space)
    return pl.pallas_call(
        body,
        name=name,
        in_specs=[spec(pltpu.SMEM)] * len(scalars) + [spec(space) for space in spaces],
        out_specs=[spec(space) for space in out_spaces],
        scratch_shapes=list(scratch),
        out_shape=[space(entry[0], entry[1]) for entry, space in zip(outs, out_spaces)],
        input_output_aliases={k + len(scalars): v for k, v in (aliases or {}).items()},
        compiler_params=pltpu.CompilerParams(vmem_limit_bytes=limit * MIB),
        cost_estimate=pl.CostEstimate(
            flops=int(flops), bytes_accessed=int(moved), transcendentals=int(trans)
        ),
    )(*scalars, *[pltpu.with_memory_space_constraint(a, space) for a, space in zip(arrays, spaces)])


def stream_call(body, name, loads, stores, scalars=(), scratch=(), limit=12, flops=0, trans=0):
    arrays, slot, views = [], [], []
    for entry in loads:
        known = [at for at, array in enumerate(arrays) if array is entry[0]]
        if not known:
            arrays.append(entry[0])
        slot.append(known[0] if known else len(arrays) - 1)
        views.append(entry[3] if len(entry) == 4 else lambda ref, *_: ref)
    n_scalar, n_store = len(scalars), len(stores)

    def kernel(*refs):
        scalar_refs, refs = refs[:n_scalar], refs[n_scalar:]
        sources, refs = refs[: len(arrays)], refs[len(arrays) :]
        targets, rest = refs[:n_store], refs[n_store:]
        ins = [Part(view(sources[which], *scalar_refs)) for view, which in zip(views, slot)]
        body(scalar_refs, ins, [Part(ref) for ref in targets], *rest)

    return resident_call(
        kernel,
        name,
        arrays,
        [(shape, dtype) for shape, dtype, _ in stores],
        scalars=scalars,
        scratch=scratch,
        limit=limit,
        flops=flops,
        trans=trans,
    )


def at_index(index):
    return lambda ref, *_: ref.at[index]


def groups_of(local):
    first = local * 2 // 3
    return ((0, first), (first, local - first))


def qkv_column(local, mat, column):
    (_, first), (_, second) = groups_of(local)
    if column < first:
        return mat * first + column
    return 3 * first + mat * second + column - first


def pack_body(spot_ref, wq, wk, wv, wo, bias, ex_ref, ez_ref, qkv_ref):
    core, x_bit, z_bit = spot_ref[0], spot_ref[1], spot_ref[2]
    width, local = wq.shape
    rows = width // 2
    outs = wo.shape[0] // 2
    mine = pl.ds(pl.multiple_of(core * rows, rows), rows)
    mine_out = pl.ds(pl.multiple_of(core * outs, outs), outs)

    @pl.when(x_bit == 0)
    def _():
        ex_ref[...] = wq[mine, :]

    @pl.when(x_bit == 1)
    def _():
        ex_ref[...] = wk[mine, :]

    @pl.when(z_bit == 0)
    def _():
        ez_ref[0:rows, :] = wv[mine, :]

    @pl.when(z_bit == 1)
    def _():
        for part in range(width // local):
            ez_ref[part * outs : (part + 1) * outs, :] = wo[mine_out, part * local : (part + 1) * local]

    ez_ref[rows:, :] = bias[...]
    for begin, extent in groups_of(local):
        for mat, ref in enumerate((wq, wk, wv)):
            to = qkv_column(local, mat, begin)
            qkv_ref[:, to : to + extent] = ref[:, begin : begin + extent]


def pack(spot, wq, wk, wv, wo, bias):
    width, local = wq.shape
    return resident_call(
        pack_body,
        "pack",
        [wq, wk, wv, wo, bias],
        [
            ((width // 2, local), BF16),
            ((width // 2 + bias.shape[0], local), BF16),
            ((width, 3 * local), BF16),
        ],
        scalars=(spot,),
    )


def assemble_body(spot_ref, *refs):
    pieces, (qkv_ref, wo_ref, bias_ref) = refs[:8], refs[8:]
    core, x_bit, z_bit = spot_ref[0], spot_ref[1], spot_ref[2]
    local, width = wo_ref.shape
    rows = width // 2
    outs = local // 2

    def put(piece, at, mat):
        for begin, extent in groups_of(local):
            to = qkv_column(local, mat, begin)
            qkv_ref[at, to : to + extent] = piece[0:rows, begin : begin + extent]

    for c_flip in range(2):
        spot = core ^ c_flip
        at = pl.ds(pl.multiple_of(spot * rows, rows), rows)
        out_at = pl.ds(pl.multiple_of(spot * outs, outs), outs)
        for flip in range(2):
            piece = pieces[2 * c_flip + flip]
            for mat in range(2):

                @pl.when((x_bit ^ flip) == mat)
                def _(piece=piece, at=at, mat=mat):
                    put(piece, at, mat)

            piece = pieces[4 + 2 * c_flip + flip]

            @pl.when((z_bit ^ flip) == 0)
            def _(piece=piece, at=at):
                put(piece, at, 2)

            @pl.when((z_bit ^ flip) == 1)
            def _(piece=piece, out_at=out_at):
                for part in range(width // local):
                    cols = slice(part * local, (part + 1) * local)
                    wo_ref[out_at, cols] = piece[part * outs : (part + 1) * outs, :]

    bias_ref[...] = pieces[4][rows : rows + bias_ref.shape[0], :].astype(F32)


def assemble(spot, pieces, width, local):
    return resident_call(
        assemble_body,
        "assemble",
        list(pieces),
        [((width, 3 * local), BF16), ((local, width), BF16), ((16, local), F32)],
        scalars=(spot,),
    )


SLOTS = 4


def attn_fwd_body(seqs, heads, first, len_ref, x_ref, wqkv_ref, wo_ref, bias_ref, *refs):
    if first:
        q_ref, kt_ref, v_ref, mt_ref, pa_hbm, pb_hbm, out_ref, xt_ref, *refs = refs
    else:
        part_ref, small_ref, *refs = refs
        q_ref, kt_ref, v_ref, mt_ref, pa_hbm, pb_hbm, out_ref, low_ref, lowt_ref, *refs = refs
    k_scr, vt_scr, p_scr, sems = refs
    local = wo_ref.shape[0]
    span = x_ref.shape[0] // seqs
    heads_a = groups_of(local)[0][1] // HD

    def save(at):
        seq, head = at // heads, at % heads
        dst = pa_hbm.at[seq, head] if head < heads_a else pb_hbm.at[seq, head - heads_a]
        return pltpu.make_async_copy(p_scr.at[at % SLOTS], dst, sems.at[at % SLOTS])

    for seq in range(seqs):
        rs = slice(seq * span, (seq + 1) * span)
        x = x_ref[rs, :]
        if first:
            xt_ref[:, rs] = x.T
        qkv = dot(x, wqkv_ref[...])
        for begin, extent in groups_of(local):
            cols = slice(begin, begin + extent)

            def take(mat):
                at = qkv_column(local, mat, begin)
                return qkv[:, at : at + extent]

            query = (take(0) + bias_ref[0:1, cols]).astype(BF16)
            q_ref[rs, cols] = query * jnp.asarray(HD**-0.5, BF16)
            k_scr[:, cols] = take(1).astype(BF16)
            v_ref[rs, cols] = (take(2) + bias_ref[1:2, cols]).astype(BF16)
        kt_ref[:, rs] = k_scr[...].T
        vt_scr[...] = v_ref[rs, :].T
        valid = lax.broadcasted_iota(jnp.int32, (span, span), 0) < len_ref[seq]
        for head in range(heads):
            at = seq * heads + head
            cols = slice(head * HD, (head + 1) * HD)
            scores = dot_nt(k_scr[:, cols], q_ref[rs, cols])
            scores = jnp.where(valid, scores, NEG_FILL)
            top = jnp.max(scores, axis=0, keepdims=True)
            weight = jnp.exp(scores - top)
            total = jnp.sum(weight, axis=0, keepdims=True)
            probs = (weight * (1.0 / total)).astype(BF16)
            if at >= SLOTS:
                save(at - SLOTS).wait()
            p_scr[at % SLOTS] = probs
            save(at).start()
            mt_ref[cols, rs] = dot(vt_scr[cols, :], probs).astype(BF16)
        share = dot_tn(mt_ref[:, rs], wo_ref[...])
        if first:
            out_ref[rs, :] = share
        else:
            resid = x.astype(F32) + share + part_ref[rs, :] + small_ref[0:1, :]
            unit, _ = norm_parts(resid)
            low = (unit * small_ref[1:2, :] + small_ref[2:3, :]).astype(BF16)
            out_ref[rs, :] = resid
            low_ref[rs, :] = low
            lowt_ref[:, rs] = low.T
    for at in range(seqs * heads - SLOTS, seqs * heads):
        save(at).wait()


def attn_fwd(lengths, x, wqkv, wo, bias, part=None, small=None):
    rows, width = x.shape
    seqs = lengths.shape[0]
    span = rows // seqs
    local = wo.shape[0]
    heads = local // HD
    (_, extent_a), (_, extent_b) = groups_of(local)
    first = part is None
    ins = [x, wqkv, wo, bias] + ([] if first else [part, small])
    outs = [
        ((rows, local), BF16),
        ((local, rows), BF16),
        ((rows, local), BF16),
        ((local, rows), BF16),
        hbm((seqs, extent_a // HD, span, span), BF16),
        hbm((seqs, extent_b // HD, span, span), BF16),
        ((rows, width), F32),
    ]
    if not first:
        outs.append(((rows, width), BF16))
    outs.append(((width, rows), BF16))
    return resident_call(
        functools.partial(attn_fwd_body, seqs, heads, first),
        "attn_fwd",
        ins,
        outs,
        scratch=[
            pltpu.VMEM((span, local), BF16),
            pltpu.VMEM((local, span), BF16),
            pltpu.VMEM((SLOTS, span, span), BF16),
            pltpu.SemaphoreType.DMA((SLOTS,)),
        ],
        limit=16,
        scalars=(lengths,),
        flops=8 * rows * width * local + 16 * rows * span * local,
        trans=rows * span * heads,
    )


def norm_parts(resid):
    center = resid - jnp.mean(resid, -1, keepdims=True)
    spread = jnp.mean(center * center, -1, keepdims=True)
    rstd = lax.rsqrt(spread + EPSILON)
    return center * rstd, rstd


def norm_back(unit, rstd, gain, grad):
    scaled = grad * gain
    return rstd * (
        scaled
        - jnp.mean(scaled, -1, keepdims=True)
        - unit * jnp.mean(scaled * unit, -1, keepdims=True)
    )


def ln2_body(
    seqs,
    len_ref,
    res1_ref,
    ffn_ref,
    small_ref,
    og_ref,
    pg_ref,
    out_ref,
    pool_ref,
    dres_ref,
    dlow_ref,
    dlowt_ref,
    sums_ref,
):
    span = res1_ref.shape[0] // seqs
    tile = span // 2
    sums = [0.0, 0.0, 0.0]
    gain = small_ref[4:5, :]
    for seq in range(seqs):
        length = len_ref[seq]
        count = length.astype(F32)
        pool = 0.0
        spread = pg_ref[seq : seq + 1, :] / count
        for part in range(2):
            rs = slice(seq * span + part * tile, seq * span + (part + 1) * tile)
            unit_one, _ = norm_parts(res1_ref[rs, :])
            hidden = unit_one * small_ref[1:2, :] + small_ref[2:3, :]
            resid = hidden + ffn_ref[rs, :] + small_ref[3:4, :]
            unit, rstd = norm_parts(resid)
            out = unit * gain + small_ref[5:6, :]
            out_ref[rs, :] = out.astype(BF16)
            valid = lax.broadcasted_iota(jnp.int32, resid.shape, 0) + part * tile < length
            pool = pool + jnp.sum(jnp.where(valid, out, 0.0), 0, keepdims=True)
            d_out = og_ref[rs, :].astype(F32) + jnp.where(valid, spread, 0.0)
            d_resid = norm_back(unit, rstd, gain, d_out)
            dres_ref[rs, :] = d_resid
            low = d_resid.astype(BF16)
            dlow_ref[rs, :] = low
            dlowt_ref[:, rs] = low.T
            for row, term in enumerate((d_resid, d_out * unit, d_out)):
                sums[row] = sums[row] + jnp.sum(term, 0, keepdims=True)
        pool_ref[seq : seq + 1, :] = pool / count
    sums_ref[...] = jnp.zeros_like(sums_ref)
    for row in range(3):
        sums_ref[row : row + 1, :] = sums[row]


def ln2(lengths, res1, ffn, small, out_grad, pool_grad):
    rows, width = res1.shape
    seqs = lengths.shape[0]
    return resident_call(
        functools.partial(ln2_body, seqs),
        "ln2",
        [res1, ffn, small, out_grad, pool_grad],
        [
            ((rows, width), BF16),
            ((seqs, width), F32),
            ((rows, width), F32),
            ((rows, width), BF16),
            ((width, rows), BF16),
            ((8, width), F32),
        ],
        scalars=(lengths,),
        flops=40 * rows * width,
    )


def gelu_pair(pre):
    bell = jnp.exp(pre * pre * -0.5)
    t = 1.0 / (1.0 + (0.3275911 * SQRT_HALF) * jnp.abs(pre))
    poly = 0.5 * 1.061405429
    poly = poly * t + 0.5 * -1.453152027
    poly = poly * t + 0.5 * 1.421413741
    poly = poly * t + 0.5 * -0.284496736
    poly = poly * t + 0.5 * 0.254829592
    tail = poly * t * bell
    phi = jnp.where(pre >= 0.0, 1.0 - tail, tail)
    return pre * phi, phi + pre * bell * INV_SQRT_2PI


ROW_TILE = 256


def ffn_fwd_body(own, spot_ref, *refs):
    h_ref, bias_ref, *refs = refs
    if own:
        wu_all, wd_all, act_ref, der_ref, acc_ref, bias_scr = refs
    else:
        pieces, refs = refs[:8], refs[8:]
        part_ref, act_ref, der_ref, acc_ref, wu_ref, wd_ref, bias_scr = refs
    units = bias_ref.shape[1]
    rows, width = h_ref.shape
    tiles = [slice(at, at + ROW_TILE) for at in range(0, rows, ROW_TILE)]
    for step in range(2):
        spot = spot_ref[0] ^ step
        if own:
            at = pl.ds(pl.multiple_of(spot * 2 * units, 2 * units), 2 * units)
            wu, wd = wu_all.at[:, at], wd_all.at[at, :]
        else:
            wu, wd = wu_ref.at[step], wd_ref.at[step]
            for flip in range(2):
                at = pl.ds(pl.multiple_of((spot_ref[1] ^ flip) * units, units), units)
                wu[:, at] = pieces[2 * step + flip][...]
                at = pl.ds(pl.multiple_of((spot_ref[2] ^ flip) * units, units), units)
                wd[at, :] = pieces[4 + 2 * step + flip][...]
        bias_scr[:, :units] = bias_ref[pl.ds(2 + 2 * spot, 1), :]
        bias_scr[:, units:] = bias_ref[pl.ds(3 + 2 * spot, 1), :]

        def down(at, act):
            share = dot(act, wd[...])
            if step == 0 and own:
                acc_ref[tiles[at], :] = share
            elif step == 0:
                acc_ref[tiles[at], :] = part_ref[tiles[at], :] + share
            else:
                acc_ref[tiles[at], :] += share

        pre = dot(h_ref[tiles[0], :], wu[...]) + bias_scr[...]
        before = None
        for at, rs in enumerate(tiles):
            now = pre
            if at + 1 < len(tiles):
                pre = dot(h_ref[tiles[at + 1], :], wu[...]) + bias_scr[...]
            act, der = gelu_pair(now)
            act = act.astype(BF16)
            act_ref[step, rs, :] = act
            der_ref[step, rs, :] = der.astype(BF16)
            if before is not None:
                down(at - 1, before)
            before = act
        down(len(tiles) - 1, before)


def ffn_fwd(spot, h, bias, wu=None, wd=None, pieces=(), part=None):
    rows, width = h.shape
    own = wu is not None
    units = 2 * bias.shape[1]
    ins = [h, bias] + ([wu, wd] if own else [*pieces, part])
    outs = [((2, rows, units), BF16), ((2, rows, units), BF16), ((rows, width), F32)]
    if not own:
        outs += [((2, width, units), BF16), ((2, units, width), BF16)]
    return resident_call(
        functools.partial(ffn_fwd_body, own),
        "ffn_fwd",
        ins,
        outs,
        scratch=[pltpu.VMEM((1, units), F32)],
        scalars=(spot,),
        flops=8 * rows * width * units,
        trans=4 * rows * units,
        limit=12,
    )


def split_out(x_bit, row_half, value, away, mine):
    @pl.when(x_bit == row_half)
    def _():
        mine[...] = value

    @pl.when(x_bit != row_half)
    def _():
        away[...] = value


def down_send_body(scalars, loads, stores):
    dft, far, own = loads
    (out,) = stores
    for at, act in enumerate((far, own)):
        out.buf[at] = dot(dft()[...], act()[...]).astype(BF16)
        out.send(at)


def down_send(dft, far_act, own_act):
    width, rows = dft.shape
    units = far_act.shape[2]
    return stream_call(
        down_send_body,
        "down_send",
        [
            (dft, 1),
            (far_act, 1, (rows, units), at_index(1)),
            (own_act, 1, (rows, units), at_index(1)),
        ],
        [((2, width, units), BF16, 2)],
        flops=4 * rows * width * units,
    )[0]


def down_keep_body(scalars, loads, stores):
    dft, far, own, got = loads
    far_left, away, far_right, own_left_away, own_left, own_right = stores
    x_bit = scalars[0][1]
    half = far_left.buf.shape[1]
    rows = far_right.buf.shape[0]
    for which, act in enumerate((far, own)):
        for part in range(2):
            rs = slice(part * rows, (part + 1) * rows)
            total = dot(dft()[rs, :], act()[...]) + got(which)[which, rs, :].astype(F32)
            low = total.astype(BF16)
            left, right = low[:, :half], low[:, half:]
            if which == 0:
                far_left.buf[rs, :] = left
                split_out(x_bit, part, right, away.buf.at[0], far_right.buf)
            else:
                split_out(x_bit, part, left, own_left_away.buf, own_left.buf)
                split_out(x_bit, part, right, away.buf.at[1], own_right.buf)
        if which == 0:
            far_left.send()
            far_right.send()


def down_keep(spot, dft, far_act, own_act, got):
    width, rows = dft.shape
    units = far_act.shape[2]
    half = units // 2
    small = ((width // 2, half), BF16, 1)
    return stream_call(
        down_keep_body,
        "down_keep",
        [
            (dft, 1),
            (far_act, 1, (rows, units), at_index(0)),
            (own_act, 1, (rows, units), at_index(0)),
            (got, 2),
        ],
        [((width, half), BF16, 1), ((2, width // 2, half), BF16, 1), small, small, small, small],
        scalars=(spot,),
        flops=4 * rows * width * units,
    )


def ffn_bwd_body(mode, scalars, loads, stores):
    wd, df, der, ht, *got = loads
    dpre, sums, *outs = stores
    rows = df.buf.shape[0]
    width = ht.buf.shape[0]
    tile = rows // 4
    bias = jnp.zeros((1, dpre.buf.shape[1]), F32)
    tiles = [slice(at * tile, (at + 1) * tile) for at in range(4)]
    d_act = dot_nt(df(0)[tiles[0], :], wd()[...])
    for at, rs in enumerate(tiles):
        now = d_act
        if at + 1 < len(tiles):
            d_act = dot_nt(df(at + 1)[tiles[at + 1], :], wd()[...])
        d_pre = (der(at)[rs, :].astype(F32) * now).astype(BF16)
        dpre.buf[rs, :] = d_pre
        dpre.send(at)
        bias = bias + jnp.sum(d_pre.astype(F32), 0, keepdims=True)
    sums.buf[...] = jnp.broadcast_to(bias, sums.buf.shape)
    sums.send()
    half_rows = width // 2
    half = width // 2
    x_bit = scalars[0][1]
    for part in range(2):
        rs = slice(part * half_rows, (part + 1) * half_rows)
        total = dot(ht()[rs, :], dpre.buf[...])
        if mode == "send":
            outs[0].buf[rs, :] = total.astype(BF16)
            outs[0].send(part)
            continue
        low = (total + got[0](part)[rs, :].astype(F32)).astype(BF16)
        left, right = low[:, :half], low[:, half:]
        if mode == "far":
            outs[0].buf[rs, :] = left
            outs[0].send(part)
            split_out(x_bit, part, right, outs[1].buf, outs[2].buf)
        else:
            split_out(x_bit, part, left, outs[0].buf, outs[1].buf)
            split_out(x_bit, part, right, outs[2].buf, outs[3].buf)


def ffn_bwd(mode, spot, df, ht, der, which, wd, wd_view, got=None):
    rows, width = df.shape
    units = der.shape[2]
    loads = [
        (wd, 1, (units, width), wd_view),
        (df, 4),
        (der, 4, (rows, units), at_index(which)),
        (ht, 1),
    ]
    stores = [((rows, units), BF16, 4), ((8, units), F32, 1)]
    small = ((width // 2, units // 2), BF16, 1)
    if mode == "send":
        stores += [((width, units), BF16, 2)]
    elif mode == "far":
        stores += [((width, units // 2), BF16, 2), small, small]
    else:
        stores += [small] * 4
    if got is not None:
        loads.append((got, 2))
    return stream_call(
        functools.partial(ffn_bwd_body, mode),
        "ffn_bwd",
        loads,
        stores,
        scalars=(spot,),
        flops=4 * rows * width * units,
    )


def hidden_back_body(scalars, loads, stores):
    d0, w0, d1, w1, d2, w2, d3, w3, resid_ref, dres2_ref, small_ref = loads
    dres, dlow, sums = stores
    rows = resid_ref.buf.shape[0]
    tile = rows // 4
    for at in range(4):
        rs = slice(at * tile, (at + 1) * tile)
        d_hidden = None
        for d_pre, weight in ((d0, w0), (d1, w1), (d2, w2), (d3, w3)):
            share = dot_nt(d_pre()[rs, :], weight()[...])
            d_hidden = share if d_hidden is None else d_hidden + share
        d_hidden = d_hidden + dres2_ref(at)[rs, :]
        unit, rstd = norm_parts(resid_ref(at)[rs, :])
        d_resid = norm_back(unit, rstd, small_ref()[1:2, :], d_hidden)
        dres.buf[rs, :] = d_resid
        dres.send(at)
        dlow.buf[rs, :] = d_resid.astype(BF16)
        dlow.send(at)
        terms = (d_resid, d_hidden * unit, d_hidden)
        for row, term in enumerate(terms):
            total = jnp.sum(term, 0, keepdims=True)
            if at == 0:
                sums.buf[row : row + 1, :] = total
            else:
                sums.buf[row : row + 1, :] += total
    sums.send()


def hidden_back(spot, d_pres, wu, wu_far, resid, d_res2, small):
    rows, width = resid.shape
    units = wu.shape[1] // 2

    def own_view(which):
        def view(ref, spot_ref):
            at = pl.multiple_of((spot_ref[0] ^ which) * units, units)
            return ref.at[:, pl.ds(at, units)]

        return view

    shape = (width, units)
    keep, send, far_keep, far_send = d_pres
    return stream_call(
        hidden_back_body,
        "hidden_back",
        [
            (keep, 1),
            (wu, 1, shape, own_view(0)),
            (send, 1),
            (wu, 1, shape, own_view(1)),
            (far_keep, 1),
            (wu_far, 1, shape, at_index(0)),
            (far_send, 1),
            (wu_far, 1, shape, at_index(1)),
            (resid, 4),
            (d_res2, 4),
            (small, 1),
        ],
        [((rows, width), F32, 4), ((rows, width), BF16, 4), ((8, width), F32, 1)],
        scalars=(spot,),
        flops=8 * rows * width * units,
    )


def attn_bwd_body(seqs, heads, scalars, loads, stores):
    wo, da, v, q, kt, probs_in = loads
    (out,) = stores
    scale = HD**-0.5
    cols_all = heads * HD
    span = da.buf.shape[0] // seqs
    for seq in range(seqs):
        rs = slice(seq * span, (seq + 1) * span)
        d_mixed = dot_nt(da(seq)[rs, :], wo()[...]).astype(BF16)
        d_query = []
        for head in range(heads):
            cols = slice(head * HD, (head + 1) * HD)
            d_mixed_h = d_mixed[:, cols]
            d_probs = dot_nt(v()[rs, cols], d_mixed_h)
            low_probs = probs_in()[seq, head]
            probs = low_probs.astype(F32)
            inner = jnp.sum(d_probs * probs, axis=0, keepdims=True)
            d_scores = (probs * (d_probs - inner)).astype(BF16)
            at = cols_all + head * HD
            out.buf[rs, at : at + HD] = dot(d_scores, q()[rs, cols]).astype(BF16)
            at = 2 * cols_all + head * HD
            out.buf[rs, at : at + HD] = dot(low_probs, d_mixed_h).astype(BF16)
            d_query.append((dot(kt()[cols, rs], d_scores) * scale).astype(BF16))
        out.buf[rs, :cols_all] = jnp.concatenate(d_query, 0).T
        out.send(seq)


def attn_bwd(group, seqs, d_attn, wo, saved):
    q, kt, v, _, probs_a, probs_b = saved
    rows, width = d_attn.shape
    span = rows // seqs
    begin, extent = group
    heads = extent // HD
    probs = probs_a if begin == 0 else probs_b
    cols = lambda ref, *_: ref.at[:, begin : begin + extent]
    rows_of = lambda ref, *_: ref.at[begin : begin + extent, :]
    loads = [
        (wo, 1, (extent, width), rows_of),
        (d_attn, seqs),
        (v, 1, (rows, extent), cols),
        (q, 1, (rows, extent), cols),
        (kt, 1, (extent, rows), rows_of),
    ]
    loads.append((probs, 1))
    return stream_call(
        functools.partial(attn_bwd_body, seqs, heads),
        "attn_bwd",
        loads,
        [((rows, 3 * extent), BF16, seqs)],
        flops=2 * rows * width * extent + 20 * rows * span * extent,
    )[0]


def proj_back_body(scalars, loads, stores, fold_scr):
    grads, xt, mt, da, weight, dx_in = loads
    keep, send, dx, sums = stores
    core = scalars[0][0]
    extent = mt.buf.shape[0]
    width = xt.buf.shape[0]
    rows = width // 2
    g_out = dot(mt()[...], da()[...]).astype(BF16)
    for part in range(width // extent):
        fold_scr[part * extent : (part + 1) * extent, :] = g_out[:, part * extent : (part + 1) * extent]
    for part in range(2):
        rs = slice(part * rows, (part + 1) * rows)
        low = dot(xt()[rs, :], grads()[...]).astype(BF16)

        def put(ref, low=low, rs=rs):
            ref[:, : 3 * extent] = low
            ref[:, 3 * extent :] = fold_scr[rs, :]

        @pl.when(core == part)
        def _(put=put):
            put(keep.buf)

        @pl.when(core != part)
        def _(put=put):
            put(send.buf)

    send.send()
    keep.send()
    total = jnp.sum(grads()[...].astype(F32), 0, keepdims=True)
    sums.buf[...] = jnp.broadcast_to(total, sums.buf.shape)
    sums.send()
    for part in range(2):
        half = dx.buf.shape[0] // 2
        rs = slice(part * half, (part + 1) * half)
        dx.buf[rs, :] = dx_in(part)[rs, :] + dot_nt(grads()[rs, :], weight()[...])
        dx.send(part)


def proj_back(group, spot, grads, d_attn, xt, wqkv, mt, dx):
    rows, width = d_attn.shape
    local = mt.shape[0]
    begin, extent = group
    at = qkv_column(local, 0, begin)
    return stream_call(
        proj_back_body,
        "proj_back",
        [
            (grads, 1),
            (xt, 1),
            (mt, 1, (extent, rows), lambda ref, *_: ref.at[begin : begin + extent, :]),
            (d_attn, 1),
            (wqkv, 1, (width, 3 * extent), lambda ref, *_: ref.at[:, at : at + 3 * extent]),
            (dx, 2),
        ],
        [
            ((width // 2, 4 * extent), BF16, 1),
            ((width // 2, 4 * extent), BF16, 1),
            ((rows, width), F32, 2),
            ((8, 3 * extent), F32, 1),
        ],
        scalars=(spot,),
        scratch=[pltpu.VMEM((width, extent), BF16)],
        flops=14 * rows * width * extent,
    )


def finish_attn_body(begin, n_prev, spot_ref, mine_ref, other_ref, *refs):
    outs = refs[n_prev : n_prev + 4]
    full_scr, fold_scr, go_scr, sems = refs[n_prev + 4 :]
    core = spot_ref[0]
    extent = fold_scr.shape[1]
    rows = mine_ref.shape[0]
    local, width = outs[3].shape
    for flip, ref in enumerate((mine_ref, other_ref)):
        at = pl.ds(pl.multiple_of((core ^ flip) * rows, rows), rows)
        fold_scr[at, :] = ref[:, 3 * extent :]
        for mat in range(3):
            full_scr[mat, at, :] = ref[:, mat * extent : (mat + 1) * extent].astype(F32)
    copies = []
    for mat in range(3):
        dst = outs[mat].at[:, begin : begin + extent]
        copies.append(pltpu.make_async_copy(full_scr.at[mat], dst, sems.at[mat]))
        copies[-1].start()
    for part in range(width // extent):
        cols = slice(part * extent, (part + 1) * extent)
        go_scr[:, cols] = fold_scr[cols, :].astype(F32)
    copies.append(pltpu.make_async_copy(go_scr, outs[3].at[begin : begin + extent, :], sems.at[3]))
    copies[-1].start()
    for copy in copies:
        copy.wait()


def finish_attn(group, local, spot, mine, other, previous=()):
    begin, extent = group
    rows, _ = mine.shape
    width = 2 * rows
    return resident_call(
        functools.partial(finish_attn_body, begin, len(previous)),
        "finish_attn",
        [mine, other] + [(p, pltpu.HBM) for p in previous],
        [hbm((width, local), F32)] * 3 + [hbm((local, width), F32)],
        scratch=[
            pltpu.VMEM((3, width, extent), F32),
            pltpu.VMEM((width, extent), BF16),
            pltpu.VMEM((extent, width), F32),
            pltpu.SemaphoreType.DMA((4,)),
        ],
        scalars=(spot,),
        aliases={2 + i: i for i in range(len(previous))},
        limit=12,
    )


def finish_body(kind, spot_ref, mine_ref, other_ref, out, scr, sems):
    width, units = mine_ref.shape
    parts = 2
    extent = units // parts
    copies = []
    for flip, ref in enumerate((mine_ref, other_ref)):
        for part in range(parts):
            at = flip * parts + part
            begin = pl.multiple_of((spot_ref[0] ^ flip) * units + part * extent, extent)
            value = ref[:, part * extent : (part + 1) * extent].astype(F32)
            scr[at] = value if kind == "up" else value.T
            place = pl.ds(begin, extent)
            dst = out.at[:, place] if kind == "up" else out.at[place, :]
            copies.append(pltpu.make_async_copy(scr.at[at], dst, sems.at[at]))
            copies[-1].start()
    for copy in copies:
        copy.wait()


def finish(kind, spot, mine, other):
    width, units = mine.shape
    shape = (width, 2 * units) if kind == "up" else (2 * units, width)
    piece = (width, units // 2) if kind == "up" else (units // 2, width)
    return resident_call(
        functools.partial(finish_body, kind),
        "finish_" + kind,
        [mine, other],
        [hbm(shape, F32)],
        scratch=[pltpu.VMEM((4, *piece), F32), pltpu.SemaphoreType.DMA((4,))],
        scalars=(spot,),
        limit=12,
    )[0]


def together(*values):
    return lax.optimization_barrier(values)


def add(*terms):
    total = terms[0].astype(F32)
    for term in terms[1:]:
        total = total + term.astype(F32)
    return total.astype(BF16)


def local(
    n_batch,
    tokens,
    lengths,
    w_query,
    b_query,
    w_key,
    w_value,
    b_value,
    w_out,
    b_out,
    gain_one,
    shift_one,
    w_up,
    b_up,
    w_down,
    b_down,
    gain_two,
    shift_two,
    out_grad,
    pool_grad,
):
    rows, width = tokens.shape
    seqs = lengths.shape[0]
    half = w_query.shape[1]
    group_a, group_b = groups_of(half)
    place = lax.axis_index("batch").astype(jnp.int32)
    core, x_bit, z_low, z_high = [(place >> bit) & 1 for bit in range(4)]
    spot = jnp.stack([core, x_bit, z_low])

    def swap(array, bit):
        return lax.ppermute(array, "batch", [(i, i ^ bit) for i in range(n_batch)])

    def swap_core(array):
        return swap(array, 1)

    def swap_x(array):
        return swap(array, 2)

    def swap_y(array):
        return lax.ppermute(array, "tensor", [(0, 1), (1, 0)])

    bias_rows = jnp.concatenate([b_query, b_value, b_up]).reshape(-1, half)
    bias_rows = jnp.pad(bias_rows, ((0, 16 - bias_rows.shape[0]), (0, 0)))
    own_bias = bias_rows.astype(F32)
    small = jnp.stack([b_out, gain_one, shift_one, b_down, gain_two, shift_two]).astype(F32)
    ex, ez, own_qkv = pack(spot, w_query, w_key, w_value, w_out, bias_rows)
    fx = lax.dynamic_slice_in_dim(w_up, (2 * core + x_bit) * half, half, 1)
    fz = lax.dynamic_slice_in_dim(w_down, (2 * core + z_low) * half, half, 0)

    ex, ez = swap_y(ex), swap_y(ez)
    fx, fz = swap_y(fx), swap_y(fz)
    *own_saved, attn_part, xt = attn_fwd(lengths, tokens, own_qkv, w_out, own_bias)
    ex, ez, attn_part, small, own_bias = together(ex, ez, attn_part, small, own_bias)
    ex_x, ez_z = swap_x(ex), swap(ez, 4)
    ex_c, ez_c = swap_core(ex), swap_core(ez)
    ex_x, ez_z, ex_c, ez_c = together(ex_x, ez_z, ex_c, ez_c)
    ex_xc, ez_zc = swap_core(ex_x), swap_core(ez_z)
    far_qkv, far_o, far_bias = assemble(
        spot, (ex, ex_x, ex_c, ex_xc, ez, ez_z, ez_c, ez_zc), width, half
    )
    *far_saved, resid_one, hidden, hidden_t = attn_fwd(
        lengths, tokens, far_qkv, far_o, far_bias, part=attn_part, small=small
    )
    hidden, fx, fz = together(hidden, fx, fz)
    fx_x, fz_z = swap_x(fx), swap(fz, 4)
    fx_c, fz_c = swap_core(fx), swap_core(fz)
    own_act, own_der, ffn_part = ffn_fwd(spot, hidden, own_bias, wu=w_up, wd=w_down)
    fx_x, fz_z, fx_c, fz_c, ffn_part = together(fx_x, fz_z, fx_c, fz_c, ffn_part)
    fx_xc, fz_zc = swap_core(fx_x), swap_core(fz_z)
    far_act, far_der, ffn_sum, wu_far, wd_far = ffn_fwd(
        spot,
        hidden,
        far_bias,
        pieces=(fx, fx_x, fx_c, fx_xc, fz, fz_z, fz_c, fz_zc),
        part=ffn_part,
    )
    output, pooled, d_resid_two, d_ffn, d_ffn_t, sums_two = ln2(
        lengths, resid_one, ffn_sum, small, out_grad, pool_grad
    )

    def pick(array, at):
        return lax.dynamic_index_in_dim(array, at, 0, keepdims=False)

    def halves(array):
        return array.reshape(2, array.shape[0] // 2, array.shape[1])

    def split(bit, *terms):
        parts = [halves(t) for t in terms]
        return add(*[pick(t, 1 - bit) for t in parts]), add(*[pick(t, bit) for t in parts])

    def join(bit, mine, got):
        return jnp.concatenate(
            [jnp.where(bit == 0, mine, got), jnp.where(bit == 0, got, mine)], axis=0
        )

    def rest(array):
        bit = 16
        while bit < n_batch:
            array = add(array, swap(array, bit))
            bit *= 2
        return array

    def cross_two(left_got, right_got, away, far):
        return swap_x(add(away, pick(halves(left_got), 1 - x_bit))), swap_y(add(far, right_got))

    def cross_three(left, left_got, left_x, right, right_x, right_y):
        mine = pick(halves(left_got), x_bit)
        return jnp.concatenate([add(left, mine, left_x), add(right, right_x, right_y)], axis=1)

    def own_view(which):
        def view(ref, spot_ref):
            at = pl.multiple_of((spot_ref[0] ^ which) * width, width)
            return ref.at[pl.ds(at, width), :]

        return view

    d_send = down_send(d_ffn_t, far_act, own_act)
    d_ffn, d_send = together(d_ffn, d_send)
    d_got = swap_core(d_send)
    dp_fs, bs_fs, u_send = ffn_bwd("send", spot, d_ffn, hidden_t, far_der, 1, wd_far, at_index(1))
    d_ffn_t, d_got, u_send = together(d_ffn_t, d_got, u_send)
    uf_got = swap_core(u_send)
    df_left, d_away, df_right, do_left_away, do_left, do_right = down_keep(
        spot, d_ffn_t, far_act, own_act, d_got
    )
    d_ffn, df_left, d_away = together(d_ffn, df_left, d_away)
    d_left_y, d_right_x = swap_y(df_left), swap_x(d_away)
    dp_os, bs_os, u_send = ffn_bwd("send", spot, d_ffn, hidden_t, own_der, 1, w_down, own_view(1))
    d_ffn, u_send, uf_got = together(d_ffn, u_send, uf_got)
    uo_got = swap_core(u_send)
    dp_fk, bs_fk, uf_left, uf_away, uf_right = ffn_bwd(
        "far", spot, d_ffn, hidden_t, far_der, 0, wd_far, at_index(0), uf_got
    )
    d_ffn, uf_left, uo_got = together(d_ffn, uf_left, uo_got)
    dp_ok, bs_ok, uo_left_away, uo_left, uo_right_away, uo_right = ffn_bwd(
        "own", spot, d_ffn, hidden_t, own_der, 0, w_down, own_view(0), uo_got
    )
    d_left_y, d_right_x, dp_ok, uf_left, uf_away = together(d_left_y, d_right_x, dp_ok, uf_left, uf_away)
    d_left_x, d_right_y = cross_two(d_left_y, d_right_x[0], do_left_away, df_right)
    u_left_y, uf_right_x, uo_right_x = swap_y(uf_left), swap_x(uf_away), swap_x(uo_right_away)
    d_resid_one, d_attn, sums_one = hidden_back(
        spot, (dp_ok, dp_os, dp_fk, dp_fs), w_up, wu_far, resid_one, d_resid_two, small
    )

    d_left_x, d_right_y, d_attn = together(d_left_x, d_right_y, d_attn)
    d_rows = cross_three(do_left, d_left_y, d_left_x, do_right, d_right_x[1], d_right_y)
    d_away, d_mine = split(z_low, d_rows)
    d_got = swap(d_away, 4)
    bias_up = lambda keep, send: jnp.where(core == 0, jnp.stack([keep, send]), jnp.stack([send, keep]))
    shared = jnp.concatenate([sums_one[:3], sums_two[:3]]).reshape(-1)
    early = jnp.concatenate([bias_up(bs_ok[0], bs_os[0]).reshape(-1), shared])
    early_got = swap_y(jnp.concatenate([bias_up(bs_fk[0], bs_fs[0]).reshape(-1), shared]))
    fa = attn_bwd(group_a, seqs, d_attn, far_o, far_saved)
    d_attn, fa, d_got, early_got, u_left_y, uf_right_x, uo_right_x = together(
        d_attn, fa, d_got, early_got, u_left_y, uf_right_x, uo_right_x
    )
    d_away, d_mine = split(z_high, d_mine, d_got)
    d_got = swap(d_away, 8)
    u_left_x, u_right_y = cross_two(u_left_y, uf_right_x, uo_left_away, uf_right)
    early = early + early_got
    early_got = swap(early, 1)
    fa_keep, fa_send, dx, fa_sums = proj_back(
        group_a, spot, fa, d_attn, xt, far_qkv, far_saved[3], d_resid_one
    )
    d_attn, fa_send, d_got, early_got = together(d_attn, fa_send, d_got, early_got)
    fa_got = swap_core(fa_send)
    d_mine = rest(add(d_mine, d_got))
    d_got = swap(d_mine, 8)
    early = early + early_got
    early_got = swap(early, 2)
    fb = attn_bwd(group_b, seqs, d_attn, far_o, far_saved)
    d_attn, fb, fa_got, d_got, early_got, u_left_x, u_right_y = together(
        d_attn, fb, fa_got, d_got, early_got, u_left_x, u_right_y
    )
    fa_y = swap_y(add(fa_keep, fa_got))
    d_mine = join(z_high, d_mine, d_got)
    d_got = swap(d_mine, 4)
    u_rows = cross_three(uo_left, u_left_y, u_left_x, uo_right, uo_right_x, u_right_y)
    u_away, u_mine = split(z_low, u_rows)
    u_got = swap(u_away, 4)
    early = early + early_got
    early_got = swap(early, 4)
    fb_keep, fb_send, dx, fb_sums = proj_back(
        group_b, spot, fb, d_attn, xt, far_qkv, far_saved[3], dx
    )
    d_attn, fb_send, early_got = together(d_attn, fb_send, early_got)
    fb_got = swap_core(fb_send)
    early = early + early_got
    early_got = swap(early, 8)
    oa = attn_bwd(group_a, seqs, d_attn, w_out, own_saved)
    d_attn, oa, fb_got, d_got, u_got, early_got = together(d_attn, oa, fb_got, d_got, u_got, early_got)
    fb_y = swap_y(add(fb_keep, fb_got))
    d_mine = join(z_low, d_mine, d_got)
    d_got = swap_x(d_mine)
    u_away, u_mine = split(z_high, u_mine, u_got)
    u_got = swap(u_away, 8)
    early = early + early_got
    bit = 16
    while bit < n_batch:
        early = early + swap(early, bit)
        bit *= 2
    oa_keep, oa_send, dx, oa_sums = proj_back(
        group_a, spot, oa, d_attn, xt, own_qkv, own_saved[3], dx
    )
    d_attn, oa_send, u_got = together(d_attn, oa_send, u_got)
    oa_got = swap_core(oa_send)
    u_mine = rest(add(u_mine, u_got))
    u_got = swap(u_mine, 8)
    ob = attn_bwd(group_b, seqs, d_attn, w_out, own_saved)
    d_attn, ob, oa_got, d_got, u_got, fa_y = together(d_attn, ob, oa_got, d_got, u_got, fa_y)
    a_away, a_mine = split(x_bit, oa_keep, oa_got, fa_y)
    a_got = swap_x(a_away)
    d_mine = join(x_bit, d_mine, d_got)
    d_other = swap_core(d_mine)
    u_mine = join(z_high, u_mine, u_got)
    u_got = swap(u_mine, 4)
    ob_keep, ob_send, d_tokens, ob_sums = proj_back(
        group_b, spot, ob, d_attn, xt, own_qkv, own_saved[3], dx
    )

    def late_sums(a, b):
        (_, ca), (_, cb) = group_a, group_b
        return jnp.concatenate([a[0, :ca], b[0, :cb], a[0, 2 * ca :], b[0, 2 * cb :]])

    ob_send, d_other, a_got, u_got, fb_y = together(ob_send, d_other, a_got, u_got, fb_y)
    ob_got = swap_core(ob_send)
    late_got = swap_y(late_sums(fa_sums, fb_sums))
    a_away, a_mine = split(z_low, a_mine, a_got)
    a_got = swap(a_away, 4)
    u_mine = join(z_low, u_mine, u_got)
    u_got = swap_x(u_mine)
    g_down = finish("down", spot, d_mine, d_other)

    ob_got, a_got, late_got, g_down = together(ob_got, a_got, late_got, g_down)
    b_away, b_mine = split(x_bit, ob_keep, ob_got, fb_y)
    b_got = swap_x(b_away)
    a_away, a_mine = split(z_high, a_mine, a_got)
    a_got = swap(a_away, 8)
    late = late_sums(oa_sums, ob_sums) + late_got
    late_got = swap(late, 1)

    b_got, a_got, late_got = together(b_got, a_got, late_got)
    b_away, b_mine = split(z_low, b_mine, b_got)
    b_got = swap(b_away, 4)
    a_mine = rest(add(a_mine, a_got))
    a_got = swap(a_mine, 8)
    late = late + late_got
    late_got = swap(late, 2)

    b_got, a_got, late_got, u_got = together(b_got, a_got, late_got, u_got)
    b_away, b_mine = split(z_high, b_mine, b_got)
    b_got = swap(b_away, 8)
    a_mine = join(z_high, a_mine, a_got)
    a_got = swap(a_mine, 4)
    u_mine = join(x_bit, u_mine, u_got)
    u_other = swap_core(u_mine)
    late = late + late_got
    late_got = swap(late, 4)

    b_got, a_got, u_other, late_got = together(b_got, a_got, u_other, late_got)
    b_mine = rest(add(b_mine, b_got))
    b_got = swap(b_mine, 8)
    a_mine = join(z_low, a_mine, a_got)
    a_got = swap_x(a_mine)
    late = late + late_got
    late_got = swap(late, 8)
    g_up = finish("up", spot, u_mine, u_other)

    b_got, g_up, late_got = together(b_got, g_up, late_got)
    b_mine = join(z_high, b_mine, b_got)
    b_got = swap(b_mine, 4)
    late = late + late_got
    bit = 16
    while bit < n_batch:
        late = late + swap(late, bit)
        bit *= 2
    a_got, late = together(a_got, late)
    a_mine = join(x_bit, a_mine, a_got)
    a_other = swap_core(a_mine)
    b_got, a_other = together(b_got, a_other)
    b_mine = join(z_low, b_mine, b_got)
    b_got = swap_x(b_mine)
    grads = finish_attn(group_a, half, spot, a_mine, a_other)
    b_got, *grads = together(b_got, *grads)
    b_mine = join(x_bit, b_mine, b_got)
    b_other = swap_core(b_mine)
    g_query, g_key, g_value, g_out = finish_attn(group_b, half, spot, b_mine, b_other, grads)

    g_bias_query, g_bias_value = jnp.split(late, 2)
    (
        g_bias_up,
        d_bias_out,
        d_gain_one,
        d_shift_one,
        d_bias_down,
        d_gain_two,
        d_shift_two,
    ) = jnp.split(early, [4 * half + width * i for i in range(6)])
    return (
        output,
        pooled,
        d_tokens,
        g_query,
        g_bias_query,
        g_key,
        g_value,
        g_bias_value,
        g_out,
        d_bias_out,
        d_gain_one,
        d_shift_one,
        g_up,
        g_bias_up,
        g_down,
        d_bias_down,
        d_gain_two,
        d_shift_two,
    )


def solution(mesh):
    return jax.shard_map(
        functools.partial(local, mesh.shape["batch"]),
        mesh=mesh,
        in_specs=(
            P(("batch", "tensor"), None),
            P(("batch", "tensor")),
            P(None, "tensor"),
            P("tensor"),
            P(None, "tensor"),
            P(None, "tensor"),
            P("tensor"),
            P("tensor", None),
            P(),
            P(),
            P(),
            P(None, "tensor"),
            P("tensor"),
            P("tensor", None),
            P(),
            P(),
            P(),
            P(("batch", "tensor"), None),
            P(("batch", "tensor"), None),
        ),
        out_specs=(
            P(("batch", "tensor"), None),
            P(("batch", "tensor"), None),
            P(("batch", "tensor"), None),
            P(None, "tensor"),
            P("tensor"),
            P(None, "tensor"),
            P(None, "tensor"),
            P("tensor"),
            P("tensor", None),
            P(),
            P(),
            P(),
            P(None, "tensor"),
            P("tensor"),
            P("tensor", None),
            P(),
            P(),
            P(),
        ),
        check_vma=False,
    )
```

```python
import functools

import jax
import jax.numpy as jnp
from jax import lax
from jax.experimental import pallas as pl
from jax.experimental.pallas import tpu as pltpu
from jax.sharding import PartitionSpec as P

HD = 64
EPSILON = 1e-12
NEG_FILL = -1e30
F32 = jnp.float32
BF16 = jnp.bfloat16
MIB = 1024 * 1024
FLOPS_PER_US = 1.1e9
SQRT_HALF = 0.7071067811865476
INV_SQRT_2PI = 0.3989422804014327


def dot(left, right):
    return lax.dot_general(left, right, (((1,), (0,)), ((), ())), preferred_element_type=F32)


def dot_nt(left, right):
    return lax.dot_general(left, right, (((1,), (1,)), ((), ())), preferred_element_type=F32)


def dot_tn(left, right):
    return lax.dot_general(left, right, (((0,), (0,)), ((), ())), preferred_element_type=F32)


class Part:
    def __init__(self, buf):
        self.buf = buf

    def __call__(self, part=None):
        return self.buf

    def send(self, part=0):
        pass

    def finish(self):
        pass


def pieces_of(src, dst, parts, axis):
    if parts == 1:
        return [(src, dst)]
    extent = dst.shape[axis] // parts
    cuts = [(slice(None),) * axis + (pl.ds(part * extent, extent),) for part in range(parts)]
    return [(src.at[cut], dst.at[cut]) for cut in cuts]


class Load:
    def __init__(self, src, buf, sems, first, parts, axis):
        self.buf = buf
        self.copies = [
            pltpu.make_async_copy(*pair, sems.at[first + at])
            for at, pair in enumerate(pieces_of(src, buf, parts, axis))
        ]
        self.waited = [False] * parts
        for copy in self.copies:
            copy.start()

    def __call__(self, part=None):
        for at in range(len(self.copies)) if part is None else (part,):
            if not self.waited[at]:
                self.waited[at] = True
                self.copies[at].wait()
        return self.buf


class Store:
    def __init__(self, buf, dst, sems, first, parts, axis):
        self.buf = buf
        self.copies = [
            pltpu.make_async_copy(*pair, sems.at[first + at])
            for at, pair in enumerate(pieces_of(buf, dst, parts, axis))
        ]
        self.sent = [False] * parts

    def send(self, part=0):
        self.sent[part] = True
        self.copies[part].start()

    def finish(self):
        for at, copy in enumerate(self.copies):
            if not self.sent[at]:
                copy.start()
        for copy in self.copies:
            copy.wait()


class Far:
    def __init__(self, array, parts=1, axis=0, shape=None, view=None):
        self.array, self.parts, self.axis = array, parts, axis
        self.shape = shape or array.shape
        self.view = view or (lambda ref, *_: ref)


class FarOut:
    def __init__(self, shape, dtype, parts=1, axis=0):
        self.shape, self.dtype, self.parts, self.axis = shape, dtype, parts, axis


class Raw:
    def __init__(self, array=None, shape=None, dtype=None):
        self.array, self.shape, self.dtype = array, shape, dtype


class Kernels:
    def __init__(self):
        self.token = None

    def wait(self, *values):
        self.token, values = lax.optimization_barrier((self.token, values))
        return values if len(values) > 1 else values[0]

    def __call__(self, body, name, ins, outs, scalars=(), scratch=(), aliases=None, limit=6, cost=4):
        spec = lambda space: pl.BlockSpec(memory_space=space)
        in_far = [isinstance(i, Far) for i in ins]
        in_raw = [isinstance(i, Raw) for i in ins]
        out_far = [isinstance(o, FarOut) for o in outs]
        out_raw = [isinstance(o, Raw) for o in outs]
        in_spaces = [pltpu.HBM if f or r else pltpu.VMEM for f, r in zip(in_far, in_raw)]
        out_spaces = [pltpu.HBM if f or r else pltpu.VMEM for f, r in zip(out_far, out_raw)]
        arrays = [i.array if f or r else i for i, f, r in zip(ins, in_far, in_raw)]
        out_types = [(o.shape, o.dtype) if f or r else o for o, f, r in zip(outs, out_far, out_raw)]
        buffers = [pltpu.VMEM(i.shape, i.array.dtype) for i, f in zip(ins, in_far) if f]
        buffers += [pltpu.VMEM(o.shape, o.dtype) for o, f in zip(outs, out_far) if f]
        n_sem = sum(i.parts for i, f in zip(ins, in_far) if f)
        n_sem += sum(o.parts for o, f in zip(outs, out_far) if f)
        n_scalar, n_in, n_out, n_buf = len(scalars), len(ins), len(outs), len(buffers)
        first = self.token is None

        def kernel(*refs):
            scalar_refs, refs = refs[:n_scalar], refs[n_scalar:]
            in_refs, refs = refs[:n_in], refs[n_in + (not first) :]
            out_refs, token_ref, refs = refs[:n_out], refs[n_out], refs[n_out + 1 :]
            bufs, sems, rest = list(refs[:n_buf]), refs[n_buf], refs[n_buf + 1 :]
            at, loads, stores = 0, [], []
            for i, f, r, ref in zip(ins, in_far, in_raw, in_refs):
                if f:
                    src = i.view(ref, *scalar_refs)
                    loads.append(Load(src, bufs.pop(0), sems, at, i.parts, i.axis))
                    at += i.parts
                else:
                    loads.append(ref if r else Part(ref))
            for o, f, r, ref in zip(outs, out_far, out_raw, out_refs):
                if f:
                    stores.append(Store(bufs.pop(0), ref, sems, at, o.parts, o.axis))
                    at += o.parts
                else:
                    stores.append(ref if r else Part(ref))
            body(scalar_refs, loads, stores, *rest)
            token_ref[...] = jnp.zeros_like(token_ref)
            for load, f in zip(loads, in_far):
                if f:
                    load()
            for store, r in zip(stores, out_raw):
                if not r:
                    store.finish()

        *results, self.token = pl.pallas_call(
            kernel,
            name=name,
            in_specs=[spec(pltpu.SMEM)] * n_scalar
            + [spec(space) for space in in_spaces]
            + ([] if first else [spec(pl.ANY)]),
            out_specs=[spec(space) for space in out_spaces] + [spec(pltpu.VMEM)],
            scratch_shapes=buffers + [pltpu.SemaphoreType.DMA((max(n_sem, 1),))] + list(scratch),
            out_shape=[space(*kind) for kind, space in zip(out_types, out_spaces)]
            + [pltpu.VMEM((8, 128), F32)],
            input_output_aliases={k + n_scalar: v for k, v in (aliases or {}).items()},
            compiler_params=pltpu.CompilerParams(vmem_limit_bytes=limit * MIB),
            cost_estimate=pl.CostEstimate(
                flops=int(cost * FLOPS_PER_US), bytes_accessed=0, transcendentals=0
            ),
        )(
            *scalars,
            *[pltpu.with_memory_space_constraint(a, space) for a, space in zip(arrays, in_spaces)],
            *([] if first else [self.token]),
        )
        return results if len(results) > 1 else results[0]


def at_index(index):
    return lambda ref, *_: ref.at[index]


def groups_of(local):
    first = local * 2 // 3
    return ((0, first), (first, local - first))


def pack_body(scalars, loads, stores, sems):
    wq, wk, wv, wo, bias = loads
    ex, ez = [store.buf for store in stores]
    core, x_bit, z_bit = [scalars[0][at] for at in range(3)]
    width, local = wq.shape
    rows = width // 2
    outs = wo.shape[0] // 2
    mine = pl.ds(pl.multiple_of(core * rows, rows), rows)
    mine_out = pl.ds(pl.multiple_of(core * outs, outs), outs)
    query = pltpu.make_async_copy(wq.at[mine, :], ex, sems.at[0])

    @pl.when(x_bit == 0)
    def _():
        query.start()

    @pl.when(x_bit == 1)
    def _():
        pltpu.make_async_copy(wk.at[mine, :], ex, sems.at[0]).start()

    values = []
    for part in range(width // local):
        dst, sem = ez.at[part * outs : (part + 1) * outs, :], sems.at[1 + part]
        own = pl.ds(pl.multiple_of(core * rows + part * outs, outs), outs)
        values.append(pltpu.make_async_copy(wv.at[own, :], dst, sem))

        @pl.when(z_bit == 0)
        def _(copy=values[-1]):
            copy.start()

        @pl.when(z_bit == 1)
        def _(dst=dst, sem=sem, part=part):
            src = wo.at[mine_out, part * local : (part + 1) * local]
            pltpu.make_async_copy(src, dst, sem).start()

    ez[rows:, :] = bias()[...]
    query.wait()
    for copy in values:
        copy.wait()


def pack(run, spot, wq, wk, wv, wo, bias):
    width, local = wq.shape
    return run(
        pack_body,
        "pack",
        [Raw(wq), Raw(wk), Raw(wv), Raw(wo), bias],
        [((width // 2, local), BF16), ((width // 2 + bias.shape[0], local), BF16)],
        scalars=(spot,),
        scratch=[pltpu.SemaphoreType.DMA((1 + width // local,))],
        cost=2,
    )


def pack_units_body(scalars, loads, stores, sems):
    wu, wd = loads
    fx, fz = [store.buf for store in stores]
    core, x_bit, z_bit = [scalars[0][at] for at in range(3)]
    units = fx.shape[1]
    up = pl.ds(pl.multiple_of((2 * core + x_bit) * units, units), units)
    down = pl.ds(pl.multiple_of((2 * core + z_bit) * units, units), units)
    copies = [
        pltpu.make_async_copy(wu.at[:, up], fx, sems.at[0]),
        pltpu.make_async_copy(wd.at[down, :], fz, sems.at[1]),
    ]
    for copy in copies:
        copy.start()
    for copy in copies:
        copy.wait()


def pack_units(run, spot, wu, wd, units):
    width = wu.shape[0]
    return run(
        pack_units_body,
        "pack_units",
        [Raw(wu), Raw(wd)],
        [((width, units), BF16), ((units, width), BF16)],
        scalars=(spot,),
        scratch=[pltpu.SemaphoreType.DMA((2,))],
        cost=2,
    )


def assemble(spot_ref, pieces, wq, wk, wv, wo, bias):
    core, x_bit, z_bit = spot_ref[0], spot_ref[1], spot_ref[2]
    local, width = wo.shape
    rows = width // 2
    outs = local // 2
    for c_flip in range(2):
        spot = core ^ c_flip
        at = pl.ds(pl.multiple_of(spot * rows, rows), rows)
        out_at = pl.ds(pl.multiple_of(spot * outs, outs), outs)
        for flip in range(2):
            piece = pieces[2 * c_flip + flip]()
            for mat, ref in enumerate((wq, wk)):

                @pl.when((x_bit ^ flip) == mat)
                def _(piece=piece, at=at, ref=ref):
                    ref[at, :] = piece[...]

            piece = pieces[4 + 2 * c_flip + flip]()

            @pl.when((z_bit ^ flip) == 0)
            def _(piece=piece, at=at):
                wv[at, :] = piece[0:rows, :]

            @pl.when((z_bit ^ flip) == 1)
            def _(piece=piece, out_at=out_at):
                for part in range(width // local):
                    cols = slice(part * local, (part + 1) * local)
                    wo[out_at, cols] = piece[part * outs : (part + 1) * outs, :]

    bias[...] = pieces[4]()[rows : rows + bias.shape[0], :].astype(F32)


SLOTS = 4


def attn_fwd_body(slots, span, heads, first, scalars, loads, stores, k_scr, vt_scr, p_scr, sems):
    len_ref = scalars[0]
    count = len(slots)
    if first:
        x_in, wq_in, wk_in, wv_in, bias_in = loads
        bias = bias_in()
    else:
        pieces, (x_in, *near_mt, near_wo, small) = loads[:8], loads[8:]
    saved, stores = stores[: 6 * count], stores[6 * count :]
    if first:
        wq, wk, wv = wq_in(), wk_in(), wv_in()
    else:
        resid_out, low_out, lowt_out, *kept, bias_out = stores
        wq, wk, wv, wo = [store.buf for store in kept]
        bias = bias_out.buf
        assemble(scalars[1], pieces, wq, wk, wv, wo, bias)
        for store in kept:
            store.send()
    local = wq.shape[1]
    heads_a = groups_of(local)[0][1] // HD

    def save(at):
        number, head = at // heads, at % heads
        pa_hbm, pb_hbm = saved[6 * number + 4 : 6 * number + 6]
        dst = pa_hbm.at[head] if head < heads_a else pb_hbm.at[head - heads_a]
        return pltpu.make_async_copy(p_scr.at[at % SLOTS], dst, sems.at[at % SLOTS])

    for number, slot in enumerate(slots):
        q_out, kt_out, v_out, mt_out = saved[6 * number : 6 * number + 4]
        rs = slice(number * span, (number + 1) * span)
        x = x_in(number)[rs, :]
        query = (dot(x, wq[...]) + bias[0:1, :]).astype(BF16)
        q_out.buf[...] = query * jnp.asarray(HD**-0.5, BF16)
        k_scr[...] = dot(x, wk[...]).astype(BF16)
        v_out.buf[...] = (dot(x, wv[...]) + bias[1:2, :]).astype(BF16)
        kt_out.buf[...] = k_scr[...].T
        vt_scr[...] = v_out.buf[...].T
        if first:
            stores[number].buf[...] = x.T
            stores[number].send()
        for store in (q_out, kt_out, v_out):
            store.send()
        valid = lax.broadcasted_iota(jnp.int32, (span, span), 0) < len_ref[slot]
        for head in range(heads):
            at = number * heads + head
            cols = slice(head * HD, (head + 1) * HD)
            scores = dot_nt(k_scr[:, cols], q_out.buf[:, cols])
            scores = jnp.where(valid, scores, NEG_FILL)
            top = jnp.max(scores, axis=0, keepdims=True)
            weight = jnp.exp(scores - top)
            total = jnp.sum(weight, axis=0, keepdims=True)
            probs = (weight * (1.0 / total)).astype(BF16)
            if at >= SLOTS:
                save(at - SLOTS).wait()
            p_scr[at % SLOTS] = probs
            save(at).start()
            mt_out.buf[cols, :] = dot(vt_scr[cols, :], probs).astype(BF16)
        mt_out.send()
        if not first:
            share = dot_tn(near_mt[number]()[...], near_wo()[...]) + dot_tn(mt_out.buf[...], wo[...])
            resid = x.astype(F32) + share + small()[0:1, :]
            unit, _ = norm_parts(resid)
            low = (unit * small()[1:2, :] + small()[2:3, :]).astype(BF16)
            resid_out.buf[rs, :] = resid
            low_out.buf[rs, :] = low
            lowt_out.buf[:, rs] = low.T
    for at in range(count * heads - SLOTS, count * heads):
        save(at).wait()


def attn_fwd(run, lengths, seqs, slots, x, own=None, far=None):
    rows, width = x.shape
    span = rows // seqs
    local = own[0].shape[1] if own else far[3].shape[0]
    heads = local // HD
    (_, extent_a), (_, extent_b) = groups_of(local)
    count = len(slots)
    tokens = pl.ds(slots[0] * span, count * span)
    x_in = Far(x, count, shape=(count * span, width), view=lambda ref, *_: ref.at[tokens, :])
    outs = []
    for _ in slots:
        outs += [
            FarOut((span, local), BF16),
            FarOut((local, span), BF16),
            FarOut((span, local), BF16),
            FarOut((local, span), BF16),
            Raw(shape=(extent_a // HD, span, span), dtype=BF16),
            Raw(shape=(extent_b // HD, span, span), dtype=BF16),
        ]
    if own:
        *weights, bias = own
        ins = [x_in, *map(Far, weights), bias]
        outs += [FarOut((width, span), BF16)] * count
        scalars = (lengths,)
    else:
        spot, pieces, near_mt, near_wo, small = far
        ins = [p if at in (3, 7) else Far(p) for at, p in enumerate(pieces)]
        ins += [x_in, *map(Far, near_mt), Far(near_wo), small]
        outs += [((rows, width), F32), ((rows, width), BF16), ((width, rows), BF16)]
        outs += [FarOut((width, local), BF16)] * 3 + [FarOut((local, width), BF16)]
        outs.append(((16, local), F32))
        scalars = (lengths, spot)
    results = run(
        functools.partial(attn_fwd_body, slots, span, heads, bool(own)),
        "attn_fwd",
        ins,
        outs,
        scratch=[
            pltpu.VMEM((span, local), BF16),
            pltpu.VMEM((local, span), BF16),
            pltpu.VMEM((SLOTS, span, span), BF16),
            pltpu.SemaphoreType.DMA((SLOTS,)),
        ],
        limit=14 if own else 24,
        scalars=scalars,
        cost=8 if own else 6,
    )
    saved = [results[6 * number : 6 * number + 6] for number in range(count)]
    return (saved, *results[6 * count :])


def norm_parts(resid):
    center = resid - jnp.mean(resid, -1, keepdims=True)
    spread = jnp.mean(center * center, -1, keepdims=True)
    rstd = lax.rsqrt(spread + EPSILON)
    return center * rstd, rstd


def norm_back(unit, rstd, gain, grad):
    scaled = grad * gain
    return rstd * (
        scaled
        - jnp.mean(scaled, -1, keepdims=True)
        - unit * jnp.mean(scaled * unit, -1, keepdims=True)
    )


def ln2_body(seqs, scalars, loads, stores):
    res1, ffn, og, small, pg = loads
    out_st, pool, dres, dlow, dlowt, sums_st = stores
    len_ref = scalars[0]
    small = small()
    rows = res1.buf.shape[0]
    span = rows // seqs
    tile = span // 4
    sums = [0.0, 0.0, 0.0]
    gain = small[4:5, :]
    for seq in range(seqs):
        length = len_ref[seq]
        count = length.astype(F32)
        total = 0.0
        spread = pg()[seq : seq + 1, :] / count
        for part in range(4):
            at = 4 * seq + part
            rs = slice(at * tile, (at + 1) * tile)
            unit_one, _ = norm_parts(res1(at)[rs, :])
            hidden = unit_one * small[1:2, :] + small[2:3, :]
            resid = hidden + ffn()[rs, :] + small[3:4, :]
            unit, rstd = norm_parts(resid)
            out = unit * gain + small[5:6, :]
            out_st.buf[rs, :] = out.astype(BF16)
            out_st.send(at)
            valid = lax.broadcasted_iota(jnp.int32, resid.shape, 0) + part * tile < length
            total = total + jnp.sum(jnp.where(valid, out, 0.0), 0, keepdims=True)
            d_out = og(at)[rs, :].astype(F32) + jnp.where(valid, spread, 0.0)
            d_resid = norm_back(unit, rstd, gain, d_out)
            dres.buf[rs, :] = d_resid
            dres.send(at)
            low = d_resid.astype(BF16)
            dlow.buf[rs, :] = low
            dlowt.buf[:, rs] = low.T
            for row, term in enumerate((d_resid, d_out * unit, d_out)):
                sums[row] = sums[row] + jnp.sum(term, 0, keepdims=True)
        pool.buf[seq : seq + 1, :] = total / count
    sums_st.buf[...] = jnp.zeros_like(sums_st.buf)
    for row in range(3):
        sums_st.buf[row : row + 1, :] = sums[row]


def ln2(run, lengths, res1, ffn, small, out_grad, pool_grad):
    rows, width = res1.shape
    seqs = lengths.shape[0]
    return run(
        functools.partial(ln2_body, seqs),
        "ln2",
        [res1, ffn, Far(out_grad, 4 * seqs), small, pool_grad],
        [
            FarOut((rows, width), BF16, 4 * seqs),
            ((seqs, width), F32),
            FarOut((rows, width), F32, 4 * seqs),
            ((rows, width), BF16),
            ((width, rows), BF16),
            ((8, width), F32),
        ],
        scalars=(lengths,),
        limit=12,
        cost=6,
    )


def gelu_pair(pre):
    bell = jnp.exp(pre * pre * -0.5)
    t = 1.0 / (1.0 + (0.3275911 * SQRT_HALF) * jnp.abs(pre))
    poly = 0.5 * 1.061405429
    poly = poly * t + 0.5 * -1.453152027
    poly = poly * t + 0.5 * 1.421413741
    poly = poly * t + 0.5 * -0.284496736
    poly = poly * t + 0.5 * 0.254829592
    tail = poly * t * bell
    phi = jnp.where(pre >= 0.0, 1.0 - tail, tail)
    return pre * phi, phi + pre * bell * INV_SQRT_2PI


ROW_TILE = 256


def ffn_fwd_body(own, scalars, loads, stores, bias_scr):
    spot_ref = scalars[0]
    h, bias, *loads = loads
    h, bias = h(), bias()
    acts, ders, (acc_out, *kept) = stores[:2], stores[2:4], stores[4:]
    acc = acc_out.buf
    units = bias.shape[1]
    rows, width = h.shape
    tiles = [slice(at, at + ROW_TILE) for at in range(0, rows, ROW_TILE)]
    for step in range(2):
        if own:
            wu, wd = loads[2 * step](), loads[2 * step + 1]()
        else:
            pieces, part = loads[:8], loads[8]
            wu, wd = kept[step].buf, kept[2 + step].buf
            for flip in range(2):
                at = pl.ds(pl.multiple_of((spot_ref[1] ^ flip) * units, units), units)
                wu[:, at] = pieces[4 * step + flip]()[...]
                at = pl.ds(pl.multiple_of((spot_ref[2] ^ flip) * units, units), units)
                wd[at, :] = pieces[4 * step + 2 + flip]()[...]
        spot = spot_ref[0] ^ step
        bias_scr[:, :units] = bias[pl.ds(2 + 2 * spot, 1), :]
        bias_scr[:, units:] = bias[pl.ds(3 + 2 * spot, 1), :]

        def down(at, act):
            share = dot(act, wd[...])
            if step == 0 and own:
                acc[tiles[at], :] = share
            elif step == 0:
                acc[tiles[at], :] = part()[tiles[at], :] + share
            else:
                acc[tiles[at], :] += share

        pre = dot(h[tiles[0], :], wu[...]) + bias_scr[...]
        before = None
        for at, rs in enumerate(tiles):
            now = pre
            if at + 1 < len(tiles):
                pre = dot(h[tiles[at + 1], :], wu[...]) + bias_scr[...]
            act, der = gelu_pair(now)
            act = act.astype(BF16)
            acts[step].buf[rs, :] = act
            ders[step].buf[rs, :] = der.astype(BF16)
            if before is not None:
                down(at - 1, before)
            before = act
        down(len(tiles) - 1, before)
        ders[step].send()


def half_view(axis, units, which):
    def view(ref, spot_ref):
        at = pl.ds(pl.multiple_of((spot_ref[0] ^ which) * units, units), units)
        return ref.at[:, at] if axis else ref.at[at, :]

    return view


def ffn_fwd(run, spot, h, bias, wu=None, wd=None, pieces=(), part=None):
    rows, width = h.shape
    own = wu is not None
    units = 2 * bias.shape[1]
    ins = [h, bias]
    if own:
        for step in range(2):
            ins.append(Far(wu, shape=(width, units), view=half_view(1, units, step)))
            ins.append(Far(wd, shape=(units, width), view=half_view(0, units, step)))
    else:
        ins += [p if at in (5, 7) else Far(p) for at, p in enumerate(pieces)] + [part]
    block = ((rows, units), BF16)
    away = FarOut((rows, units), BF16)
    outs = [block, block, away, away if own else block, ((rows, width), F32)]
    if not own:
        outs += [((width, units), BF16)] * 2 + [((units, width), BF16)] * 2
    results = run(
        functools.partial(ffn_fwd_body, own),
        "ffn_fwd",
        ins,
        outs,
        scratch=[pltpu.VMEM((1, units), F32)],
        scalars=(spot,),
        limit=14,
        cost=10,
    )
    return (results[0:2], results[2:4], *results[4:])


def split_out(x_bit, row_half, value, away, mine):
    @pl.when(x_bit == row_half)
    def _():
        mine[...] = value

    @pl.when(x_bit != row_half)
    def _():
        away[...] = value


def down_send_body(scalars, loads, stores):
    dft, far, own = [load() for load in loads]
    for at, act in enumerate((far, own)):
        stores[0].buf[at] = dot(dft[...], act[...]).astype(BF16)


def down_send(run, dft, far_act, own_act):
    width, rows = dft.shape
    units = far_act[0].shape[1]
    return run(
        down_send_body,
        "down_send",
        [dft, far_act[1], own_act[1]],
        [((2, width, units), BF16)],
        cost=3,
    )


def down_keep_body(scalars, loads, stores):
    dft, far, own, got = loads
    far_left, away, far_right, own_left_away, own_left, own_right = [store.buf for store in stores]
    x_bit = scalars[0][1]
    rows, half = far_right.shape
    for which, act in enumerate((far, own)):
        for part in range(2):
            rs = slice(part * rows, (part + 1) * rows)
            total = dot(dft()[rs, :], act()[...]) + got(which)[which, rs, :].astype(F32)
            low = total.astype(BF16)
            left, right = low[:, :half], low[:, half:]
            if which == 0:
                far_left[rs, :] = left
                split_out(x_bit, part, right, away.at[0], far_right)
            else:
                split_out(x_bit, part, left, own_left_away, own_left)
                split_out(x_bit, part, right, away.at[1], own_right)


def down_keep(run, spot, dft, far_act, own_act, got):
    width, rows = dft.shape
    units = far_act[0].shape[1]
    half = units // 2
    small = ((width // 2, half), BF16)
    return run(
        down_keep_body,
        "down_keep",
        [dft, far_act[0], own_act[0], got],
        [((width, half), BF16), ((2, width // 2, half), BF16), small, small, small, small],
        scalars=(spot,),
        limit=8,
        cost=5,
    )


def ffn_bwd_body(mode, scalars, loads, stores):
    wd, der, df, ht, *got = loads
    dpre, sums, *outs = [store.buf for store in stores]
    dpre_out = stores[0]
    rows = df.buf.shape[0]
    width = ht.buf.shape[0]
    tile = rows // 4
    bias = jnp.zeros((1, dpre.shape[1]), F32)
    tiles = [slice(at * tile, (at + 1) * tile) for at in range(4)]
    d_act = dot_nt(df()[tiles[0], :], wd()[...])
    for at, rs in enumerate(tiles):
        now = d_act
        if at + 1 < len(tiles):
            d_act = dot_nt(df()[tiles[at + 1], :], wd()[...])
        d_pre = (der()[rs, :].astype(F32) * now).astype(BF16)
        dpre[rs, :] = d_pre
        bias = bias + jnp.sum(d_pre.astype(F32), 0, keepdims=True)
    dpre_out.send()
    sums[...] = jnp.broadcast_to(bias, sums.shape)
    half = width // 2
    x_bit = scalars[0][1]
    for part in range(2):
        rs = slice(part * half, (part + 1) * half)
        total = dot(ht()[rs, :], dpre[...])
        if mode == "send":
            outs[0][rs, :] = total.astype(BF16)
            continue
        low = (total + got[0]()[rs, :].astype(F32)).astype(BF16)
        left, right = low[:, :half], low[:, half:]
        if mode == "far":
            outs[0][rs, :] = left
            split_out(x_bit, part, right, outs[1], outs[2])
        else:
            split_out(x_bit, part, left, outs[0], outs[1])
            split_out(x_bit, part, right, outs[2], outs[3])


def ffn_bwd(run, mode, spot, df, ht, der, which, wd, wd_view, got=None):
    rows, width = df.shape
    units = der[which].shape[1]
    der_in = Far(der[which]) if wd_view or which == 0 else der[which]
    ins = [Far(wd, shape=(units, width), view=wd_view) if wd_view else wd, der_in, df, ht]
    outs = [FarOut((rows, units), BF16) if mode == "send" else ((rows, units), BF16), ((8, units), F32)]
    small = ((width // 2, units // 2), BF16)
    if mode == "send":
        outs += [((width, units), BF16)]
    elif mode == "far":
        outs += [((width, units // 2), BF16), small, small]
    else:
        outs += [small] * 4
    if got is not None:
        ins.append(got)
    return run(
        functools.partial(ffn_bwd_body, mode),
        "ffn_bwd",
        ins,
        outs,
        scalars=(spot,),
        limit=10,
        cost=5,
    )


def hidden_back_body(scalars, loads, stores, acc_scr):
    (*pairs, resid_in, dres2_in, small) = loads
    dres, dlow, sums_out = stores
    sums = sums_out.buf
    small = small()
    rows = acc_scr.shape[0]
    tile = rows // 4
    tiles = [slice(at * tile, (at + 1) * tile) for at in range(4)]
    for pair in range(3):
        d_pre, weight = pairs[2 * pair](), pairs[2 * pair + 1]()
        for rs in tiles:
            share = dot_nt(d_pre[rs, :], weight[...])
            acc_scr[rs, :] = share if pair == 0 else acc_scr[rs, :] + share
    d_pre, weight = pairs[6](), pairs[7]()
    for at, rs in enumerate(tiles):
        d_hidden = acc_scr[rs, :] + dot_nt(d_pre[rs, :], weight[...]) + dres2_in(at)[rs, :]
        unit, rstd = norm_parts(resid_in(at)[rs, :])
        d_resid = norm_back(unit, rstd, small[1:2, :], d_hidden)
        dres.buf[rs, :] = d_resid
        dres.send(at)
        dlow.buf[rs, :] = d_resid.astype(BF16)
        for row, term in enumerate((d_resid, d_hidden * unit, d_hidden)):
            total = jnp.sum(term, 0, keepdims=True)
            if at == 0:
                sums[row : row + 1, :] = total
            else:
                sums[row : row + 1, :] += total


def hidden_back(run, spot, d_pres, wu, wu_far, resid, d_res2, small):
    rows, width = resid.shape
    units = wu.shape[1] // 2
    keep, send, far_keep, far_send = d_pres
    near = [Far(wu, shape=(width, units), view=half_view(1, units, which)) for which in range(2)]
    ins = [far_keep, wu_far[0], keep, near[0], Far(far_send), wu_far[1], Far(send), near[1]]
    return run(
        hidden_back_body,
        "hidden_back",
        ins + [resid, Far(d_res2, 4), small],
        [FarOut((rows, width), F32, 4), ((rows, width), BF16), ((8, width), F32)],
        scalars=(spot,),
        scratch=[pltpu.VMEM((rows, width), F32)],
        limit=22,
        cost=8,
    )


def attn_bwd_body(slots, begin, extent, last, scalars, loads, stores, *scratch):
    wo, da, *loads = [load() for load in loads]
    scale = HD**-0.5
    heads = extent // HD
    width = da.shape[1]
    count = len(slots)
    outs = stores[:count]
    span = loads[0].shape[0]
    mixed = []
    for slot in slots:
        d_attn = da[slot * span : (slot + 1) * span, :]
        mixed.append(dot_nt(d_attn, wo[begin : begin + extent, :]).astype(BF16))
    for number in range(count):
        q, kt, v, probs_ref = loads[4 * number : 4 * number + 4]
        out = outs[number].buf
        d_query = []
        for head in range(heads):
            cols = slice(begin + head * HD, begin + (head + 1) * HD)
            d_mixed_h = mixed[number][:, head * HD : (head + 1) * HD]
            d_probs = dot_nt(v[:, cols], d_mixed_h)
            low_probs = probs_ref[head]
            probs = low_probs.astype(F32)
            inner = jnp.sum(d_probs * probs, axis=0, keepdims=True)
            d_scores = (probs * (d_probs - inner)).astype(BF16)
            at = extent + head * HD
            out[:, at : at + HD] = dot(d_scores, q[:, cols]).astype(BF16)
            at = 2 * extent + head * HD
            out[:, at : at + HD] = dot(low_probs, d_mixed_h).astype(BF16)
            d_query.append((dot(kt[cols, :], d_scores) * scale).astype(BF16))
        out[:, :extent] = jnp.concatenate(d_query, 0).T
        outs[number].send()
    if not last:
        return
    before = loads[4 * count :]
    seqs = da.shape[0] // span
    mts, xts, before = before[:seqs], before[seqs : 2 * seqs], before[2 * seqs :]
    grads = [*before, *[store.buf for store in outs]]
    keep, send, sums = [store.buf for store in stores[count:]]
    (fold_scr,) = scratch
    core = scalars[0][0]
    g_out = None
    for slot, mt in enumerate(mts):
        share = dot(mt[begin : begin + extent, :], da[slot * span : (slot + 1) * span, :])
        g_out = share if g_out is None else g_out + share
    g_out = g_out.astype(BF16)
    for part in range(width // extent):
        fold_scr[part * extent : (part + 1) * extent, :] = g_out[:, part * extent : (part + 1) * extent]
    half = width // 2
    for part in range(2):
        rs = slice(part * half, (part + 1) * half)
        total = None
        for xt, grad in zip(xts, grads):
            share = dot(xt[rs, :], grad[...])
            total = share if total is None else total + share
        low = total.astype(BF16)

        def put(ref, low=low, rs=rs):
            ref[:, : 3 * extent] = low
            ref[:, 3 * extent :] = fold_scr[rs, :]

        @pl.when(core == part)
        def _(put=put):
            put(keep)

        @pl.when(core != part)
        def _(put=put):
            put(send)

    total = 0.0
    for grad in grads:
        total = total + jnp.sum(grad[...].astype(F32), 0, keepdims=True)
    sums[...] = jnp.broadcast_to(total, sums.shape)


def attn_bwd(run, group, spot, slots, d_attn, wo, xts, saved, before=()):
    rows, width = d_attn.shape
    begin, extent = group
    span = rows // len(xts)
    last = slots[-1] == len(xts) - 1
    ins = [wo, d_attn]
    for slot in slots:
        q, kt, v, _, probs_a, probs_b = saved[slot]
        ins += [q, kt, v, probs_a if begin == 0 else probs_b]
    outs = [FarOut((span, 3 * extent), BF16)] * len(slots)
    if last:
        ins += [saved[slot][3] for slot in range(len(xts))] + list(xts) + list(map(Far, before))
        outs += [
            ((width // 2, 4 * extent), BF16),
            ((width // 2, 4 * extent), BF16),
            ((8, 3 * extent), F32),
        ]
    return run(
        functools.partial(attn_bwd_body, slots, begin, extent, last),
        "attn_bwd",
        ins,
        outs,
        scalars=(spot,),
        scratch=[pltpu.VMEM((width, extent), BF16)] if last else [],
        limit=10,
        cost=6,
    )


def tokens_back_body(groups, seqs, scalars, loads, stores):
    *loads, dres = loads
    (out,) = stores
    rows = out.buf.shape[0]
    span = rows // seqs
    per = 2 * seqs + 3
    for which in range(2):
        wq, wk, wv, *grads = loads[per * which : per * (which + 1)]
        for number, (begin, extent) in enumerate(groups):
            last = which == 1 and number == len(groups) - 1
            for slot in range(seqs):
                rs = slice(slot * span, (slot + 1) * span)
                grad = grads[number * seqs + slot]()
                total = None
                for mat, weight in enumerate((wq, wk, wv)):
                    share = dot_nt(
                        grad[:, mat * extent : (mat + 1) * extent], weight()[:, begin : begin + extent]
                    )
                    total = share if total is None else total + share
                if which or number:
                    total = total + out.buf[rs, :]
                if last:
                    total = total + dres(slot)[rs, :]
                out.buf[rs, :] = total
                if last:
                    out.send(slot)


def tokens_back(run, groups, seqs, d_resid, far, own):
    rows, width = d_resid.shape
    return run(
        functools.partial(tokens_back_body, groups, seqs),
        "tokens_back",
        [Far(a) for a in (*far, *own)] + [Far(d_resid, seqs)],
        [FarOut((rows, width), F32, seqs)],
        limit=22,
        cost=10,
    )


def collect_body(scalars, loads, stores):
    keep, send, one, two, a_sums, b_sums = [load() for load in loads]
    out = stores[0].buf
    core = scalars[0][0]
    out[...] = jnp.zeros_like(out)
    out[pl.ds(core, 1), :] = keep[0:1, :]
    out[pl.ds(1 - core, 1), :] = send[0:1, :]
    extent_a, extent_b = a_sums.shape[1] // 3, b_sums.shape[1] // 3
    local = extent_a + extent_b
    for at, mat in enumerate((0, 2)):
        begin = at * local
        out[2:3, begin : begin + extent_a] = a_sums[0:1, mat * extent_a : (mat + 1) * extent_a]
        out[2:3, begin + extent_a : begin + local] = b_sums[0:1, mat * extent_b : (mat + 1) * extent_b]
    out[3:6, :] = one[0:3, :]
    out[6:9, :] = two[0:3, :]


def collect(run, spot, *sums):
    return run(collect_body, "collect", list(sums), [((16, sums[2].shape[1]), F32)], scalars=(spot,))


def finish_attn_body(begin, n_prev, scalars, loads, stores, full_scr, fold_scr, go_scr, sems):
    core = scalars[0][0]
    mine, other = [load() for load in loads[:2]]
    rows = mine.shape[0]
    extent, width = go_scr.shape
    copies = []

    def ship(src, dst):
        copies.append(pltpu.make_async_copy(src, dst, sems.at[len(copies)]))
        copies[-1].start()

    for flip, ref in enumerate((mine, other)):
        at = pl.ds(pl.multiple_of((core ^ flip) * rows, rows), rows)
        fold_scr[at, :] = ref[:, 3 * extent :]
        for mat in range(3):
            full_scr[mat, at, :] = ref[:, mat * extent : (mat + 1) * extent].astype(F32)
    for mat in range(3):
        ship(full_scr.at[mat], stores[mat].at[:, begin : begin + extent])
    for part in range(width // extent):
        cols = slice(part * extent, (part + 1) * extent)
        go_scr[:, cols] = fold_scr[cols, :].astype(F32)
    ship(go_scr, stores[3].at[begin : begin + extent, :])
    for copy in copies:
        copy.wait()


def finish_attn(run, group, local, spot, mine, other, previous=()):
    begin, extent = group
    width = 2 * mine.shape[0]
    return run(
        functools.partial(finish_attn_body, begin, len(previous)),
        "finish_attn",
        [mine, other] + [Raw(p) for p in previous],
        [Raw(shape=(width, local), dtype=F32)] * 3 + [Raw(shape=(local, width), dtype=F32)],
        scratch=[
            pltpu.VMEM((3, width, extent), F32),
            pltpu.VMEM((width, extent), BF16),
            pltpu.VMEM((extent, width), F32),
            pltpu.SemaphoreType.DMA((4,)),
        ],
        scalars=(spot,),
        aliases={2 + i: i for i in range(len(previous))},
        limit=8,
        cost=2,
    )


def finish_body(kind, scalars, loads, stores, scr, sems):
    mine, other = [load() for load in loads]
    (out,) = stores
    width, units = mine.shape
    parts = 2
    extent = units // parts
    copies = []
    for flip, ref in enumerate((mine, other)):
        for part in range(parts):
            at = flip * parts + part
            begin = pl.multiple_of((scalars[0][0] ^ flip) * units + part * extent, extent)
            value = ref[:, part * extent : (part + 1) * extent].astype(F32)
            scr[at] = value if kind == "up" else value.T
            place = pl.ds(begin, extent)
            dst = out.at[:, place] if kind == "up" else out.at[place, :]
            copies.append(pltpu.make_async_copy(scr.at[at], dst, sems.at[at]))
            copies[-1].start()
    for copy in copies:
        copy.wait()


def finish(run, kind, spot, mine, other):
    width, units = mine.shape
    shape = (width, 2 * units) if kind == "up" else (2 * units, width)
    piece = (width, units // 2) if kind == "up" else (units // 2, width)
    return run(
        functools.partial(finish_body, kind),
        "finish_" + kind,
        [mine, other],
        [Raw(shape=shape, dtype=F32)],
        scratch=[pltpu.VMEM((4, *piece), F32), pltpu.SemaphoreType.DMA((4,))],
        scalars=(spot,),
        limit=8,
        cost=3,
    )


def add(*terms):
    total = terms[0].astype(F32)
    for term in terms[1:]:
        total = total + term.astype(F32)
    return total.astype(BF16)


def local(
    n_batch,
    tokens,
    lengths,
    w_query,
    b_query,
    w_key,
    w_value,
    b_value,
    w_out,
    b_out,
    gain_one,
    shift_one,
    w_up,
    b_up,
    w_down,
    b_down,
    gain_two,
    shift_two,
    out_grad,
    pool_grad,
):
    rows, width = tokens.shape
    seqs = lengths.shape[0]
    half = w_query.shape[1]
    groups = groups_of(half)
    place = lax.axis_index("batch").astype(jnp.int32)
    core, x_bit, z_low, z_high = [(place >> bit) & 1 for bit in range(4)]
    spot = jnp.stack([core, x_bit, z_low])
    run = Kernels()

    def swap(array, bit):
        return lax.ppermute(array, "batch", [(i, i ^ bit) for i in range(n_batch)])

    def swap_core(array):
        return swap(array, 1)

    def swap_x(array):
        return swap(array, 2)

    def swap_y(array):
        return lax.ppermute(array, "tensor", [(0, 1), (1, 0)])

    bias_rows = jnp.concatenate([b_query, b_value, b_up]).reshape(-1, half)
    bias_rows = jnp.pad(bias_rows, ((0, 16 - bias_rows.shape[0]), (0, 0)))
    own_bias = bias_rows.astype(F32)
    small = jnp.stack([b_out, gain_one, shift_one, b_down, gain_two, shift_two]).astype(F32)
    ex, ez = pack(run, spot, w_query, w_key, w_value, w_out, bias_rows)
    ex, ez = swap_y(ex), swap_y(ez)
    fx, fz = pack_units(run, spot, w_up, w_down, half)
    fx, fz = swap_y(fx), swap_y(fz)
    own_saved, xts = [], []
    own = (w_query, w_key, w_value, own_bias)
    for slot in range(seqs):
        saved, xt = attn_fwd(run, lengths, seqs, (slot,), tokens, own=own)
        own_saved += saved
        xts.append(xt)
        if slot == 0:
            ex, ez = run.wait(ex, ez)
            ex_x, ez_z = swap_x(ex), swap(ez, 4)
            ex_c, ez_c = swap_core(ex), swap_core(ez)
    ex_x, ez_z, ex_c, ez_c, fx = run.wait(ex_x, ez_z, ex_c, ez_c, fx)
    ex_xc, ez_zc = swap_core(ex_x), swap_core(ez_z)
    fx_x, fx_c = swap_x(fx), swap_core(fx)
    pieces = (ex, ex_x, ex_c, ex_xc, ez, ez_z, ez_c, ez_zc)
    near_mt = [saved[3] for saved in own_saved]
    far_saved, resid_one, hidden, hidden_t, far_q, far_k, far_v, far_o, far_bias = attn_fwd(
        run, lengths, seqs, tuple(range(seqs)), tokens, far=(spot, pieces, near_mt, w_out, small)
    )
    fz, fx_x, fx_c = run.wait(fz, fx_x, fx_c)
    fz_z, fz_c = swap(fz, 4), swap_core(fz)
    fx_xc = swap_core(fx_x)
    own_act, own_der, ffn_part = ffn_fwd(run, spot, hidden, own_bias, wu=w_up, wd=w_down)
    fx_xc, fz_z, fz_c = run.wait(fx_xc, fz_z, fz_c)
    fz_zc = swap_core(fz_z)
    far_act, far_der, ffn_sum, *far_weights = ffn_fwd(
        run,
        spot,
        hidden,
        far_bias,
        pieces=(fx, fx_x, fz, fz_z, fx_c, fx_xc, fz_c, fz_zc),
        part=ffn_part,
    )
    wu_far, wd_far = far_weights[:2], far_weights[2:]
    output, pooled, d_resid_two, d_ffn, d_ffn_t, sums_two = ln2(
        run, lengths, resid_one, ffn_sum, small, out_grad, pool_grad
    )

    def pick(array, at):
        return lax.dynamic_index_in_dim(array, at, 0, keepdims=False)

    def halves(array):
        return array.reshape(2, array.shape[0] // 2, array.shape[1])

    def split(bit, *terms):
        parts = [halves(t) for t in terms]
        return add(*[pick(t, 1 - bit) for t in parts]), add(*[pick(t, bit) for t in parts])

    def join(bit, mine, got):
        return jnp.concatenate(
            [jnp.where(bit == 0, mine, got), jnp.where(bit == 0, got, mine)], axis=0
        )

    def rest(array):
        bit = 16
        while bit < n_batch:
            array = add(array, swap(array, bit))
            bit *= 2
        return array

    def cross_two(left_got, right_got, away, far):
        return swap_x(add(away, pick(halves(left_got), 1 - x_bit))), swap_y(add(far, right_got))

    def cross_three(left, left_got, left_x, right, right_x, right_y):
        mine = pick(halves(left_got), x_bit)
        return jnp.concatenate([add(left, mine, left_x), add(right, right_x, right_y)], axis=1)

    d_got = swap_core(run.wait(down_send(run, d_ffn_t, far_act, own_act)))
    bwd = functools.partial(ffn_bwd, run)
    dp_fs, bs_fs, u_send = bwd("send", spot, d_ffn, hidden_t, far_der, 1, wd_far[1], None)
    d_got, u_send = run.wait(d_got, u_send)
    uf_got = swap_core(u_send)
    df_left, d_away, df_right, do_left_away, do_left, do_right = down_keep(
        run, spot, d_ffn_t, far_act, own_act, d_got
    )
    df_left, d_away = run.wait(df_left, d_away)
    d_left_y, d_right_x = swap_y(df_left), swap_x(d_away)
    dp_os, bs_os, u_send = bwd("send", spot, d_ffn, hidden_t, own_der, 1, w_down, half_view(0, width, 1))
    uf_got, u_send = run.wait(uf_got, u_send)
    uo_got = swap_core(u_send)
    dp_fk, bs_fk, uf_left, uf_away, uf_right = bwd(
        "far", spot, d_ffn, hidden_t, far_der, 0, wd_far[0], None, uf_got
    )
    uo_got, uf_left, uf_away = run.wait(uo_got, uf_left, uf_away)
    u_left_y, uf_right_x = swap_y(uf_left), swap_x(uf_away)
    dp_ok, bs_ok, uo_left_away, uo_left, uo_right_away, uo_right = bwd(
        "own", spot, d_ffn, hidden_t, own_der, 0, w_down, half_view(0, width, 0), uo_got
    )
    d_left_y, d_right_x, uo_right_away = run.wait(d_left_y, d_right_x, uo_right_away)
    d_left_x, d_right_y = cross_two(d_left_y, d_right_x[0], do_left_away, df_right)
    uo_right_x = swap_x(uo_right_away)
    d_resid_one, d_attn, sums_one = hidden_back(
        run, spot, (dp_ok, dp_os, dp_fk, dp_fs), w_up, wu_far, resid_one, d_resid_two, small
    )

    first, others = (0,), tuple(range(1, seqs))
    far_bwd = functools.partial(
        attn_bwd, run, spot=spot, d_attn=d_attn, wo=far_o, xts=xts, saved=far_saved
    )
    own_bwd = functools.partial(
        attn_bwd, run, spot=spot, d_attn=d_attn, wo=w_out, xts=xts, saved=own_saved
    )
    d_left_x, d_right_y = run.wait(d_left_x, d_right_y)
    d_rows = cross_three(do_left, d_left_y, d_left_x, do_right, d_right_x[1], d_right_y)
    d_away, d_mine = split(z_low, d_rows)
    d_got = swap(d_away, 4)
    fa_0 = far_bwd(groups[0], slots=first)
    d_got = run.wait(d_got)
    d_away, d_mine = split(z_high, d_mine, d_got)
    d_got = swap(d_away, 8)
    *fa_1, fa_keep, fa_send, fa_sums = far_bwd(groups[0], slots=others, before=(fa_0,))
    d_got, u_left_y, uf_right_x, uo_right_x, fa_send = run.wait(
        d_got, u_left_y, uf_right_x, uo_right_x, fa_send
    )
    u_left_x, u_right_y = cross_two(u_left_y, uf_right_x, uo_left_away, uf_right)
    fa_got = swap_core(fa_send)
    d_mine = rest(add(d_mine, d_got))
    d_got = swap(d_mine, 8)
    *fb, fb_keep, fb_send, fb_sums = far_bwd(groups[1], slots=first + others)
    fa_got, d_got, u_left_x, u_right_y, fb_send = run.wait(fa_got, d_got, u_left_x, u_right_y, fb_send)
    fa_y = swap_y(add(fa_keep, fa_got))
    u_rows = cross_three(uo_left, u_left_y, u_left_x, uo_right, uo_right_x, u_right_y)
    u_away, u_mine = split(z_low, u_rows)
    u_got = swap(u_away, 4)
    d_mine = join(z_high, d_mine, d_got)
    d_got = swap(d_mine, 4)
    fb_got = swap_core(fb_send)
    oa_0 = own_bwd(groups[0], slots=first)

    u_got, fb_got = run.wait(u_got, fb_got)
    u_away, u_mine = split(z_high, u_mine, u_got)
    u_got = swap(u_away, 8)
    fb_y = swap_y(add(fb_keep, fb_got))
    sums_got = swap_y(collect(run, spot, bs_fk, bs_fs, sums_one, sums_two, fa_sums, fb_sums))
    *oa_1, oa_keep, oa_send, oa_sums = own_bwd(groups[0], slots=others, before=(oa_0,))
    u_got, d_got, fa_y, oa_send = run.wait(u_got, d_got, fa_y, oa_send)
    oa_got = swap_core(oa_send)
    u_mine = rest(add(u_mine, u_got))
    u_got = swap(u_mine, 8)
    d_mine = join(z_low, d_mine, d_got)
    d_got = swap_x(d_mine)
    *ob, ob_keep, ob_send, ob_sums = own_bwd(groups[1], slots=first + others)

    oa_got, u_got, fb_y, ob_send = run.wait(oa_got, u_got, fb_y, ob_send)
    ob_got = swap_core(ob_send)
    a_away, a_mine = split(x_bit, oa_keep, oa_got, fa_y)
    a_got = swap_x(a_away)
    u_mine = join(z_high, u_mine, u_got)
    u_got = swap(u_mine, 4)
    ob_got, sums_got = run.wait(ob_got, sums_got)
    b_away, b_mine = split(x_bit, ob_keep, ob_got, fb_y)
    b_got = swap_x(b_away)
    sums = collect(run, spot, bs_ok, bs_os, sums_one, sums_two, oa_sums, ob_sums) + sums_got
    sums_got = swap_x(sums)
    d_tokens = tokens_back(
        run,
        groups,
        seqs,
        d_resid_one,
        (far_q, far_k, far_v, fa_0, *fa_1, *fb),
        (w_query, w_key, w_value, oa_0, *oa_1, *ob),
    )
    a_got, b_got = run.wait(a_got, b_got)
    a_away, a_mine = split(z_low, a_mine, a_got)
    a_got = swap(a_away, 4)
    b_away, b_mine = split(z_low, b_mine, b_got)
    b_got = swap(b_away, 4)
    u_got, d_got, sums_got = run.wait(u_got, d_got, sums_got)
    u_mine = join(z_low, u_mine, u_got)
    u_got = swap_x(u_mine)
    d_mine = join(x_bit, d_mine, d_got)
    d_other = swap_core(d_mine)
    sums = sums + sums_got
    sums_got = swap(sums, 1)

    a_got, b_got = run.wait(a_got, b_got)
    a_mine = add(a_mine, a_got)
    a_got = swap(a_mine, 8)
    b_mine = add(b_mine, b_got)
    b_got = swap(b_mine, 8)
    d_other, sums_got = run.wait(d_other, sums_got)
    sums = sums + sums_got
    sums_got = swap(sums, 4)
    g_down = finish(run, "down", spot, d_mine, d_other)

    a_got = run.wait(a_got)
    a_mine = rest(add(a_mine, a_got))
    a_got = swap(a_mine, 4)
    b_got = run.wait(b_got)
    b_mine = rest(add(b_mine, b_got))
    b_got = swap(b_mine, 4)
    u_got, sums_got = run.wait(u_got, sums_got)
    u_mine = join(x_bit, u_mine, u_got)
    u_other = swap_core(u_mine)
    sums = sums + sums_got
    sums_got = swap(sums, 8)
    a_got = run.wait(a_got)
    a_mine = join(z_low, a_mine, a_got)
    a_got = swap_x(a_mine)
    b_got = run.wait(b_got)
    b_mine = join(z_low, b_mine, b_got)
    b_got = swap_x(b_mine)
    u_other, sums_got = run.wait(u_other, sums_got)
    sums = sums + sums_got
    bit = 16
    while bit < n_batch:
        sums = sums + swap(sums, bit)
        bit *= 2
    g_up = finish(run, "up", spot, u_mine, u_other)
    a_got, sums = run.wait(a_got, sums)
    a_mine = join(x_bit, a_mine, a_got)
    a_other = swap_core(a_mine)
    b_got = run.wait(b_got)
    b_mine = join(x_bit, b_mine, b_got)
    b_other = swap_core(b_mine)
    a_other = run.wait(a_other)
    grads = finish_attn(run, groups[0], half, spot, a_mine, a_other)
    b_other = run.wait(b_other)
    g_query, g_key, g_value, g_out = finish_attn(run, groups[1], half, spot, b_mine, b_other, grads)

    g_bias_up = sums[0:2].reshape(-1)
    g_bias_query, g_bias_value = sums[2, :half], sums[2, half:]
    d_bias_out, d_gain_one, d_shift_one, d_bias_down, d_gain_two, d_shift_two = [sums[3 + i] for i in range(6)]
    return (
        output,
        pooled,
        d_tokens,
        g_query,
        g_bias_query,
        g_key,
        g_value,
        g_bias_value,
        g_out,
        d_bias_out,
        d_gain_one,
        d_shift_one,
        g_up,
        g_bias_up,
        g_down,
        d_bias_down,
        d_gain_two,
        d_shift_two,
    )


def solution(mesh):
    return jax.shard_map(
        functools.partial(local, mesh.shape["batch"]),
        mesh=mesh,
        in_specs=(
            P(("batch", "tensor"), None),
            P(("batch", "tensor")),
            P(None, "tensor"),
            P("tensor"),
            P(None, "tensor"),
            P(None, "tensor"),
            P("tensor"),
            P("tensor", None),
            P(),
            P(),
            P(),
            P(None, "tensor"),
            P("tensor"),
            P("tensor", None),
            P(),
            P(),
            P(),
            P(("batch", "tensor"), None),
            P(("batch", "tensor"), None),
        ),
        out_specs=(
            P(("batch", "tensor"), None),
            P(("batch", "tensor"), None),
            P(("batch", "tensor"), None),
            P(None, "tensor"),
            P("tensor"),
            P(None, "tensor"),
            P(None, "tensor"),
            P("tensor"),
            P("tensor", None),
            P(),
            P(),
            P(),
            P(None, "tensor"),
            P("tensor"),
            P("tensor", None),
            P(),
            P(),
            P(),
        ),
        check_vma=False,
    )
```

```python
import functools

import jax
import jax.numpy as jnp
from jax import lax
from jax.experimental import pallas as pl
from jax.experimental.pallas import tpu as pltpu
from jax.sharding import PartitionSpec as P

HD = 64
EPSILON = 1e-12
NEG_FILL = -1e30
F32 = jnp.float32
BF16 = jnp.bfloat16
MIB = 1024 * 1024
FLOPS_PER_US = 1.1e9
SQRT_HALF = 0.7071067811865476
INV_SQRT_2PI = 0.3989422804014327


def dot(left, right):
    return lax.dot_general(left, right, (((1,), (0,)), ((), ())), preferred_element_type=F32)


def dot_nt(left, right):
    return lax.dot_general(left, right, (((1,), (1,)), ((), ())), preferred_element_type=F32)


def dot_tn(left, right):
    return lax.dot_general(left, right, (((0,), (0,)), ((), ())), preferred_element_type=F32)


class Part:
    def __init__(self, buf):
        self.buf = buf

    def __call__(self, part=None):
        return self.buf

    def send(self, part=0):
        pass

    def finish(self):
        pass


def pieces_of(src, dst, parts, axis):
    if parts == 1:
        return [(src, dst)]
    extent = dst.shape[axis] // parts
    cuts = [(slice(None),) * axis + (pl.ds(part * extent, extent),) for part in range(parts)]
    return [(src.at[cut], dst.at[cut]) for cut in cuts]


class Load:
    def __init__(self, src, buf, sems, first, parts, axis):
        self.buf = buf
        self.copies = [
            pltpu.make_async_copy(*pair, sems.at[first + at])
            for at, pair in enumerate(pieces_of(src, buf, parts, axis))
        ]
        self.waited = [False] * parts
        for copy in self.copies:
            copy.start()

    def __call__(self, part=None):
        for at in range(len(self.copies)) if part is None else (part,):
            if not self.waited[at]:
                self.waited[at] = True
                self.copies[at].wait()
        return self.buf


class Store:
    def __init__(self, buf, dst, sems, first, parts, axis):
        self.buf = buf
        self.copies = [
            pltpu.make_async_copy(*pair, sems.at[first + at])
            for at, pair in enumerate(pieces_of(buf, dst, parts, axis))
        ]
        self.sent = [False] * parts

    def send(self, part=0):
        self.sent[part] = True
        self.copies[part].start()

    def finish(self):
        for at, copy in enumerate(self.copies):
            if not self.sent[at]:
                copy.start()
        for copy in self.copies:
            copy.wait()


class Far:
    def __init__(self, array, parts=1, axis=0, shape=None, view=None):
        self.array, self.parts, self.axis = array, parts, axis
        self.shape = shape or array.shape
        self.view = view or (lambda ref, *_: ref)


class FarOut:
    def __init__(self, shape, dtype, parts=1, axis=0):
        self.shape, self.dtype, self.parts, self.axis = shape, dtype, parts, axis


class Raw:
    def __init__(self, array=None, shape=None, dtype=None):
        self.array, self.shape, self.dtype = array, shape, dtype


class Kernels:
    def __init__(self):
        self.token = None

    def wait(self, *values):
        self.token, values = lax.optimization_barrier((self.token, values))
        return values if len(values) > 1 else values[0]

    def __call__(self, body, name, ins, outs, scalars=(), scratch=(), aliases=None, limit=6, cost=4):
        spec = lambda space: pl.BlockSpec(memory_space=space)
        in_far = [isinstance(i, Far) for i in ins]
        in_raw = [isinstance(i, Raw) for i in ins]
        out_far = [isinstance(o, FarOut) for o in outs]
        out_raw = [isinstance(o, Raw) for o in outs]
        in_spaces = [pltpu.HBM if f or r else pltpu.VMEM for f, r in zip(in_far, in_raw)]
        out_spaces = [pltpu.HBM if f or r else pltpu.VMEM for f, r in zip(out_far, out_raw)]
        arrays = [i.array if f or r else i for i, f, r in zip(ins, in_far, in_raw)]
        out_types = [(o.shape, o.dtype) if f or r else o for o, f, r in zip(outs, out_far, out_raw)]
        buffers = [pltpu.VMEM(i.shape, i.array.dtype) for i, f in zip(ins, in_far) if f]
        buffers += [pltpu.VMEM(o.shape, o.dtype) for o, f in zip(outs, out_far) if f]
        n_sem = sum(i.parts for i, f in zip(ins, in_far) if f)
        n_sem += sum(o.parts for o, f in zip(outs, out_far) if f)
        n_scalar, n_in, n_out, n_buf = len(scalars), len(ins), len(outs), len(buffers)
        first = self.token is None

        def kernel(*refs):
            scalar_refs, refs = refs[:n_scalar], refs[n_scalar:]
            in_refs, refs = refs[:n_in], refs[n_in + (not first) :]
            out_refs, token_ref, refs = refs[:n_out], refs[n_out], refs[n_out + 1 :]
            bufs, sems, rest = list(refs[:n_buf]), refs[n_buf], refs[n_buf + 1 :]
            at, loads, stores = 0, [], []
            for i, f, r, ref in zip(ins, in_far, in_raw, in_refs):
                if f:
                    src = i.view(ref, *scalar_refs)
                    loads.append(Load(src, bufs.pop(0), sems, at, i.parts, i.axis))
                    at += i.parts
                else:
                    loads.append(ref if r else Part(ref))
            for o, f, r, ref in zip(outs, out_far, out_raw, out_refs):
                if f:
                    stores.append(Store(bufs.pop(0), ref, sems, at, o.parts, o.axis))
                    at += o.parts
                else:
                    stores.append(ref if r else Part(ref))
            body(scalar_refs, loads, stores, *rest)
            token_ref[...] = jnp.zeros_like(token_ref)
            for load, f in zip(loads, in_far):
                if f:
                    load()
            for store, r in zip(stores, out_raw):
                if not r:
                    store.finish()

        *results, self.token = pl.pallas_call(
            kernel,
            name=name,
            in_specs=[spec(pltpu.SMEM)] * n_scalar
            + [spec(space) for space in in_spaces]
            + ([] if first else [spec(pl.ANY)]),
            out_specs=[spec(space) for space in out_spaces] + [spec(pltpu.VMEM)],
            scratch_shapes=buffers + [pltpu.SemaphoreType.DMA((max(n_sem, 1),))] + list(scratch),
            out_shape=[space(*kind) for kind, space in zip(out_types, out_spaces)]
            + [pltpu.VMEM((8, 128), F32)],
            input_output_aliases={k + n_scalar: v for k, v in (aliases or {}).items()},
            compiler_params=pltpu.CompilerParams(vmem_limit_bytes=limit * MIB),
            cost_estimate=pl.CostEstimate(
                flops=int(cost * FLOPS_PER_US), bytes_accessed=0, transcendentals=0
            ),
        )(
            *scalars,
            *[pltpu.with_memory_space_constraint(a, space) for a, space in zip(arrays, in_spaces)],
            *([] if first else [self.token]),
        )
        return results if len(results) > 1 else results[0]


def at_index(index):
    return lambda ref, *_: ref.at[index]


def groups_of(local):
    first = local * 2 // 3
    return ((0, first), (first, local - first))


def pack_body(scalars, loads, stores, sems):
    wq, wk, wv, wo, bias = loads
    ex, ez = [store.buf for store in stores]
    core, x_bit, z_bit = [scalars[0][at] for at in range(3)]
    width, local = wq.shape
    rows = width // 2
    outs = wo.shape[0] // 2
    mine = pl.ds(pl.multiple_of(core * rows, rows), rows)
    mine_out = pl.ds(pl.multiple_of(core * outs, outs), outs)
    query = pltpu.make_async_copy(wq.at[mine, :], ex, sems.at[0])

    @pl.when(x_bit == 0)
    def _():
        query.start()

    @pl.when(x_bit == 1)
    def _():
        pltpu.make_async_copy(wk.at[mine, :], ex, sems.at[0]).start()

    values = []
    for part in range(width // local):
        dst, sem = ez.at[part * outs : (part + 1) * outs, :], sems.at[1 + part]
        own = pl.ds(pl.multiple_of(core * rows + part * outs, outs), outs)
        values.append(pltpu.make_async_copy(wv.at[own, :], dst, sem))

        @pl.when(z_bit == 0)
        def _(copy=values[-1]):
            copy.start()

        @pl.when(z_bit == 1)
        def _(dst=dst, sem=sem, part=part):
            src = wo.at[mine_out, part * local : (part + 1) * local]
            pltpu.make_async_copy(src, dst, sem).start()

    ez[rows:, :] = bias()[...]
    query.wait()
    for copy in values:
        copy.wait()


def pack(run, spot, wq, wk, wv, wo, bias):
    width, local = wq.shape
    return run(
        pack_body,
        "pack",
        [Raw(wq), Raw(wk), Raw(wv), Raw(wo), bias],
        [((width // 2, local), BF16), ((width // 2 + bias.shape[0], local), BF16)],
        scalars=(spot,),
        scratch=[pltpu.SemaphoreType.DMA((1 + width // local,))],
        cost=2,
    )


def pack_units_body(scalars, loads, stores, sems):
    wu, wd = loads
    fx, fz = [store.buf for store in stores]
    core, x_bit, z_bit = [scalars[0][at] for at in range(3)]
    units = fx.shape[1]
    up = pl.ds(pl.multiple_of((2 * core + x_bit) * units, units), units)
    down = pl.ds(pl.multiple_of((2 * core + z_bit) * units, units), units)
    copies = [
        pltpu.make_async_copy(wu.at[:, up], fx, sems.at[0]),
        pltpu.make_async_copy(wd.at[down, :], fz, sems.at[1]),
    ]
    for copy in copies:
        copy.start()
    for copy in copies:
        copy.wait()


def pack_units(run, spot, wu, wd, units):
    width = wu.shape[0]
    return run(
        pack_units_body,
        "pack_units",
        [Raw(wu), Raw(wd)],
        [((width, units), BF16), ((units, width), BF16)],
        scalars=(spot,),
        scratch=[pltpu.SemaphoreType.DMA((2,))],
        cost=2,
    )


def assemble(spot_ref, pieces, wq, wk, wv, wo, bias):
    core, x_bit, z_bit = spot_ref[0], spot_ref[1], spot_ref[2]
    local, width = wo.shape
    rows = width // 2
    outs = local // 2
    for c_flip in range(2):
        spot = core ^ c_flip
        at = pl.ds(pl.multiple_of(spot * rows, rows), rows)
        out_at = pl.ds(pl.multiple_of(spot * outs, outs), outs)
        for flip in range(2):
            piece = pieces[2 * c_flip + flip]()
            for mat, ref in enumerate((wq, wk)):

                @pl.when((x_bit ^ flip) == mat)
                def _(piece=piece, at=at, ref=ref):
                    ref[at, :] = piece[...]

            piece = pieces[4 + 2 * c_flip + flip]()

            @pl.when((z_bit ^ flip) == 0)
            def _(piece=piece, at=at):
                wv[at, :] = piece[0:rows, :]

            @pl.when((z_bit ^ flip) == 1)
            def _(piece=piece, out_at=out_at):
                for part in range(width // local):
                    cols = slice(part * local, (part + 1) * local)
                    wo[out_at, cols] = piece[part * outs : (part + 1) * outs, :]

    bias[...] = pieces[4]()[rows : rows + bias.shape[0], :].astype(F32)


SLOTS = 4


def attn_fwd_body(slots, span, heads, first, scalars, loads, stores, k_scr, vt_scr, p_scr, sems):
    len_ref = scalars[0]
    count = len(slots)
    if first:
        x_in, wq_in, wk_in, wv_in, bias_in = loads
        bias = bias_in()
    else:
        pieces, (x_in, *near_mt, near_wo, small) = loads[:8], loads[8:]
    saved, stores = stores[: 6 * count], stores[6 * count :]
    if first:
        wq, wk, wv = wq_in(), wk_in(), wv_in()
    else:
        resid_out, low_out, lowt_out, *kept, bias_out = stores
        wq, wk, wv, wo = [store.buf for store in kept]
        bias = bias_out.buf
        assemble(scalars[1], pieces, wq, wk, wv, wo, bias)
        for store in kept:
            store.send()
    local = wq.shape[1]
    heads_a = groups_of(local)[0][1] // HD

    def save(at):
        number, head = at // heads, at % heads
        pa_hbm, pb_hbm = saved[6 * number + 4 : 6 * number + 6]
        dst = pa_hbm.at[head] if head < heads_a else pb_hbm.at[head - heads_a]
        return pltpu.make_async_copy(p_scr.at[at % SLOTS], dst, sems.at[at % SLOTS])

    for number, slot in enumerate(slots):
        q_out, kt_out, v_out, mt_out = saved[6 * number : 6 * number + 4]
        rs = slice(number * span, (number + 1) * span)
        x = x_in(number)[rs, :]
        query = (dot(x, wq[...]) + bias[0:1, :]).astype(BF16)
        q_out.buf[...] = query * jnp.asarray(HD**-0.5, BF16)
        k_scr[...] = dot(x, wk[...]).astype(BF16)
        v_out.buf[...] = (dot(x, wv[...]) + bias[1:2, :]).astype(BF16)
        kt_out.buf[...] = k_scr[...].T
        vt_scr[...] = v_out.buf[...].T
        if first:
            stores[number].buf[...] = x.T
            stores[number].send()
        for store in (q_out, kt_out, v_out):
            store.send()
        valid = lax.broadcasted_iota(jnp.int32, (span, span), 0) < len_ref[slot]
        def scores_of(head):
            cols = slice(head * HD, (head + 1) * HD)
            return dot_nt(k_scr[:, cols], q_out.buf[:, cols])

        scores = scores_of(0)
        for head in range(heads):
            at = number * heads + head
            cols = slice(head * HD, (head + 1) * HD)
            now = jnp.where(valid, scores, NEG_FILL)
            if head + 1 < heads:
                scores = scores_of(head + 1)
            top = jnp.max(now, axis=0, keepdims=True)
            weight = jnp.exp(now - top)
            total = jnp.sum(weight, axis=0, keepdims=True)
            probs = (weight * (1.0 / total)).astype(BF16)
            if at >= SLOTS:
                save(at - SLOTS).wait()
            p_scr[at % SLOTS] = probs
            save(at).start()
            mt_out.buf[cols, :] = dot(vt_scr[cols, :], probs).astype(BF16)
        mt_out.send()
        if not first:
            share = dot_tn(near_mt[number]()[...], near_wo()[...]) + dot_tn(mt_out.buf[...], wo[...])
            resid = x.astype(F32) + share + small()[0:1, :]
            unit, _ = norm_parts(resid)
            low = (unit * small()[1:2, :] + small()[2:3, :]).astype(BF16)
            resid_out.buf[rs, :] = resid
            low_out.buf[rs, :] = low
            lowt_out.buf[:, rs] = low.T
    for at in range(count * heads - SLOTS, count * heads):
        save(at).wait()


def attn_fwd(run, lengths, seqs, slots, x, own=None, far=None):
    rows, width = x.shape
    span = rows // seqs
    local = own[0].shape[1] if own else far[3].shape[0]
    heads = local // HD
    (_, extent_a), (_, extent_b) = groups_of(local)
    count = len(slots)
    tokens = pl.ds(slots[0] * span, count * span)
    x_in = Far(x, count, shape=(count * span, width), view=lambda ref, *_: ref.at[tokens, :])
    outs = []
    for _ in slots:
        outs += [
            FarOut((span, local), BF16),
            FarOut((local, span), BF16),
            FarOut((span, local), BF16),
            FarOut((local, span), BF16),
            Raw(shape=(extent_a // HD, span, span), dtype=BF16),
            Raw(shape=(extent_b // HD, span, span), dtype=BF16),
        ]
    if own:
        *weights, bias = own
        ins = [x_in, *map(Far, weights), bias]
        outs += [FarOut((width, span), BF16)] * count
        scalars = (lengths,)
    else:
        spot, pieces, near_mt, near_wo, small = far
        ins = [p if at in (3, 7) else Far(p) for at, p in enumerate(pieces)]
        ins += [x_in, *map(Far, near_mt), Far(near_wo), small]
        outs += [((rows, width), F32), ((rows, width), BF16), ((width, rows), BF16)]
        outs += [FarOut((width, local), BF16)] * 3 + [FarOut((local, width), BF16)]
        outs.append(((16, local), F32))
        scalars = (lengths, spot)
    results = run(
        functools.partial(attn_fwd_body, slots, span, heads, bool(own)),
        "attn_fwd",
        ins,
        outs,
        scratch=[
            pltpu.VMEM((span, local), BF16),
            pltpu.VMEM((local, span), BF16),
            pltpu.VMEM((SLOTS, span, span), BF16),
            pltpu.SemaphoreType.DMA((SLOTS,)),
        ],
        limit=14 if own else 24,
        scalars=scalars,
        cost=8 if own else 6,
    )
    saved = [results[6 * number : 6 * number + 6] for number in range(count)]
    return (saved, *results[6 * count :])


def norm_parts(resid):
    center = resid - jnp.mean(resid, -1, keepdims=True)
    spread = jnp.mean(center * center, -1, keepdims=True)
    rstd = lax.rsqrt(spread + EPSILON)
    return center * rstd, rstd


def norm_back(unit, rstd, gain, grad):
    scaled = grad * gain
    return rstd * (
        scaled
        - jnp.mean(scaled, -1, keepdims=True)
        - unit * jnp.mean(scaled * unit, -1, keepdims=True)
    )


def ln2_body(seqs, scalars, loads, stores):
    res1, ffn, og, small, pg = loads
    out_st, pool, dres, dlow, dlowt, sums_st = stores
    len_ref = scalars[0]
    small = small()
    rows = res1.buf.shape[0]
    span = rows // seqs
    tile = span // 4
    sums = [0.0, 0.0, 0.0]
    gain = small[4:5, :]
    for seq in range(seqs):
        length = len_ref[seq]
        count = length.astype(F32)
        total = 0.0
        spread = pg()[seq : seq + 1, :] / count
        for part in range(4):
            at = 4 * seq + part
            rs = slice(at * tile, (at + 1) * tile)
            unit_one, _ = norm_parts(res1(at)[rs, :])
            hidden = unit_one * small[1:2, :] + small[2:3, :]
            resid = hidden + ffn()[rs, :] + small[3:4, :]
            unit, rstd = norm_parts(resid)
            out = unit * gain + small[5:6, :]
            out_st.buf[rs, :] = out.astype(BF16)
            out_st.send(at)
            valid = lax.broadcasted_iota(jnp.int32, resid.shape, 0) + part * tile < length
            total = total + jnp.sum(jnp.where(valid, out, 0.0), 0, keepdims=True)
            d_out = og(at)[rs, :].astype(F32) + jnp.where(valid, spread, 0.0)
            d_resid = norm_back(unit, rstd, gain, d_out)
            dres.buf[rs, :] = d_resid
            dres.send(at)
            low = d_resid.astype(BF16)
            dlow.buf[rs, :] = low
            dlowt.buf[:, rs] = low.T
            for row, term in enumerate((d_resid, d_out * unit, d_out)):
                sums[row] = sums[row] + jnp.sum(term, 0, keepdims=True)
        pool.buf[seq : seq + 1, :] = total / count
    sums_st.buf[...] = jnp.zeros_like(sums_st.buf)
    for row in range(3):
        sums_st.buf[row : row + 1, :] = sums[row]


def ln2(run, lengths, res1, ffn, small, out_grad, pool_grad):
    rows, width = res1.shape
    seqs = lengths.shape[0]
    return run(
        functools.partial(ln2_body, seqs),
        "ln2",
        [res1, ffn, out_grad, small, pool_grad],
        [
            FarOut((rows, width), BF16, 4 * seqs),
            ((seqs, width), F32),
            FarOut((rows, width), F32, 4 * seqs),
            ((rows, width), BF16),
            ((width, rows), BF16),
            ((8, width), F32),
        ],
        scalars=(lengths,),
        limit=12,
        cost=6,
    )


def gelu_pair(pre):
    bell = jnp.exp(pre * pre * -0.5)
    t = 1.0 / (1.0 + (0.3275911 * SQRT_HALF) * jnp.abs(pre))
    poly = 0.5 * 1.061405429
    poly = poly * t + 0.5 * -1.453152027
    poly = poly * t + 0.5 * 1.421413741
    poly = poly * t + 0.5 * -0.284496736
    poly = poly * t + 0.5 * 0.254829592
    tail = poly * t * bell
    phi = jnp.where(pre >= 0.0, 1.0 - tail, tail)
    return pre * phi, phi + pre * bell * INV_SQRT_2PI


ROW_TILE = 256


def ffn_fwd_body(own, scalars, loads, stores, bias_scr):
    spot_ref = scalars[0]
    h, bias, *loads = loads
    h, bias = h(), bias()
    acts, ders, (acc_out, *kept) = stores[:2], stores[2:4], stores[4:]
    acc = acc_out.buf
    units = bias.shape[1]
    rows, width = h.shape
    tiles = [slice(at, at + ROW_TILE) for at in range(0, rows, ROW_TILE)]
    for step in range(2):
        if own:
            half = pl.ds(pl.multiple_of((spot_ref[0] ^ step) * 2 * units, 2 * units), 2 * units)
            wu, wd = loads[0]().at[:, half], loads[1]().at[half, :]
        else:
            pieces, part = loads[:8], loads[8]
            wu, wd = kept[step].buf, kept[2 + step].buf
            for flip in range(2):
                at = pl.ds(pl.multiple_of((spot_ref[1] ^ flip) * units, units), units)
                wu[:, at] = pieces[4 * step + flip]()[...]
                at = pl.ds(pl.multiple_of((spot_ref[2] ^ flip) * units, units), units)
                wd[at, :] = pieces[4 * step + 2 + flip]()[...]
        spot = spot_ref[0] ^ step
        bias_scr[:, :units] = bias[pl.ds(2 + 2 * spot, 1), :]
        bias_scr[:, units:] = bias[pl.ds(3 + 2 * spot, 1), :]

        def down(at, act):
            share = dot(act, wd[...])
            if step == 0 and own:
                acc[tiles[at], :] = share
            elif step == 0:
                acc[tiles[at], :] = part()[tiles[at], :] + share
            else:
                acc[tiles[at], :] += share

        pre = dot(h[tiles[0], :], wu[...]) + bias_scr[...]
        before = None
        for at, rs in enumerate(tiles):
            now = pre
            if at + 1 < len(tiles):
                pre = dot(h[tiles[at + 1], :], wu[...]) + bias_scr[...]
            act, der = gelu_pair(now)
            act = act.astype(BF16)
            acts[step].buf[rs, :] = act
            ders[step].buf[rs, :] = der.astype(BF16)
            if before is not None:
                down(at - 1, before)
            before = act
        down(len(tiles) - 1, before)
        ders[step].send()


def half_view(axis, units, which):
    def view(ref, spot_ref):
        at = pl.ds(pl.multiple_of((spot_ref[0] ^ which) * units, units), units)
        return ref.at[:, at] if axis else ref.at[at, :]

    return view


def ffn_fwd(run, spot, h, bias, wu=None, wd=None, pieces=(), part=None):
    rows, width = h.shape
    own = wu is not None
    units = 2 * bias.shape[1]
    ins = [h, bias]
    if own:
        ins += [wu, wd]
    else:
        ins += [p if at in (5, 7) else Far(p) for at, p in enumerate(pieces)] + [part]
    block = ((rows, units), BF16)
    away = FarOut((rows, units), BF16)
    outs = [block, block, block if own else away, block, ((rows, width), F32)]
    if not own:
        outs += [((width, units), BF16)] * 2 + [((units, width), BF16)] * 2
    results = run(
        functools.partial(ffn_fwd_body, own),
        "ffn_fwd",
        ins,
        outs,
        scratch=[pltpu.VMEM((1, units), F32)],
        scalars=(spot,),
        limit=14,
        cost=10,
    )
    return (results[0:2], results[2:4], *results[4:])


def split_out(x_bit, row_half, value, away, mine):
    @pl.when(x_bit == row_half)
    def _():
        mine[...] = value

    @pl.when(x_bit != row_half)
    def _():
        away[...] = value


def down_send_body(scalars, loads, stores):
    dft, far, own = [load() for load in loads]
    for at, act in enumerate((far, own)):
        stores[0].buf[at] = dot(dft[...], act[...]).astype(BF16)


def down_send(run, dft, far_act, own_act):
    width, rows = dft.shape
    units = far_act[0].shape[1]
    return run(
        down_send_body,
        "down_send",
        [dft, far_act[1], own_act[1]],
        [((2, width, units), BF16)],
        cost=3,
    )


def down_keep_body(scalars, loads, stores):
    dft, far, own, got = loads
    far_left, away, far_right, own_left_away, own_left, own_right = [store.buf for store in stores]
    x_bit = scalars[0][1]
    rows, half = far_right.shape
    for which, act in enumerate((far, own)):
        for part in range(2):
            rs = slice(part * rows, (part + 1) * rows)
            total = dot(dft()[rs, :], act()[...]) + got(which)[which, rs, :].astype(F32)
            low = total.astype(BF16)
            left, right = low[:, :half], low[:, half:]
            if which == 0:
                far_left[rs, :] = left
                split_out(x_bit, part, right, away.at[0], far_right)
            else:
                split_out(x_bit, part, left, own_left_away, own_left)
                split_out(x_bit, part, right, away.at[1], own_right)


def down_keep(run, spot, dft, far_act, own_act, got):
    width, rows = dft.shape
    units = far_act[0].shape[1]
    half = units // 2
    small = ((width // 2, half), BF16)
    return run(
        down_keep_body,
        "down_keep",
        [dft, far_act[0], own_act[0], got],
        [((width, half), BF16), ((2, width // 2, half), BF16), small, small, small, small],
        scalars=(spot,),
        limit=8,
        cost=5,
    )


def ffn_bwd_body(mode, wd_view, scalars, loads, stores):
    wd, der, df, ht, *got = loads
    wd = wd() if wd_view is None else wd_view(wd(), scalars[0])
    dpre, sums, *outs = [store.buf for store in stores]
    dpre_out = stores[0]
    rows = df.buf.shape[0]
    width = ht.buf.shape[0]
    tile = rows // 4
    bias = jnp.zeros((1, dpre.shape[1]), F32)
    tiles = [slice(at * tile, (at + 1) * tile) for at in range(4)]
    d_act = dot_nt(df()[tiles[0], :], wd[...])
    for at, rs in enumerate(tiles):
        now = d_act
        if at + 1 < len(tiles):
            d_act = dot_nt(df()[tiles[at + 1], :], wd[...])
        d_pre = (der()[rs, :].astype(F32) * now).astype(BF16)
        dpre[rs, :] = d_pre
        bias = bias + jnp.sum(d_pre.astype(F32), 0, keepdims=True)
    dpre_out.send()
    sums[...] = jnp.broadcast_to(bias, sums.shape)
    half = width // 2
    x_bit = scalars[0][1]
    for part in range(2):
        rs = slice(part * half, (part + 1) * half)
        total = dot(ht()[rs, :], dpre[...])
        if mode == "send":
            outs[0][rs, :] = total.astype(BF16)
            continue
        low = (total + got[0]()[rs, :].astype(F32)).astype(BF16)
        left, right = low[:, :half], low[:, half:]
        if mode == "far":
            outs[0][rs, :] = left
            split_out(x_bit, part, right, outs[1], outs[2])
        else:
            split_out(x_bit, part, left, outs[0], outs[1])
            split_out(x_bit, part, right, outs[2].at[1], outs[3])
    if mode == "own":
        outs[2][0] = got[1]()[...]


def ffn_bwd(run, mode, spot, df, ht, der, which, wd, wd_view, got=()):
    rows, width = df.shape
    units = der[which].shape[1]
    der_in = Far(der[which]) if not wd_view and which == 0 else der[which]
    ins = [Far(wd) if mode == "far" else wd, der_in, df, Far(ht) if mode == "far" else ht]
    outs = [FarOut((rows, units), BF16) if mode == "send" else ((rows, units), BF16), ((8, units), F32)]
    small = ((width // 2, units // 2), BF16)
    if mode == "send":
        outs += [((width, units), BF16)]
    elif mode == "far":
        outs += [((width, units // 2), BF16), small, small]
    else:
        outs += [small, small, ((2, width // 2, units // 2), BF16), small]
    ins += got
    return run(
        functools.partial(ffn_bwd_body, mode, wd_view),
        "ffn_bwd",
        ins,
        outs,
        scalars=(spot,),
        limit=10,
        cost=5,
    )


def hidden_back_body(scalars, loads, stores, acc_scr):
    (*pairs, resid_in, dres2_in, small) = loads
    dres, dlow, sums_out = stores
    sums = sums_out.buf
    small = small()
    rows = acc_scr.shape[0]
    tile = rows // 4
    tiles = [slice(at * tile, (at + 1) * tile) for at in range(4)]
    for pair in range(3):
        d_pre, weight = pairs[2 * pair](), pairs[2 * pair + 1]()
        for rs in tiles:
            share = dot_nt(d_pre[rs, :], weight[...])
            acc_scr[rs, :] = share if pair == 0 else acc_scr[rs, :] + share
    d_pre, weight = pairs[6](), pairs[7]()
    for at, rs in enumerate(tiles):
        d_hidden = acc_scr[rs, :] + dot_nt(d_pre[rs, :], weight[...]) + dres2_in(at)[rs, :]
        unit, rstd = norm_parts(resid_in(at)[rs, :])
        d_resid = norm_back(unit, rstd, small[1:2, :], d_hidden)
        dres.buf[rs, :] = d_resid
        dres.send(at)
        dlow.buf[rs, :] = d_resid.astype(BF16)
        for row, term in enumerate((d_resid, d_hidden * unit, d_hidden)):
            total = jnp.sum(term, 0, keepdims=True)
            if at == 0:
                sums[row : row + 1, :] = total
            else:
                sums[row : row + 1, :] += total


def hidden_back(run, spot, d_pres, wu, wu_far, resid, d_res2, small):
    rows, width = resid.shape
    units = wu.shape[1] // 2
    keep, send, far_keep, far_send = d_pres
    near = [Far(wu, shape=(width, units), view=half_view(1, units, which)) for which in range(2)]
    ins = [far_keep, wu_far[0], keep, near[0], Far(far_send), wu_far[1], Far(send), near[1]]
    return run(
        hidden_back_body,
        "hidden_back",
        ins + [resid, Far(d_res2, 4), small],
        [FarOut((rows, width), F32, 4), ((rows, width), BF16), ((8, width), F32)],
        scalars=(spot,),
        scratch=[pltpu.VMEM((rows, width), F32)],
        limit=22,
        cost=8,
    )


def attn_bwd_body(slots, begin, extent, last, scalars, loads, stores, *scratch):
    wo, da, *loads = [load() for load in loads]
    scale = HD**-0.5
    heads = extent // HD
    width = da.shape[1]
    count = len(slots)
    outs = stores[:count]
    span = loads[0].shape[0]
    mixed = []
    for slot in slots:
        d_attn = da[slot * span : (slot + 1) * span, :]
        mixed.append(dot_nt(d_attn, wo[begin : begin + extent, :]).astype(BF16))
    for number in range(count):
        q, kt, v, probs_ref = loads[4 * number : 4 * number + 4]
        out = outs[number].buf
        d_query = []
        for head in range(heads):
            cols = slice(begin + head * HD, begin + (head + 1) * HD)
            d_mixed_h = mixed[number][:, head * HD : (head + 1) * HD]
            d_probs = dot_nt(v[:, cols], d_mixed_h)
            low_probs = probs_ref[head]
            probs = low_probs.astype(F32)
            inner = jnp.sum(d_probs * probs, axis=0, keepdims=True)
            d_scores = (probs * (d_probs - inner)).astype(BF16)
            at = extent + head * HD
            out[:, at : at + HD] = dot(d_scores, q[:, cols]).astype(BF16)
            at = 2 * extent + head * HD
            out[:, at : at + HD] = dot(low_probs, d_mixed_h).astype(BF16)
            d_query.append((dot(kt[cols, :], d_scores) * scale).astype(BF16))
        out[:, :extent] = jnp.concatenate(d_query, 0).T
        outs[number].send()
    if not last:
        return
    before = loads[4 * count :]
    seqs = da.shape[0] // span
    mts, xts, before = before[:seqs], before[seqs : 2 * seqs], before[2 * seqs :]
    grads = [*before, *[store.buf for store in outs]]
    keep, send, sums = [store.buf for store in stores[count:]]
    (fold_scr,) = scratch
    core = scalars[0][0]
    g_out = None
    for slot, mt in enumerate(mts):
        share = dot(mt[begin : begin + extent, :], da[slot * span : (slot + 1) * span, :])
        g_out = share if g_out is None else g_out + share
    g_out = g_out.astype(BF16)
    for part in range(width // extent):
        fold_scr[part * extent : (part + 1) * extent, :] = g_out[:, part * extent : (part + 1) * extent]
    half = width // 2
    for part in range(2):
        rs = slice(part * half, (part + 1) * half)
        total = None
        for xt, grad in zip(xts, grads):
            share = dot(xt[rs, :], grad[...])
            total = share if total is None else total + share
        low = total.astype(BF16)

        def put(ref, low=low, rs=rs):
            ref[:, : 3 * extent] = low
            ref[:, 3 * extent :] = fold_scr[rs, :]

        @pl.when(core == part)
        def _(put=put):
            put(keep)

        @pl.when(core != part)
        def _(put=put):
            put(send)

    total = 0.0
    for grad in grads:
        total = total + jnp.sum(grad[...].astype(F32), 0, keepdims=True)
    sums[...] = jnp.broadcast_to(total, sums.shape)


def attn_bwd(run, group, spot, slots, d_attn, wo, xts, saved, before=()):
    rows, width = d_attn.shape
    begin, extent = group
    span = rows // len(xts)
    last = slots[-1] == len(xts) - 1
    ins = [wo, d_attn]
    for slot in slots:
        q, kt, v, _, probs_a, probs_b = saved[slot]
        ins += [q, kt, v, probs_a if begin == 0 else probs_b]
    outs = [FarOut((span, 3 * extent), BF16)] * len(slots)
    if last:
        ins += [saved[slot][3] for slot in range(len(xts))] + list(xts) + list(map(Far, before))
        outs += [
            ((width // 2, 4 * extent), BF16),
            ((width // 2, 4 * extent), BF16),
            ((8, 3 * extent), F32),
        ]
    return run(
        functools.partial(attn_bwd_body, slots, begin, extent, last),
        "attn_bwd",
        ins,
        outs,
        scalars=(spot,),
        scratch=[pltpu.VMEM((width, extent), BF16)] if last else [],
        limit=10,
        cost=6,
    )


def tokens_back_body(groups, seqs, scalars, loads, stores):
    wq, wk, wv, *grads, before = loads
    (out,) = stores
    span = out.buf.shape[0] // seqs
    for number, (begin, extent) in enumerate(groups):
        last = number == len(groups) - 1
        for slot in range(seqs):
            rs = slice(slot * span, (slot + 1) * span)
            grad = grads[number * seqs + slot]()
            total = None
            for mat, weight in enumerate((wq, wk, wv)):
                share = dot_nt(
                    grad[:, mat * extent : (mat + 1) * extent], weight()[:, begin : begin + extent]
                )
                total = share if total is None else total + share
            total = total + (out.buf[rs, :] if number else before(slot)[rs, :])
            out.buf[rs, :] = total
            if last:
                out.send(slot)


def tokens_back(run, groups, seqs, before, weights, grads):
    rows, width = before.shape
    return run(
        functools.partial(tokens_back_body, groups, seqs),
        "tokens_back",
        [Far(a) for a in (*weights, *grads)] + [Far(before, seqs)],
        [FarOut((rows, width), F32, seqs)],
        limit=16,
        cost=3,
    )


def collect_body(scalars, loads, stores):
    keep, send, one, two, a_sums, b_sums = [load() for load in loads]
    out = stores[0].buf
    core = scalars[0][0]
    out[...] = jnp.zeros_like(out)
    out[pl.ds(core, 1), :] = keep[0:1, :]
    out[pl.ds(1 - core, 1), :] = send[0:1, :]
    extent_a, extent_b = a_sums.shape[1] // 3, b_sums.shape[1] // 3
    local = extent_a + extent_b
    for at, mat in enumerate((0, 2)):
        begin = at * local
        out[2:3, begin : begin + extent_a] = a_sums[0:1, mat * extent_a : (mat + 1) * extent_a]
        out[2:3, begin + extent_a : begin + local] = b_sums[0:1, mat * extent_b : (mat + 1) * extent_b]
    out[3:6, :] = one[0:3, :]
    out[6:9, :] = two[0:3, :]


def collect(run, spot, *sums):
    return run(collect_body, "collect", list(sums), [((16, sums[2].shape[1]), F32)], scalars=(spot,))


def finish_attn_body(begin, n_prev, scalars, loads, stores, full_scr, fold_scr, go_scr, sems):
    core = scalars[0][0]
    mine, other = [load() for load in loads[:2]]
    rows = mine.shape[0]
    extent, width = go_scr.shape
    copies = []

    def ship(src, dst):
        copies.append(pltpu.make_async_copy(src, dst, sems.at[len(copies)]))
        copies[-1].start()

    for flip, ref in enumerate((mine, other)):
        at = pl.ds(pl.multiple_of((core ^ flip) * rows, rows), rows)
        fold_scr[at, :] = ref[:, 3 * extent :]
        for mat in range(3):
            full_scr[mat, at, :] = ref[:, mat * extent : (mat + 1) * extent].astype(F32)
    for mat in range(3):
        ship(full_scr.at[mat], stores[mat].at[:, begin : begin + extent])
    for part in range(width // extent):
        cols = slice(part * extent, (part + 1) * extent)
        go_scr[:, cols] = fold_scr[cols, :].astype(F32)
    ship(go_scr, stores[3].at[begin : begin + extent, :])
    for copy in copies:
        copy.wait()


def finish_attn(run, group, local, spot, mine, other, previous=()):
    begin, extent = group
    width = 2 * mine.shape[0]
    return run(
        functools.partial(finish_attn_body, begin, len(previous)),
        "finish_attn",
        [mine, other] + [Raw(p) for p in previous],
        [Raw(shape=(width, local), dtype=F32)] * 3 + [Raw(shape=(local, width), dtype=F32)],
        scratch=[
            pltpu.VMEM((3, width, extent), F32),
            pltpu.VMEM((width, extent), BF16),
            pltpu.VMEM((extent, width), F32),
            pltpu.SemaphoreType.DMA((4,)),
        ],
        scalars=(spot,),
        aliases={2 + i: i for i in range(len(previous))},
        limit=8,
        cost=0.2,
    )


def finish_body(kind, scalars, loads, stores, scr, sems):
    mine, other = [load() for load in loads]
    (out,) = stores
    width, units = mine.shape
    parts = 2
    extent = units // parts
    copies = []
    for flip, ref in enumerate((mine, other)):
        for part in range(parts):
            at = flip * parts + part
            begin = pl.multiple_of((scalars[0][0] ^ flip) * units + part * extent, extent)
            value = ref[:, part * extent : (part + 1) * extent].astype(F32)
            scr[at] = value if kind == "up" else value.T
            place = pl.ds(begin, extent)
            dst = out.at[:, place] if kind == "up" else out.at[place, :]
            copies.append(pltpu.make_async_copy(scr.at[at], dst, sems.at[at]))
            copies[-1].start()
    for copy in copies:
        copy.wait()


def finish(run, kind, spot, mine, other):
    width, units = mine.shape
    shape = (width, 2 * units) if kind == "up" else (2 * units, width)
    piece = (width, units // 2) if kind == "up" else (units // 2, width)
    return run(
        functools.partial(finish_body, kind),
        "finish_" + kind,
        [mine, other],
        [Raw(shape=shape, dtype=F32)],
        scratch=[pltpu.VMEM((4, *piece), F32), pltpu.SemaphoreType.DMA((4,))],
        scalars=(spot,),
        limit=8,
        cost=0.2,
    )


def add(*terms):
    total = terms[0].astype(F32)
    for term in terms[1:]:
        total = total + term.astype(F32)
    return total.astype(BF16)


def local(
    n_batch,
    tokens,
    lengths,
    w_query,
    b_query,
    w_key,
    w_value,
    b_value,
    w_out,
    b_out,
    gain_one,
    shift_one,
    w_up,
    b_up,
    w_down,
    b_down,
    gain_two,
    shift_two,
    out_grad,
    pool_grad,
):
    rows, width = tokens.shape
    seqs = lengths.shape[0]
    half = w_query.shape[1]
    groups = groups_of(half)
    place = lax.axis_index("batch").astype(jnp.int32)
    core, x_bit, z_low, z_high = [(place >> bit) & 1 for bit in range(4)]
    spot = jnp.stack([core, x_bit, z_low])
    run = Kernels()

    def swap(array, bit):
        return lax.ppermute(array, "batch", [(i, i ^ bit) for i in range(n_batch)])

    def swap_core(array):
        return swap(array, 1)

    def swap_x(array):
        return swap(array, 2)

    def swap_y(array):
        return lax.ppermute(array, "tensor", [(0, 1), (1, 0)])

    bias_rows = jnp.concatenate([b_query, b_value, b_up]).reshape(-1, half)
    bias_rows = jnp.pad(bias_rows, ((0, 16 - bias_rows.shape[0]), (0, 0)))
    own_bias = bias_rows.astype(F32)
    small = jnp.stack([b_out, gain_one, shift_one, b_down, gain_two, shift_two]).astype(F32)
    ex, ez = pack(run, spot, w_query, w_key, w_value, w_out, bias_rows)
    ex, ez = swap_y(ex), swap_y(ez)
    fx, fz = pack_units(run, spot, w_up, w_down, half)
    fx, fz = swap_y(fx), swap_y(fz)
    own_saved, xts = [], []
    own = (w_query, w_key, w_value, own_bias)
    for slot in range(seqs):
        saved, xt = attn_fwd(run, lengths, seqs, (slot,), tokens, own=own)
        own_saved += saved
        xts.append(xt)
        if slot == 0:
            ex, ez = run.wait(ex, ez)
            ex_x, ez_z = swap_x(ex), swap(ez, 4)
            ex_c, ez_c = swap_core(ex), swap_core(ez)
    ex_x, ez_z, ex_c, ez_c, fx = run.wait(ex_x, ez_z, ex_c, ez_c, fx)
    ex_xc, ez_zc = swap_core(ex_x), swap_core(ez_z)
    fx_x, fx_c = swap_x(fx), swap_core(fx)
    pieces = (ex, ex_x, ex_c, ex_xc, ez, ez_z, ez_c, ez_zc)
    near_mt = [saved[3] for saved in own_saved]
    far_saved, resid_one, hidden, hidden_t, far_q, far_k, far_v, far_o, far_bias = attn_fwd(
        run, lengths, seqs, tuple(range(seqs)), tokens, far=(spot, pieces, near_mt, w_out, small)
    )
    fz, fx_x, fx_c = run.wait(fz, fx_x, fx_c)
    fz_z, fz_c = swap(fz, 4), swap_core(fz)
    fx_xc = swap_core(fx_x)
    own_act, own_der, ffn_part = ffn_fwd(run, spot, hidden, own_bias, wu=w_up, wd=w_down)
    fx_xc, fz_z, fz_c = run.wait(fx_xc, fz_z, fz_c)
    fz_zc = swap_core(fz_z)
    far_act, far_der, ffn_sum, *far_weights = ffn_fwd(
        run,
        spot,
        hidden,
        far_bias,
        pieces=(fx, fx_x, fz, fz_z, fx_c, fx_xc, fz_c, fz_zc),
        part=ffn_part,
    )
    wu_far, wd_far = far_weights[:2], far_weights[2:]
    output, pooled, d_resid_two, d_ffn, d_ffn_t, sums_two = ln2(
        run, lengths, resid_one, ffn_sum, small, out_grad, pool_grad
    )

    def pick(array, at):
        return lax.dynamic_index_in_dim(array, at, 0, keepdims=False)

    def halves(array):
        return array.reshape(2, array.shape[0] // 2, array.shape[1])

    def split(bit, *terms):
        parts = [halves(t) for t in terms]
        return add(*[pick(t, 1 - bit) for t in parts]), add(*[pick(t, bit) for t in parts])

    def join(bit, mine, got):
        return jnp.concatenate(
            [jnp.where(bit == 0, mine, got), jnp.where(bit == 0, got, mine)], axis=0
        )

    def rest(array):
        bit = 16
        while bit < n_batch:
            array = add(array, swap(array, bit))
            bit *= 2
        return array

    def cross_two(left_got, right_got, away, far):
        return swap_x(add(away, pick(halves(left_got), 1 - x_bit))), swap_y(add(far, right_got))

    def cross_three(left, left_got, left_x, right, right_x, right_y):
        mine = pick(halves(left_got), x_bit)
        return jnp.concatenate([add(left, mine, left_x), add(right, right_x, right_y)], axis=1)

    d_got = swap_core(run.wait(down_send(run, d_ffn_t, far_act, own_act)))
    bwd = functools.partial(ffn_bwd, run)
    dp_fs, bs_fs, u_send = bwd("send", spot, d_ffn, hidden_t, far_der, 1, wd_far[1], None)
    d_got, u_send = run.wait(d_got, u_send)
    uf_got = swap_core(u_send)
    df_left, d_away, df_right, do_left_away, do_left, do_right = down_keep(
        run, spot, d_ffn_t, far_act, own_act, d_got
    )
    df_left, d_away = run.wait(df_left, d_away)
    d_left_y, d_right_x = swap_y(df_left), swap_x(d_away)
    dp_os, bs_os, u_send = bwd("send", spot, d_ffn, hidden_t, own_der, 1, w_down, half_view(0, width, 1))
    uf_got, u_send = run.wait(uf_got, u_send)
    uo_got = swap_core(u_send)
    dp_fk, bs_fk, uf_left, uf_away, uf_right = bwd(
        "far", spot, d_ffn, hidden_t, far_der, 0, wd_far[0], None, (uf_got,)
    )
    uo_got, uf_left = run.wait(uo_got, uf_left)
    u_left_y = swap_y(uf_left)
    dp_ok, bs_ok, uo_left_away, uo_left, u_away, uo_right = bwd(
        "own", spot, d_ffn, hidden_t, own_der, 0, w_down, half_view(0, width, 0), (uo_got, uf_away)
    )
    d_left_y, d_right_x, u_away = run.wait(d_left_y, d_right_x, u_away)
    d_left_x, d_right_y = cross_two(d_left_y, d_right_x[0], do_left_away, df_right)
    u_right_x = swap_x(u_away)
    d_resid_one, d_attn, sums_one = hidden_back(
        run, spot, (dp_ok, dp_os, dp_fk, dp_fs), w_up, wu_far, resid_one, d_resid_two, small
    )

    first, others = (0,), tuple(range(1, seqs))
    far_bwd = functools.partial(
        attn_bwd, run, spot=spot, d_attn=d_attn, wo=far_o, xts=xts, saved=far_saved
    )
    own_bwd = functools.partial(
        attn_bwd, run, spot=spot, d_attn=d_attn, wo=w_out, xts=xts, saved=own_saved
    )
    d_left_x, d_right_y = run.wait(d_left_x, d_right_y)
    d_rows = cross_three(do_left, d_left_y, d_left_x, do_right, d_right_x[1], d_right_y)
    d_away, d_mine = split(z_low, d_rows)
    d_got = swap(d_away, 4)
    fa_0 = far_bwd(groups[0], slots=first)
    d_got = run.wait(d_got)
    d_away, d_mine = split(z_high, d_mine, d_got)
    d_got = swap(d_away, 8)
    *fa_1, fa_keep, fa_send, fa_sums = far_bwd(groups[0], slots=others, before=(fa_0,))
    d_got, u_left_y, u_right_x, fa_send = run.wait(d_got, u_left_y, u_right_x, fa_send)
    u_left_x, u_right_y = cross_two(u_left_y, u_right_x[0], uo_left_away, uf_right)
    fa_got = swap_core(fa_send)
    d_mine = rest(add(d_mine, d_got))
    d_got = swap(d_mine, 8)
    *fb, fb_keep, fb_send, fb_sums = far_bwd(groups[1], slots=first + others)
    fa_got, u_left_x, u_right_y, fb_send = run.wait(fa_got, u_left_x, u_right_y, fb_send)
    fa_y = swap_y(add(fa_keep, fa_got))
    u_rows = cross_three(uo_left, u_left_y, u_left_x, uo_right, u_right_x[1], u_right_y)
    u_away, u_mine = split(z_low, u_rows)
    u_got = swap(u_away, 4)
    fb_got = swap_core(fb_send)
    oa_0 = own_bwd(groups[0], slots=first)

    u_got, fb_got, d_got = run.wait(u_got, fb_got, d_got)
    u_away, u_mine = split(z_high, u_mine, u_got)
    u_got = swap(u_away, 8)
    d_mine = join(z_high, d_mine, d_got)
    d_got = swap(d_mine, 4)
    fb_y = swap_y(add(fb_keep, fb_got))
    sums_got = swap_y(collect(run, spot, bs_fk, bs_fs, sums_one, sums_two, fa_sums, fb_sums))
    *oa_1, oa_keep, oa_send, oa_sums = own_bwd(groups[0], slots=others, before=(oa_0,))
    u_got, d_got, fa_y, oa_send = run.wait(u_got, d_got, fa_y, oa_send)
    oa_got = swap_core(oa_send)
    u_mine = rest(add(u_mine, u_got))
    u_got = swap(u_mine, 8)
    d_mine = join(z_low, d_mine, d_got)
    d_got = swap_x(d_mine)
    *ob, ob_keep, ob_send, ob_sums = own_bwd(groups[1], slots=first + others)

    oa_got, u_got, fb_y, ob_send, sums_got = run.wait(oa_got, u_got, fb_y, ob_send, sums_got)
    ob_got = swap_core(ob_send)
    a_away, a_mine = split(x_bit, oa_keep, oa_got, fa_y)
    a_got = swap_x(a_away)
    u_mine = join(z_high, u_mine, u_got)
    u_got = swap(u_mine, 4)
    sums = collect(run, spot, bs_ok, bs_os, sums_one, sums_two, oa_sums, ob_sums) + sums_got
    ob_got = run.wait(ob_got)
    b_away, b_mine = split(z_low, ob_keep, ob_got, fb_y)
    b_got = swap(b_away, 4)
    sums_got = swap_x(sums)
    dx = tokens_back(run, groups, seqs, d_resid_one, (far_q, far_k, far_v), (fa_0, *fa_1, *fb))

    a_got, b_got, u_got, d_got, sums_got = run.wait(a_got, b_got, u_got, d_got, sums_got)
    a_away, a_mine = split(z_low, a_mine, a_got)
    a_got = swap(a_away, 4)
    b_away, b_mine = split(x_bit, b_mine, b_got)
    b_got = swap_x(b_away)
    d_mine = join(x_bit, d_mine, d_got)
    d_other = swap_core(d_mine)
    u_mine = join(z_low, u_mine, u_got)
    sums = sums + sums_got
    sums_got = swap(sums, 1)
    d_other = run.wait(d_other)
    g_down = finish(run, "down", spot, d_mine, d_other)

    a_got, b_got, sums_got, u_mine = run.wait(a_got, b_got, sums_got, u_mine)
    a_mine = add(a_mine, a_got)
    a_got = swap(a_mine, 8)
    b_mine = add(b_mine, b_got)
    b_got = swap(b_mine, 8)
    u_got = swap_x(u_mine)
    sums = sums + sums_got
    sums_got = swap(sums, 4)
    d_tokens = tokens_back(run, groups, seqs, dx, (w_query, w_key, w_value), (oa_0, *oa_1, *ob))

    a_got, b_got, u_got, sums_got = run.wait(a_got, b_got, u_got, sums_got)
    a_mine = rest(add(a_mine, a_got))
    a_got = swap(a_mine, 4)
    b_mine = rest(add(b_mine, b_got))
    b_got = swap_x(b_mine)
    u_mine = join(x_bit, u_mine, u_got)
    u_other = swap_core(u_mine)
    sums = sums + sums_got
    sums_got = swap(sums, 8)
    u_other = run.wait(u_other)
    g_up = finish(run, "up", spot, u_mine, u_other)

    a_got, b_got, sums_got = run.wait(a_got, b_got, sums_got)
    a_mine = join(z_low, a_mine, a_got)
    a_got = swap_x(a_mine)
    b_mine = join(x_bit, b_mine, b_got)
    b_got = swap(b_mine, 4)
    sums = sums + sums_got
    bit = 16
    while bit < n_batch:
        sums = sums + swap(sums, bit)
        bit *= 2
    a_got, b_got, sums = run.wait(a_got, b_got, sums)
    a_mine = join(x_bit, a_mine, a_got)
    a_other = swap_core(a_mine)
    b_mine = join(z_low, b_mine, b_got)
    b_other = swap_core(b_mine)
    b_other = run.wait(b_other)
    grads = finish_attn(run, groups[1], half, spot, b_mine, b_other)
    a_other = run.wait(a_other)
    g_query, g_key, g_value, g_out = finish_attn(run, groups[0], half, spot, a_mine, a_other, grads)

    g_bias_up = sums[0:2].reshape(-1)
    g_bias_query, g_bias_value = sums[2, :half], sums[2, half:]
    d_bias_out, d_gain_one, d_shift_one, d_bias_down, d_gain_two, d_shift_two = [sums[3 + i] for i in range(6)]
    return (
        output,
        pooled,
        d_tokens,
        g_query,
        g_bias_query,
        g_key,
        g_value,
        g_bias_value,
        g_out,
        d_bias_out,
        d_gain_one,
        d_shift_one,
        g_up,
        g_bias_up,
        g_down,
        d_bias_down,
        d_gain_two,
        d_shift_two,
    )


def solution(mesh):
    return jax.shard_map(
        functools.partial(local, mesh.shape["batch"]),
        mesh=mesh,
        in_specs=(
            P(("batch", "tensor"), None),
            P(("batch", "tensor")),
            P(None, "tensor"),
            P("tensor"),
            P(None, "tensor"),
            P(None, "tensor"),
            P("tensor"),
            P("tensor", None),
            P(),
            P(),
            P(),
            P(None, "tensor"),
            P("tensor"),
            P("tensor", None),
            P(),
            P(),
            P(),
            P(("batch", "tensor"), None),
            P(("batch", "tensor"), None),
        ),
        out_specs=(
            P(("batch", "tensor"), None),
            P(("batch", "tensor"), None),
            P(("batch", "tensor"), None),
            P(None, "tensor"),
            P("tensor"),
            P(None, "tensor"),
            P(None, "tensor"),
            P("tensor"),
            P("tensor", None),
            P(),
            P(),
            P(),
            P(None, "tensor"),
            P("tensor"),
            P("tensor", None),
            P(),
            P(),
            P(),
        ),
        check_vma=False,
    )
```

```python
import functools

import jax
import jax.numpy as jnp
from jax import lax
from jax.experimental import pallas as pl
from jax.experimental.pallas import tpu as pltpu
from jax.sharding import PartitionSpec as P

HD = 64
EPSILON = 1e-12
NEG_FILL = -1e30
F32 = jnp.float32
BF16 = jnp.bfloat16
MIB = 1024 * 1024
FLOPS_PER_US = 1.1e9
SQRT_HALF = 0.7071067811865476
INV_SQRT_2PI = 0.3989422804014327


def dot(left, right):
    return lax.dot_general(left, right, (((1,), (0,)), ((), ())), preferred_element_type=F32)


def dot_nt(left, right):
    return lax.dot_general(left, right, (((1,), (1,)), ((), ())), preferred_element_type=F32)


def dot_tn(left, right):
    return lax.dot_general(left, right, (((0,), (0,)), ((), ())), preferred_element_type=F32)


class Part:
    def __init__(self, buf):
        self.buf = buf

    def __call__(self, part=None):
        return self.buf

    def send(self, part=0):
        pass

    def finish(self):
        pass


def pieces_of(src, dst, parts, axis):
    if parts == 1:
        return [(src, dst)]
    extent = dst.shape[axis] // parts
    cuts = [(slice(None),) * axis + (pl.ds(part * extent, extent),) for part in range(parts)]
    return [(src.at[cut], dst.at[cut]) for cut in cuts]


class Load:
    def __init__(self, src, buf, sems, first, parts, axis):
        self.buf = buf
        self.copies = [
            pltpu.make_async_copy(*pair, sems.at[first + at])
            for at, pair in enumerate(pieces_of(src, buf, parts, axis))
        ]
        self.waited = [False] * parts
        for copy in self.copies:
            copy.start()

    def __call__(self, part=None):
        for at in range(len(self.copies)) if part is None else (part,):
            if not self.waited[at]:
                self.waited[at] = True
                self.copies[at].wait()
        return self.buf


class Store:
    def __init__(self, buf, dst, sems, first, parts, axis):
        self.buf = buf
        self.copies = [
            pltpu.make_async_copy(*pair, sems.at[first + at])
            for at, pair in enumerate(pieces_of(buf, dst, parts, axis))
        ]
        self.sent = [False] * parts

    def send(self, part=0):
        self.sent[part] = True
        self.copies[part].start()

    def finish(self):
        for at, copy in enumerate(self.copies):
            if not self.sent[at]:
                copy.start()
        for copy in self.copies:
            copy.wait()


class Far:
    def __init__(self, array, parts=1, axis=0, shape=None, view=None):
        self.array, self.parts, self.axis = array, parts, axis
        self.shape = shape or array.shape
        self.view = view or (lambda ref, *_: ref)


class FarOut:
    def __init__(self, shape, dtype, parts=1, axis=0):
        self.shape, self.dtype, self.parts, self.axis = shape, dtype, parts, axis


class Raw:
    def __init__(self, array=None, shape=None, dtype=None):
        self.array, self.shape, self.dtype = array, shape, dtype


class Kernels:
    def __init__(self):
        self.token = None

    def wait(self, *values):
        self.token, values = lax.optimization_barrier((self.token, values))
        return values if len(values) > 1 else values[0]

    def __call__(self, body, name, ins, outs, scalars=(), scratch=(), aliases=None, limit=6, cost=4):
        spec = lambda space: pl.BlockSpec(memory_space=space)
        in_far = [isinstance(i, Far) for i in ins]
        in_raw = [isinstance(i, Raw) for i in ins]
        out_far = [isinstance(o, FarOut) for o in outs]
        out_raw = [isinstance(o, Raw) for o in outs]
        in_spaces = [pltpu.HBM if f or r else pltpu.VMEM for f, r in zip(in_far, in_raw)]
        out_spaces = [pltpu.HBM if f or r else pltpu.VMEM for f, r in zip(out_far, out_raw)]
        arrays = [i.array if f or r else i for i, f, r in zip(ins, in_far, in_raw)]
        out_types = [(o.shape, o.dtype) if f or r else o for o, f, r in zip(outs, out_far, out_raw)]
        buffers = [pltpu.VMEM(i.shape, i.array.dtype) for i, f in zip(ins, in_far) if f]
        buffers += [pltpu.VMEM(o.shape, o.dtype) for o, f in zip(outs, out_far) if f]
        n_sem = sum(i.parts for i, f in zip(ins, in_far) if f)
        n_sem += sum(o.parts for o, f in zip(outs, out_far) if f)
        n_scalar, n_in, n_out, n_buf = len(scalars), len(ins), len(outs), len(buffers)
        first = self.token is None

        def kernel(*refs):
            scalar_refs, refs = refs[:n_scalar], refs[n_scalar:]
            in_refs, refs = refs[:n_in], refs[n_in + (not first) :]
            out_refs, token_ref, refs = refs[:n_out], refs[n_out], refs[n_out + 1 :]
            bufs, sems, rest = list(refs[:n_buf]), refs[n_buf], refs[n_buf + 1 :]
            at, loads, stores = 0, [], []
            for i, f, r, ref in zip(ins, in_far, in_raw, in_refs):
                if f:
                    src = i.view(ref, *scalar_refs)
                    loads.append(Load(src, bufs.pop(0), sems, at, i.parts, i.axis))
                    at += i.parts
                else:
                    loads.append(ref if r else Part(ref))
            for o, f, r, ref in zip(outs, out_far, out_raw, out_refs):
                if f:
                    stores.append(Store(bufs.pop(0), ref, sems, at, o.parts, o.axis))
                    at += o.parts
                else:
                    stores.append(ref if r else Part(ref))
            body(scalar_refs, loads, stores, *rest)
            token_ref[...] = jnp.zeros_like(token_ref)
            for load, f in zip(loads, in_far):
                if f:
                    load()
            for store, r in zip(stores, out_raw):
                if not r:
                    store.finish()

        *results, self.token = pl.pallas_call(
            kernel,
            name=name,
            in_specs=[spec(pltpu.SMEM)] * n_scalar
            + [spec(space) for space in in_spaces]
            + ([] if first else [spec(pl.ANY)]),
            out_specs=[spec(space) for space in out_spaces] + [spec(pltpu.VMEM)],
            scratch_shapes=buffers + [pltpu.SemaphoreType.DMA((max(n_sem, 1),))] + list(scratch),
            out_shape=[space(*kind) for kind, space in zip(out_types, out_spaces)]
            + [pltpu.VMEM((8, 128), F32)],
            input_output_aliases={k + n_scalar: v for k, v in (aliases or {}).items()},
            compiler_params=pltpu.CompilerParams(vmem_limit_bytes=limit * MIB),
            cost_estimate=pl.CostEstimate(
                flops=int(cost * FLOPS_PER_US), bytes_accessed=0, transcendentals=0
            ),
        )(
            *scalars,
            *[pltpu.with_memory_space_constraint(a, space) for a, space in zip(arrays, in_spaces)],
            *([] if first else [self.token]),
        )
        return results if len(results) > 1 else results[0]


def at_index(index):
    return lambda ref, *_: ref.at[index]


def groups_of(local):
    first = local * 2 // 3
    return ((0, first), (first, local - first))


def pack_body(scalars, loads, stores, sems):
    wq, wk, wv, wo, bias = loads
    ex, ez = [store.buf for store in stores]
    core, x_bit, z_bit = [scalars[0][at] for at in range(3)]
    width, local = wq.shape
    rows = width // 2
    outs = wo.shape[0] // 2
    mine = pl.ds(pl.multiple_of(core * rows, rows), rows)
    mine_out = pl.ds(pl.multiple_of(core * outs, outs), outs)
    query = pltpu.make_async_copy(wq.at[mine, :], ex, sems.at[0])

    @pl.when(x_bit == 0)
    def _():
        query.start()

    @pl.when(x_bit == 1)
    def _():
        pltpu.make_async_copy(wk.at[mine, :], ex, sems.at[0]).start()

    values = []
    for part in range(width // local):
        dst, sem = ez.at[part * outs : (part + 1) * outs, :], sems.at[1 + part]
        own = pl.ds(pl.multiple_of(core * rows + part * outs, outs), outs)
        values.append(pltpu.make_async_copy(wv.at[own, :], dst, sem))

        @pl.when(z_bit == 0)
        def _(copy=values[-1]):
            copy.start()

        @pl.when(z_bit == 1)
        def _(dst=dst, sem=sem, part=part):
            src = wo.at[mine_out, part * local : (part + 1) * local]
            pltpu.make_async_copy(src, dst, sem).start()

    ez[rows:, :] = bias()[...]
    query.wait()
    for copy in values:
        copy.wait()


def pack(run, spot, wq, wk, wv, wo, bias):
    width, local = wq.shape
    return run(
        pack_body,
        "pack",
        [Raw(wq), Raw(wk), Raw(wv), Raw(wo), bias],
        [((width // 2, local), BF16), ((width // 2 + bias.shape[0], local), BF16)],
        scalars=(spot,),
        scratch=[pltpu.SemaphoreType.DMA((1 + width // local,))],
        cost=2,
    )


def pack_units_body(scalars, loads, stores, sems):
    wu, wd = loads
    fx, fz = [store.buf for store in stores]
    core, x_bit, z_bit = [scalars[0][at] for at in range(3)]
    units = fx.shape[1]
    up = pl.ds(pl.multiple_of((2 * core + x_bit) * units, units), units)
    down = pl.ds(pl.multiple_of((2 * core + z_bit) * units, units), units)
    copies = [
        pltpu.make_async_copy(wu.at[:, up], fx, sems.at[0]),
        pltpu.make_async_copy(wd.at[down, :], fz, sems.at[1]),
    ]
    for copy in copies:
        copy.start()
    for copy in copies:
        copy.wait()


def pack_units(run, spot, wu, wd, units):
    width = wu.shape[0]
    return run(
        pack_units_body,
        "pack_units",
        [Raw(wu), Raw(wd)],
        [((width, units), BF16), ((units, width), BF16)],
        scalars=(spot,),
        scratch=[pltpu.SemaphoreType.DMA((2,))],
        cost=2,
    )


def assemble(spot_ref, pieces, wq, wk, wv, wo, bias):
    core, x_bit, z_bit = spot_ref[0], spot_ref[1], spot_ref[2]
    local, width = wo.shape
    rows = width // 2
    outs = local // 2
    for c_flip in range(2):
        spot = core ^ c_flip
        at = pl.ds(pl.multiple_of(spot * rows, rows), rows)
        out_at = pl.ds(pl.multiple_of(spot * outs, outs), outs)
        for flip in range(2):
            piece = pieces[2 * c_flip + flip]()
            for mat, ref in enumerate((wq, wk)):

                @pl.when((x_bit ^ flip) == mat)
                def _(piece=piece, at=at, ref=ref):
                    ref[at, :] = piece[...]

            piece = pieces[4 + 2 * c_flip + flip]()

            @pl.when((z_bit ^ flip) == 0)
            def _(piece=piece, at=at):
                wv[at, :] = piece[0:rows, :]

            @pl.when((z_bit ^ flip) == 1)
            def _(piece=piece, out_at=out_at):
                for part in range(width // local):
                    cols = slice(part * local, (part + 1) * local)
                    wo[out_at, cols] = piece[part * outs : (part + 1) * outs, :]

    bias[...] = pieces[4]()[rows : rows + bias.shape[0], :].astype(F32)


SLOTS = 4


def attn_fwd_body(slots, span, heads, first, scalars, loads, stores, k_scr, vt_scr, p_scr, sems):
    len_ref = scalars[0]
    count = len(slots)
    if first:
        x_in, wq_in, wk_in, wv_in, bias_in = loads
        bias = bias_in()
    else:
        pieces, (x_in, *near_mt, near_wo, small) = loads[:8], loads[8:]
    saved, stores = stores[: 6 * count], stores[6 * count :]
    if first:
        wq, wk, wv = wq_in(), wk_in(), wv_in()
    else:
        resid_out, low_out, lowt_out, *kept, bias_out = stores
        wq, wk, wv, wo = [store.buf for store in kept]
        bias = bias_out.buf
        assemble(scalars[1], pieces, wq, wk, wv, wo, bias)
        for store in kept:
            store.send()
    local = wq.shape[1]
    heads_a = groups_of(local)[0][1] // HD

    def save(at):
        number, head = at // heads, at % heads
        pa_hbm, pb_hbm = saved[6 * number + 4 : 6 * number + 6]
        dst = pa_hbm.at[head] if head < heads_a else pb_hbm.at[head - heads_a]
        return pltpu.make_async_copy(p_scr.at[at % SLOTS], dst, sems.at[at % SLOTS])

    for number, slot in enumerate(slots):
        q_out, kt_out, v_out, mt_out = saved[6 * number : 6 * number + 4]
        rs = slice(number * span, (number + 1) * span)
        x = x_in(number)[rs, :]
        query = (dot(x, wq[...]) + bias[0:1, :]).astype(BF16)
        q_out.buf[...] = query * jnp.asarray(HD**-0.5, BF16)
        k_scr[...] = dot(x, wk[...]).astype(BF16)
        v_out.buf[...] = (dot(x, wv[...]) + bias[1:2, :]).astype(BF16)
        kt_out.buf[...] = k_scr[...].T
        vt_scr[...] = v_out.buf[...].T
        if first:
            stores[number].buf[...] = x.T
            stores[number].send()
        for store in (q_out, kt_out, v_out):
            store.send()
        valid = lax.broadcasted_iota(jnp.int32, (span, span), 0) < len_ref[slot]
        def scores_of(head):
            cols = slice(head * HD, (head + 1) * HD)
            return dot_nt(k_scr[:, cols], q_out.buf[:, cols])

        scores = scores_of(0)
        for head in range(heads):
            at = number * heads + head
            cols = slice(head * HD, (head + 1) * HD)
            now = jnp.where(valid, scores, NEG_FILL)
            if head + 1 < heads:
                scores = scores_of(head + 1)
            top = jnp.max(now, axis=0, keepdims=True)
            weight = jnp.exp(now - top)
            total = jnp.sum(weight, axis=0, keepdims=True)
            probs = (weight * (1.0 / total)).astype(BF16)
            if at >= SLOTS:
                save(at - SLOTS).wait()
            p_scr[at % SLOTS] = probs
            save(at).start()
            mt_out.buf[cols, :] = dot(vt_scr[cols, :], probs).astype(BF16)
        mt_out.send()
        if not first:
            share = dot_tn(near_mt[number]()[...], near_wo()[...]) + dot_tn(mt_out.buf[...], wo[...])
            resid = x.astype(F32) + share + small()[0:1, :]
            unit, _ = norm_parts(resid)
            low = (unit * small()[1:2, :] + small()[2:3, :]).astype(BF16)
            resid_out.buf[rs, :] = resid
            low_out.buf[rs, :] = low
            lowt_out.buf[:, rs] = low.T
    for at in range(count * heads - SLOTS, count * heads):
        save(at).wait()


def attn_fwd(run, lengths, seqs, slots, x, own=None, far=None):
    rows, width = x.shape
    span = rows // seqs
    local = own[0].shape[1] if own else far[3].shape[0]
    heads = local // HD
    (_, extent_a), (_, extent_b) = groups_of(local)
    count = len(slots)
    tokens = pl.ds(slots[0] * span, count * span)
    x_in = Far(x, count, shape=(count * span, width), view=lambda ref, *_: ref.at[tokens, :])
    outs = []
    for _ in slots:
        outs += [
            FarOut((span, local), BF16),
            FarOut((local, span), BF16),
            FarOut((span, local), BF16),
            FarOut((local, span), BF16),
            Raw(shape=(extent_a // HD, span, span), dtype=BF16),
            Raw(shape=(extent_b // HD, span, span), dtype=BF16),
        ]
    if own:
        *weights, bias = own
        ins = [x_in, *map(Far, weights), bias]
        outs += [FarOut((width, span), BF16)] * count
        scalars = (lengths,)
    else:
        spot, pieces, near_mt, near_wo, small = far
        ins = [p if at in (3, 7) else Far(p) for at, p in enumerate(pieces)]
        ins += [x_in, *map(Far, near_mt), Far(near_wo), small]
        outs += [((rows, width), F32), ((rows, width), BF16), ((width, rows), BF16)]
        outs += [FarOut((width, local), BF16)] * 3 + [FarOut((local, width), BF16)]
        outs.append(((16, local), F32))
        scalars = (lengths, spot)
    results = run(
        functools.partial(attn_fwd_body, slots, span, heads, bool(own)),
        "attn_fwd",
        ins,
        outs,
        scratch=[
            pltpu.VMEM((span, local), BF16),
            pltpu.VMEM((local, span), BF16),
            pltpu.VMEM((SLOTS, span, span), BF16),
            pltpu.SemaphoreType.DMA((SLOTS,)),
        ],
        limit=14 if own else 24,
        scalars=scalars,
        cost=8 if own else 6,
    )
    saved = [results[6 * number : 6 * number + 6] for number in range(count)]
    return (saved, *results[6 * count :])


def norm_parts(resid):
    center = resid - jnp.mean(resid, -1, keepdims=True)
    spread = jnp.mean(center * center, -1, keepdims=True)
    rstd = lax.rsqrt(spread + EPSILON)
    return center * rstd, rstd


def norm_back(unit, rstd, gain, grad):
    scaled = grad * gain
    return rstd * (
        scaled
        - jnp.mean(scaled, -1, keepdims=True)
        - unit * jnp.mean(scaled * unit, -1, keepdims=True)
    )


def ln2_body(seqs, scalars, loads, stores):
    res1, ffn, og, small, pg = loads
    out_st, pool, dres, dlow, dlowt, sums_st = stores
    len_ref = scalars[0]
    small = small()
    rows = res1.buf.shape[0]
    span = rows // seqs
    tile = span // 4
    sums = [0.0, 0.0, 0.0]
    gain = small[4:5, :]
    for seq in range(seqs):
        length = len_ref[seq]
        count = length.astype(F32)
        total = 0.0
        spread = pg()[seq : seq + 1, :] / count
        for part in range(4):
            at = 4 * seq + part
            rs = slice(at * tile, (at + 1) * tile)
            unit_one, _ = norm_parts(res1(at)[rs, :])
            hidden = unit_one * small[1:2, :] + small[2:3, :]
            resid = hidden + ffn()[rs, :] + small[3:4, :]
            unit, rstd = norm_parts(resid)
            out = unit * gain + small[5:6, :]
            out_st.buf[rs, :] = out.astype(BF16)
            out_st.send(at)
            valid = lax.broadcasted_iota(jnp.int32, resid.shape, 0) + part * tile < length
            total = total + jnp.sum(jnp.where(valid, out, 0.0), 0, keepdims=True)
            d_out = og(at)[rs, :].astype(F32) + jnp.where(valid, spread, 0.0)
            d_resid = norm_back(unit, rstd, gain, d_out)
            dres.buf[rs, :] = d_resid
            dres.send(at)
            low = d_resid.astype(BF16)
            dlow.buf[rs, :] = low
            dlowt.buf[:, rs] = low.T
            for row, term in enumerate((d_resid, d_out * unit, d_out)):
                sums[row] = sums[row] + jnp.sum(term, 0, keepdims=True)
        pool.buf[seq : seq + 1, :] = total / count
    sums_st.buf[...] = jnp.zeros_like(sums_st.buf)
    for row in range(3):
        sums_st.buf[row : row + 1, :] = sums[row]


def ln2(run, lengths, res1, ffn, small, out_grad, pool_grad):
    rows, width = res1.shape
    seqs = lengths.shape[0]
    return run(
        functools.partial(ln2_body, seqs),
        "ln2",
        [res1, ffn, out_grad, small, pool_grad],
        [
            FarOut((rows, width), BF16, 4 * seqs),
            ((seqs, width), F32),
            FarOut((rows, width), F32, 4 * seqs),
            ((rows, width), BF16),
            ((width, rows), BF16),
            ((8, width), F32),
        ],
        scalars=(lengths,),
        limit=12,
        cost=6,
    )


def gelu_pair(pre):
    bell = jnp.exp(pre * pre * -0.5)
    t = 1.0 / (1.0 + (0.3275911 * SQRT_HALF) * jnp.abs(pre))
    poly = 0.5 * 1.061405429
    poly = poly * t + 0.5 * -1.453152027
    poly = poly * t + 0.5 * 1.421413741
    poly = poly * t + 0.5 * -0.284496736
    poly = poly * t + 0.5 * 0.254829592
    tail = poly * t * bell
    phi = jnp.where(pre >= 0.0, 1.0 - tail, tail)
    return pre * phi, phi + pre * bell * INV_SQRT_2PI


ROW_TILE = 256


def ffn_fwd_body(own, scalars, loads, stores, bias_scr):
    spot_ref = scalars[0]
    h, bias, *loads = loads
    h, bias = h(), bias()
    acts, ders, (acc_out, *kept) = stores[:2], stores[2:4], stores[4:]
    acc = acc_out.buf
    units = bias.shape[1]
    rows, width = h.shape
    tiles = [slice(at, at + ROW_TILE) for at in range(0, rows, ROW_TILE)]
    for step in range(2):
        if own:
            half = pl.ds(pl.multiple_of((spot_ref[0] ^ step) * 2 * units, 2 * units), 2 * units)
            wu, wd = loads[0]().at[:, half], loads[1]().at[half, :]
        else:
            pieces, part = loads[:8], loads[8]
            wu, wd = kept[step].buf, kept[2 + step].buf
            for flip in range(2):
                at = pl.ds(pl.multiple_of((spot_ref[1] ^ flip) * units, units), units)
                wu[:, at] = pieces[4 * step + flip]()[...]
                at = pl.ds(pl.multiple_of((spot_ref[2] ^ flip) * units, units), units)
                wd[at, :] = pieces[4 * step + 2 + flip]()[...]
        spot = spot_ref[0] ^ step
        bias_scr[:, :units] = bias[pl.ds(2 + 2 * spot, 1), :]
        bias_scr[:, units:] = bias[pl.ds(3 + 2 * spot, 1), :]

        def down(at, act):
            share = dot(act, wd[...])
            if step == 0 and own:
                acc[tiles[at], :] = share
            elif step == 0:
                acc[tiles[at], :] = part()[tiles[at], :] + share
            else:
                acc[tiles[at], :] += share

        pre = dot(h[tiles[0], :], wu[...]) + bias_scr[...]
        before = None
        for at, rs in enumerate(tiles):
            now = pre
            if at + 1 < len(tiles):
                pre = dot(h[tiles[at + 1], :], wu[...]) + bias_scr[...]
            act, der = gelu_pair(now)
            act = act.astype(BF16)
            acts[step].buf[rs, :] = act
            ders[step].buf[rs, :] = der.astype(BF16)
            if before is not None:
                down(at - 1, before)
            before = act
        down(len(tiles) - 1, before)
        acts[step].send()
        ders[step].send()


def half_view(axis, units, which):
    def view(ref, spot_ref):
        at = pl.ds(pl.multiple_of((spot_ref[0] ^ which) * units, units), units)
        return ref.at[:, at] if axis else ref.at[at, :]

    return view


def ffn_fwd(run, spot, h, bias, wu=None, wd=None, pieces=(), part=None):
    rows, width = h.shape
    own = wu is not None
    units = 2 * bias.shape[1]
    ins = [h, bias]
    if own:
        ins += [wu, wd]
    else:
        ins += [p if at in (5, 7) else Far(p) for at, p in enumerate(pieces)] + [part]
    block = ((rows, units), BF16)
    away = FarOut((rows, units), BF16)
    act = away if own else block
    outs = [act, act, block if own else away, block, ((rows, width), F32)]
    if not own:
        outs += [((width, units), BF16)] * 2 + [((units, width), BF16)] * 2
    results = run(
        functools.partial(ffn_fwd_body, own),
        "ffn_fwd",
        ins,
        outs,
        scratch=[pltpu.VMEM((1, units), F32)],
        scalars=(spot,),
        limit=14,
        cost=10,
    )
    return (results[0:2], results[2:4], *results[4:])


def split_out(x_bit, row_half, value, away, mine):
    @pl.when(x_bit == row_half)
    def _():
        mine[...] = value

    @pl.when(x_bit != row_half)
    def _():
        away[...] = value


def down_send_body(scalars, loads, stores):
    dft, far, own = loads
    for at, act in enumerate((far, own)):
        stores[0].buf[at] = dot(dft()[...], act()[...]).astype(BF16)


def down_send(run, dft, far_act, own_act):
    width, rows = dft.shape
    units = far_act[0].shape[1]
    return run(
        down_send_body,
        "down_send",
        [dft, far_act[1], Far(own_act[1])],
        [((2, width, units), BF16)],
        cost=3,
    )


def down_keep_body(scalars, loads, stores):
    dft, far, own, got = loads
    far_left, away, far_right, own_left_away, own_left, own_right = [store.buf for store in stores]
    x_bit = scalars[0][1]
    rows, half = far_right.shape
    for which, act in enumerate((far, own)):
        for part in range(2):
            rs = slice(part * rows, (part + 1) * rows)
            total = dot(dft()[rs, :], act()[...]) + got(which)[which, rs, :].astype(F32)
            low = total.astype(BF16)
            left, right = low[:, :half], low[:, half:]
            if which == 0:
                far_left[rs, :] = left
                split_out(x_bit, part, right, away.at[0], far_right)
            else:
                split_out(x_bit, part, left, own_left_away, own_left)
                split_out(x_bit, part, right, away.at[1], own_right)


def down_keep(run, spot, dft, far_act, own_act, got):
    width, rows = dft.shape
    units = far_act[0].shape[1]
    half = units // 2
    small = ((width // 2, half), BF16)
    return run(
        down_keep_body,
        "down_keep",
        [dft, far_act[0], Far(own_act[0]), got],
        [((width, half), BF16), ((2, width // 2, half), BF16), small, small, small, small],
        scalars=(spot,),
        limit=10,
        cost=5,
    )


def ffn_bwd_body(mode, wd_view, scalars, loads, stores):
    wd, der, df, ht, *got = loads
    wd = wd() if wd_view is None else wd_view(wd(), scalars[0])
    dpre, sums, *outs = [store.buf for store in stores]
    dpre_out = stores[0]
    rows = df.buf.shape[0]
    width = ht.buf.shape[0]
    tile = rows // 4
    bias = jnp.zeros((1, dpre.shape[1]), F32)
    tiles = [slice(at * tile, (at + 1) * tile) for at in range(4)]
    d_act = dot_nt(df()[tiles[0], :], wd[...])
    for at, rs in enumerate(tiles):
        now = d_act
        if at + 1 < len(tiles):
            d_act = dot_nt(df()[tiles[at + 1], :], wd[...])
        d_pre = (der()[rs, :].astype(F32) * now).astype(BF16)
        dpre[rs, :] = d_pre
        bias = bias + jnp.sum(d_pre.astype(F32), 0, keepdims=True)
    dpre_out.send()
    sums[...] = jnp.broadcast_to(bias, sums.shape)
    half = width // 2
    x_bit = scalars[0][1]
    for part in range(2):
        rs = slice(part * half, (part + 1) * half)
        total = dot(ht()[rs, :], dpre[...])
        if mode == "send":
            outs[0][rs, :] = total.astype(BF16)
            continue
        low = (total + got[0]()[rs, :].astype(F32)).astype(BF16)
        left, right = low[:, :half], low[:, half:]
        if mode == "far":
            outs[0][rs, :] = left
            split_out(x_bit, part, right, outs[1], outs[2])
        else:
            split_out(x_bit, part, left, outs[0], outs[1])
            split_out(x_bit, part, right, outs[2].at[1], outs[3])
    if mode == "own":
        outs[2][0] = got[1]()[...]


def ffn_bwd(run, mode, spot, df, ht, der, which, wd, wd_view, got=()):
    rows, width = df.shape
    units = der[which].shape[1]
    der_in = Far(der[which]) if not wd_view and which == 0 else der[which]
    ins = [Far(wd) if mode == "far" else wd, der_in, df, Far(ht) if mode == "far" else ht]
    outs = [FarOut((rows, units), BF16) if mode == "send" else ((rows, units), BF16), ((8, units), F32)]
    small = ((width // 2, units // 2), BF16)
    if mode == "send":
        outs += [((width, units), BF16)]
    elif mode == "far":
        outs += [((width, units // 2), BF16), small, small]
    else:
        outs += [small, small, ((2, width // 2, units // 2), BF16), small]
    ins += got
    return run(
        functools.partial(ffn_bwd_body, mode, wd_view),
        "ffn_bwd",
        ins,
        outs,
        scalars=(spot,),
        limit=10,
        cost=5,
    )


def hidden_back_body(scalars, loads, stores, acc_scr):
    (*pairs, resid_in, dres2_in, small) = loads
    dres, dlow, sums_out = stores
    sums = sums_out.buf
    small = small()
    rows = acc_scr.shape[0]
    tile = rows // 4
    tiles = [slice(at * tile, (at + 1) * tile) for at in range(4)]
    for pair in range(3):
        d_pre, weight = pairs[2 * pair](), pairs[2 * pair + 1]()
        for rs in tiles:
            share = dot_nt(d_pre[rs, :], weight[...])
            acc_scr[rs, :] = share if pair == 0 else acc_scr[rs, :] + share
    d_pre, weight = pairs[6](), pairs[7]()
    for at, rs in enumerate(tiles):
        d_hidden = acc_scr[rs, :] + dot_nt(d_pre[rs, :], weight[...]) + dres2_in(at)[rs, :]
        unit, rstd = norm_parts(resid_in(at)[rs, :])
        d_resid = norm_back(unit, rstd, small[1:2, :], d_hidden)
        dres.buf[rs, :] = d_resid
        dres.send(at)
        dlow.buf[rs, :] = d_resid.astype(BF16)
        for row, term in enumerate((d_resid, d_hidden * unit, d_hidden)):
            total = jnp.sum(term, 0, keepdims=True)
            if at == 0:
                sums[row : row + 1, :] = total
            else:
                sums[row : row + 1, :] += total


def hidden_back(run, spot, d_pres, wu, wu_far, resid, d_res2, small):
    rows, width = resid.shape
    units = wu.shape[1] // 2
    keep, send, far_keep, far_send = d_pres
    near = [Far(wu, shape=(width, units), view=half_view(1, units, which)) for which in range(2)]
    ins = [far_keep, wu_far[0], keep, near[0], Far(far_send), wu_far[1], Far(send), near[1]]
    return run(
        hidden_back_body,
        "hidden_back",
        ins + [resid, Far(d_res2, 4), small],
        [FarOut((rows, width), F32, 4), ((rows, width), BF16), ((8, width), F32)],
        scalars=(spot,),
        scratch=[pltpu.VMEM((rows, width), F32)],
        limit=22,
        cost=8,
    )


def attn_bwd_body(slots, begin, extent, last, scalars, loads, stores, *scratch):
    wo, da, *loads = [load() for load in loads]
    scale = HD**-0.5
    heads = extent // HD
    width = da.shape[1]
    count = len(slots)
    outs = stores[:count]
    span = loads[0].shape[0]
    mixed = []
    for slot in slots:
        d_attn = da[slot * span : (slot + 1) * span, :]
        mixed.append(dot_nt(d_attn, wo[begin : begin + extent, :]).astype(BF16))
    for number in range(count):
        q, kt, v, probs_ref = loads[4 * number : 4 * number + 4]
        out = outs[number].buf
        d_query = []
        for head in range(heads):
            cols = slice(begin + head * HD, begin + (head + 1) * HD)
            d_mixed_h = mixed[number][:, head * HD : (head + 1) * HD]
            d_probs = dot_nt(v[:, cols], d_mixed_h)
            low_probs = probs_ref[head]
            probs = low_probs.astype(F32)
            inner = jnp.sum(d_probs * probs, axis=0, keepdims=True)
            d_scores = (probs * (d_probs - inner)).astype(BF16)
            at = extent + head * HD
            out[:, at : at + HD] = dot(d_scores, q[:, cols]).astype(BF16)
            at = 2 * extent + head * HD
            out[:, at : at + HD] = dot(low_probs, d_mixed_h).astype(BF16)
            d_query.append((dot(kt[cols, :], d_scores) * scale).astype(BF16))
        out[:, :extent] = jnp.concatenate(d_query, 0).T
        outs[number].send()
    if not last:
        return
    before = loads[4 * count :]
    seqs = da.shape[0] // span
    mts, xts, before = before[:seqs], before[seqs : 2 * seqs], before[2 * seqs :]
    grads = [*before, *[store.buf for store in outs]]
    keep, send, sums = [store.buf for store in stores[count:]]
    (fold_scr,) = scratch
    core = scalars[0][0]
    g_out = None
    for slot, mt in enumerate(mts):
        share = dot(mt[begin : begin + extent, :], da[slot * span : (slot + 1) * span, :])
        g_out = share if g_out is None else g_out + share
    g_out = g_out.astype(BF16)
    for part in range(width // extent):
        fold_scr[part * extent : (part + 1) * extent, :] = g_out[:, part * extent : (part + 1) * extent]
    half = width // 2
    for part in range(2):
        rs = slice(part * half, (part + 1) * half)
        total = None
        for xt, grad in zip(xts, grads):
            share = dot(xt[rs, :], grad[...])
            total = share if total is None else total + share
        low = total.astype(BF16)

        def put(ref, low=low, rs=rs):
            ref[:, : 3 * extent] = low
            ref[:, 3 * extent :] = fold_scr[rs, :]

        @pl.when(core == part)
        def _(put=put):
            put(keep)

        @pl.when(core != part)
        def _(put=put):
            put(send)

    total = 0.0
    for grad in grads:
        total = total + jnp.sum(grad[...].astype(F32), 0, keepdims=True)
    sums[...] = jnp.broadcast_to(total, sums.shape)


def attn_bwd(run, group, spot, slots, d_attn, wo, xts, saved, before=()):
    rows, width = d_attn.shape
    begin, extent = group
    span = rows // len(xts)
    last = slots[-1] == len(xts) - 1
    ins = [wo, d_attn]
    for slot in slots:
        q, kt, v, _, probs_a, probs_b = saved[slot]
        ins += [q, kt, v, probs_a if begin == 0 else probs_b]
    outs = [FarOut((span, 3 * extent), BF16)] * len(slots)
    if last:
        ins += [saved[slot][3] for slot in range(len(xts))] + list(xts) + list(map(Far, before))
        outs += [
            ((width // 2, 4 * extent), BF16),
            ((width // 2, 4 * extent), BF16),
            ((8, 3 * extent), F32),
        ]
    return run(
        functools.partial(attn_bwd_body, slots, begin, extent, last),
        "attn_bwd",
        ins,
        outs,
        scalars=(spot,),
        scratch=[pltpu.VMEM((width, extent), BF16)] if last else [],
        limit=10,
        cost=6,
    )


def tokens_back_body(groups, seqs, scalars, loads, stores):
    wq, wk, wv, *grads, before = loads
    (out,) = stores
    span = out.buf.shape[0] // seqs
    for number, (begin, extent) in enumerate(groups):
        last = number == len(groups) - 1
        for slot in range(seqs):
            rs = slice(slot * span, (slot + 1) * span)
            grad = grads[number * seqs + slot]()
            total = None
            for mat, weight in enumerate((wq, wk, wv)):
                share = dot_nt(
                    grad[:, mat * extent : (mat + 1) * extent], weight()[:, begin : begin + extent]
                )
                total = share if total is None else total + share
            total = total + (out.buf[rs, :] if number else before(slot)[rs, :])
            out.buf[rs, :] = total
            if last:
                out.send(slot)


def tokens_back(run, groups, seqs, before, weights, grads):
    rows, width = before.shape
    return run(
        functools.partial(tokens_back_body, groups, seqs),
        "tokens_back",
        [Far(a) for a in (*weights, *grads)] + [Far(before, seqs)],
        [FarOut((rows, width), F32, seqs)],
        limit=16,
        cost=3,
    )


def collect_body(scalars, loads, stores):
    keep, send, one, two, a_sums, b_sums = [load() for load in loads]
    out = stores[0].buf
    core = scalars[0][0]
    out[...] = jnp.zeros_like(out)
    out[pl.ds(core, 1), :] = keep[0:1, :]
    out[pl.ds(1 - core, 1), :] = send[0:1, :]
    extent_a, extent_b = a_sums.shape[1] // 3, b_sums.shape[1] // 3
    local = extent_a + extent_b
    for at, mat in enumerate((0, 2)):
        begin = at * local
        out[2:3, begin : begin + extent_a] = a_sums[0:1, mat * extent_a : (mat + 1) * extent_a]
        out[2:3, begin + extent_a : begin + local] = b_sums[0:1, mat * extent_b : (mat + 1) * extent_b]
    out[3:6, :] = one[0:3, :]
    out[6:9, :] = two[0:3, :]


def collect(run, spot, *sums):
    return run(collect_body, "collect", list(sums), [((16, sums[2].shape[1]), F32)], scalars=(spot,))


def finish_attn_body(groups, scalars, loads, stores, full_scr, fold_scr, go_scr, sems):
    core = scalars[0][0]
    pairs = [[load() for load in loads[:2]], [load() for load in loads[2:]]]
    rows = pairs[0][0].shape[0]
    local, width = go_scr.shape
    copies = []

    def ship(src, dst):
        copies.append(pltpu.make_async_copy(src, dst, sems.at[len(copies)]))
        copies[-1].start()

    for mat in range(4):
        for (begin, extent), pair in zip(groups, pairs):
            for flip, ref in enumerate(pair):
                at = pl.ds(pl.multiple_of((core ^ flip) * rows, rows), rows)
                value = ref[:, mat * extent : (mat + 1) * extent]
                if mat < 3:
                    full_scr[mat, at, begin : begin + extent] = value.astype(F32)
                else:
                    fold_scr[at, begin : begin + extent] = value
        if mat < 3:
            ship(full_scr.at[mat], stores[mat])
    for begin, extent in groups:
        for part in range(width // extent):
            cols = slice(part * extent, (part + 1) * extent)
            go_scr[begin : begin + extent, cols] = fold_scr[cols, begin : begin + extent].astype(F32)
        ship(go_scr.at[begin : begin + extent, :], stores[3].at[begin : begin + extent, :])
    for copy in copies:
        copy.wait()


def finish_attn(run, groups, local, spot, *pieces):
    width = 2 * pieces[0].shape[0]
    return run(
        functools.partial(finish_attn_body, groups),
        "finish_attn",
        list(pieces),
        [Raw(shape=(width, local), dtype=F32)] * 3 + [Raw(shape=(local, width), dtype=F32)],
        scratch=[
            pltpu.VMEM((3, width, local), F32),
            pltpu.VMEM((width, local), BF16),
            pltpu.VMEM((local, width), F32),
            pltpu.SemaphoreType.DMA((3 + len(groups),)),
        ],
        scalars=(spot,),
        limit=10,
        cost=0.2,
    )


def finish_body(kind, scalars, loads, stores, scr, sems):
    mine, other = [load() for load in loads]
    (out,) = stores
    width, units = mine.shape
    parts = 2
    extent = units // parts
    copies = []
    for flip, ref in enumerate((mine, other)):
        for part in range(parts):
            at = flip * parts + part
            begin = pl.multiple_of((scalars[0][0] ^ flip) * units + part * extent, extent)
            value = ref[:, part * extent : (part + 1) * extent].astype(F32)
            scr[at] = value if kind == "up" else value.T
            place = pl.ds(begin, extent)
            dst = out.at[:, place] if kind == "up" else out.at[place, :]
            copies.append(pltpu.make_async_copy(scr.at[at], dst, sems.at[at]))
            copies[-1].start()
    for copy in copies:
        copy.wait()


def finish(run, kind, spot, mine, other):
    width, units = mine.shape
    shape = (width, 2 * units) if kind == "up" else (2 * units, width)
    piece = (width, units // 2) if kind == "up" else (units // 2, width)
    return run(
        functools.partial(finish_body, kind),
        "finish_" + kind,
        [mine, other],
        [Raw(shape=shape, dtype=F32)],
        scratch=[pltpu.VMEM((4, *piece), F32), pltpu.SemaphoreType.DMA((4,))],
        scalars=(spot,),
        limit=8,
        cost=0.2,
    )


def add(*terms):
    total = terms[0].astype(F32)
    for term in terms[1:]:
        total = total + term.astype(F32)
    return total.astype(BF16)


def local(
    n_batch,
    tokens,
    lengths,
    w_query,
    b_query,
    w_key,
    w_value,
    b_value,
    w_out,
    b_out,
    gain_one,
    shift_one,
    w_up,
    b_up,
    w_down,
    b_down,
    gain_two,
    shift_two,
    out_grad,
    pool_grad,
):
    rows, width = tokens.shape
    seqs = lengths.shape[0]
    half = w_query.shape[1]
    groups = groups_of(half)
    place = lax.axis_index("batch").astype(jnp.int32)
    core, x_bit, z_low, z_high = [(place >> bit) & 1 for bit in range(4)]
    spot = jnp.stack([core, x_bit, z_low])
    run = Kernels()

    def swap(array, bit):
        return lax.ppermute(array, "batch", [(i, i ^ bit) for i in range(n_batch)])

    def swap_core(array):
        return swap(array, 1)

    def swap_x(array):
        return swap(array, 2)

    def swap_y(array):
        return lax.ppermute(array, "tensor", [(0, 1), (1, 0)])

    bias_rows = jnp.concatenate([b_query, b_value, b_up]).reshape(-1, half)
    bias_rows = jnp.pad(bias_rows, ((0, 16 - bias_rows.shape[0]), (0, 0)))
    own_bias = bias_rows.astype(F32)
    small = jnp.stack([b_out, gain_one, shift_one, b_down, gain_two, shift_two]).astype(F32)
    ex, ez = pack(run, spot, w_query, w_key, w_value, w_out, bias_rows)
    ex, ez = swap_y(ex), swap_y(ez)
    fx, fz = pack_units(run, spot, w_up, w_down, half)
    fx, fz = swap_y(fx), swap_y(fz)
    own_saved, xts = [], []
    own = (w_query, w_key, w_value, own_bias)
    for slot in range(seqs):
        saved, xt = attn_fwd(run, lengths, seqs, (slot,), tokens, own=own)
        own_saved += saved
        xts.append(xt)
        if slot == 0:
            ex, ez = run.wait(ex, ez)
            ex_x, ez_z = swap_x(ex), swap(ez, 4)
            ex_c, ez_c = swap_core(ex), swap_core(ez)
    ex_x, ez_z, ex_c, ez_c, fx = run.wait(ex_x, ez_z, ex_c, ez_c, fx)
    ex_xc, ez_zc = swap_core(ex_x), swap_core(ez_z)
    fx_x, fx_c = swap_x(fx), swap_core(fx)
    pieces = (ex, ex_x, ex_c, ex_xc, ez, ez_z, ez_c, ez_zc)
    near_mt = [saved[3] for saved in own_saved]
    far_saved, resid_one, hidden, hidden_t, far_q, far_k, far_v, far_o, far_bias = attn_fwd(
        run, lengths, seqs, tuple(range(seqs)), tokens, far=(spot, pieces, near_mt, w_out, small)
    )
    fz, fx_x, fx_c = run.wait(fz, fx_x, fx_c)
    fz_z, fz_c = swap(fz, 4), swap_core(fz)
    fx_xc = swap_core(fx_x)
    own_act, own_der, ffn_part = ffn_fwd(run, spot, hidden, own_bias, wu=w_up, wd=w_down)
    fx_xc, fz_z, fz_c = run.wait(fx_xc, fz_z, fz_c)
    fz_zc = swap_core(fz_z)
    far_act, far_der, ffn_sum, *far_weights = ffn_fwd(
        run,
        spot,
        hidden,
        far_bias,
        pieces=(fx, fx_x, fz, fz_z, fx_c, fx_xc, fz_c, fz_zc),
        part=ffn_part,
    )
    wu_far, wd_far = far_weights[:2], far_weights[2:]
    output, pooled, d_resid_two, d_ffn, d_ffn_t, sums_two = ln2(
        run, lengths, resid_one, ffn_sum, small, out_grad, pool_grad
    )

    def pick(array, at):
        return lax.dynamic_index_in_dim(array, at, 0, keepdims=False)

    def halves(array):
        return array.reshape(2, array.shape[0] // 2, array.shape[1])

    def split(bit, *terms):
        parts = [halves(t) for t in terms]
        return add(*[pick(t, 1 - bit) for t in parts]), add(*[pick(t, bit) for t in parts])

    def join(bit, mine, got):
        return jnp.concatenate(
            [jnp.where(bit == 0, mine, got), jnp.where(bit == 0, got, mine)], axis=0
        )

    def rest(array):
        bit = 16
        while bit < n_batch:
            array = add(array, swap(array, bit))
            bit *= 2
        return array

    def cross_two(left_got, right_got, away, far):
        return swap_x(add(away, pick(halves(left_got), 1 - x_bit))), swap_y(add(far, right_got))

    def cross_three(left, left_got, left_x, right, right_x, right_y):
        mine = pick(halves(left_got), x_bit)
        return jnp.concatenate([add(left, mine, left_x), add(right, right_x, right_y)], axis=1)

    d_got = swap_core(run.wait(down_send(run, d_ffn_t, far_act, own_act)))
    bwd = functools.partial(ffn_bwd, run)
    dp_fs, bs_fs, u_send = bwd("send", spot, d_ffn, hidden_t, far_der, 1, wd_far[1], None)
    d_got, u_send = run.wait(d_got, u_send)
    uf_got = swap_core(u_send)
    df_left, d_away, df_right, do_left_away, do_left, do_right = down_keep(
        run, spot, d_ffn_t, far_act, own_act, d_got
    )
    df_left, d_away = run.wait(df_left, d_away)
    d_left_y, d_right_x = swap_y(df_left), swap_x(d_away)
    dp_os, bs_os, u_send = bwd("send", spot, d_ffn, hidden_t, own_der, 1, w_down, half_view(0, width, 1))
    uf_got, u_send = run.wait(uf_got, u_send)
    uo_got = swap_core(u_send)
    dp_fk, bs_fk, uf_left, uf_away, uf_right = bwd(
        "far", spot, d_ffn, hidden_t, far_der, 0, wd_far[0], None, (uf_got,)
    )
    uo_got, uf_left = run.wait(uo_got, uf_left)
    u_left_y = swap_y(uf_left)
    dp_ok, bs_ok, uo_left_away, uo_left, u_away, uo_right = bwd(
        "own", spot, d_ffn, hidden_t, own_der, 0, w_down, half_view(0, width, 0), (uo_got, uf_away)
    )
    d_left_y, d_right_x, u_away = run.wait(d_left_y, d_right_x, u_away)
    d_left_x, d_right_y = cross_two(d_left_y, d_right_x[0], do_left_away, df_right)
    u_right_x = swap_x(u_away)
    d_resid_one, d_attn, sums_one = hidden_back(
        run, spot, (dp_ok, dp_os, dp_fk, dp_fs), w_up, wu_far, resid_one, d_resid_two, small
    )

    first, others = (0,), tuple(range(1, seqs))
    far_bwd = functools.partial(
        attn_bwd, run, spot=spot, d_attn=d_attn, wo=far_o, xts=xts, saved=far_saved
    )
    own_bwd = functools.partial(
        attn_bwd, run, spot=spot, d_attn=d_attn, wo=w_out, xts=xts, saved=own_saved
    )
    d_left_x, d_right_y = run.wait(d_left_x, d_right_y)
    d_rows = cross_three(do_left, d_left_y, d_left_x, do_right, d_right_x[1], d_right_y)
    d_away, d_mine = split(z_low, d_rows)
    d_got = swap(d_away, 4)
    fa_0 = far_bwd(groups[0], slots=first)
    d_got = run.wait(d_got)
    d_away, d_mine = split(z_high, d_mine, d_got)
    d_got = swap(d_away, 8)
    *fa_1, fa_keep, fa_send, fa_sums = far_bwd(groups[0], slots=others, before=(fa_0,))
    d_got, u_left_y, u_right_x, fa_send = run.wait(d_got, u_left_y, u_right_x, fa_send)
    u_left_x, u_right_y = cross_two(u_left_y, u_right_x[0], uo_left_away, uf_right)
    fa_got = swap_core(fa_send)
    d_mine = rest(add(d_mine, d_got))
    d_got = swap(d_mine, 8)
    *fb, fb_keep, fb_send, fb_sums = far_bwd(groups[1], slots=first + others)
    fa_got, u_left_x, u_right_y, fb_send = run.wait(fa_got, u_left_x, u_right_y, fb_send)
    fa_y = swap_y(add(fa_keep, fa_got))
    u_rows = cross_three(uo_left, u_left_y, u_left_x, uo_right, u_right_x[1], u_right_y)
    u_away, u_mine = split(z_low, u_rows)
    u_got = swap(u_away, 4)
    fb_got = swap_core(fb_send)
    oa_0 = own_bwd(groups[0], slots=first)

    u_got, fb_got, d_got = run.wait(u_got, fb_got, d_got)
    u_away, u_mine = split(z_high, u_mine, u_got)
    u_got = swap(u_away, 8)
    d_mine = join(z_high, d_mine, d_got)
    d_got = swap(d_mine, 4)
    fb_y = swap_y(add(fb_keep, fb_got))
    sums_got = swap_y(collect(run, spot, bs_fk, bs_fs, sums_one, sums_two, fa_sums, fb_sums))
    *oa_1, oa_keep, oa_send, oa_sums = own_bwd(groups[0], slots=others, before=(oa_0,))
    u_got, d_got, fa_y, oa_send = run.wait(u_got, d_got, fa_y, oa_send)
    oa_got = swap_core(oa_send)
    u_mine = rest(add(u_mine, u_got))
    u_got = swap(u_mine, 8)
    d_mine = join(z_low, d_mine, d_got)
    d_got = swap_x(d_mine)
    *ob, ob_keep, ob_send, ob_sums = own_bwd(groups[1], slots=first + others)

    oa_got, u_got, fb_y, ob_send, sums_got = run.wait(oa_got, u_got, fb_y, ob_send, sums_got)
    ob_got = swap_core(ob_send)
    a_away, a_mine = split(x_bit, oa_keep, oa_got, fa_y)
    a_got = swap_x(a_away)
    u_mine = join(z_high, u_mine, u_got)
    u_got = swap(u_mine, 4)
    sums = collect(run, spot, bs_ok, bs_os, sums_one, sums_two, oa_sums, ob_sums) + sums_got
    ob_got = run.wait(ob_got)
    b_away, b_mine = split(z_low, ob_keep, ob_got, fb_y)
    b_got = swap(b_away, 4)
    sums_got = swap_x(sums)
    dx = tokens_back(run, groups, seqs, d_resid_one, (far_q, far_k, far_v), (fa_0, *fa_1, *fb))

    a_got, b_got, u_got, d_got, sums_got = run.wait(a_got, b_got, u_got, d_got, sums_got)
    a_away, a_mine = split(z_low, a_mine, a_got)
    a_got = swap(a_away, 4)
    b_away, b_mine = split(x_bit, b_mine, b_got)
    b_got = swap_x(b_away)
    d_mine = join(x_bit, d_mine, d_got)
    d_other = swap_core(d_mine)
    u_mine = join(z_low, u_mine, u_got)
    sums = sums + sums_got
    sums_got = swap(sums, 1)
    d_other = run.wait(d_other)
    g_down = finish(run, "down", spot, d_mine, d_other)

    a_got, b_got, sums_got, u_mine = run.wait(a_got, b_got, sums_got, u_mine)
    a_mine = add(a_mine, a_got)
    a_got = swap(a_mine, 8)
    b_mine = add(b_mine, b_got)
    b_got = swap(b_mine, 8)
    u_got = swap_x(u_mine)
    sums = sums + sums_got
    sums_got = swap(sums, 4)
    d_tokens = tokens_back(run, groups, seqs, dx, (w_query, w_key, w_value), (oa_0, *oa_1, *ob))

    a_got, b_got, u_got, sums_got = run.wait(a_got, b_got, u_got, sums_got)
    a_mine = rest(add(a_mine, a_got))
    a_got = swap(a_mine, 4)
    b_mine = rest(add(b_mine, b_got))
    b_got = swap_x(b_mine)
    u_mine = join(x_bit, u_mine, u_got)
    u_other = swap_core(u_mine)
    sums = sums + sums_got
    sums_got = swap(sums, 8)
    u_other = run.wait(u_other)
    g_up = finish(run, "up", spot, u_mine, u_other)

    a_got, b_got, sums_got = run.wait(a_got, b_got, sums_got)
    a_mine = join(z_low, a_mine, a_got)
    a_got = swap_x(a_mine)
    b_mine = join(x_bit, b_mine, b_got)
    b_got = swap(b_mine, 4)
    sums = sums + sums_got
    bit = 16
    while bit < n_batch:
        sums = sums + swap(sums, bit)
        bit *= 2
    a_got, b_got, sums = run.wait(a_got, b_got, sums)
    a_mine = join(x_bit, a_mine, a_got)
    a_other = swap_core(a_mine)
    b_mine = join(z_low, b_mine, b_got)
    b_other = swap_core(b_mine)
    a_other, b_other = run.wait(a_other, b_other)
    g_query, g_key, g_value, g_out = finish_attn(
        run, groups, half, spot, a_mine, a_other, b_mine, b_other
    )

    g_bias_up = sums[0:2].reshape(-1)
    g_bias_query, g_bias_value = sums[2, :half], sums[2, half:]
    d_bias_out, d_gain_one, d_shift_one, d_bias_down, d_gain_two, d_shift_two = [sums[3 + i] for i in range(6)]
    return (
        output,
        pooled,
        d_tokens,
        g_query,
        g_bias_query,
        g_key,
        g_value,
        g_bias_value,
        g_out,
        d_bias_out,
        d_gain_one,
        d_shift_one,
        g_up,
        g_bias_up,
        g_down,
        d_bias_down,
        d_gain_two,
        d_shift_two,
    )


def solution(mesh):
    return jax.shard_map(
        functools.partial(local, mesh.shape["batch"]),
        mesh=mesh,
        in_specs=(
            P(("batch", "tensor"), None),
            P(("batch", "tensor")),
            P(None, "tensor"),
            P("tensor"),
            P(None, "tensor"),
            P(None, "tensor"),
            P("tensor"),
            P("tensor", None),
            P(),
            P(),
            P(),
            P(None, "tensor"),
            P("tensor"),
            P("tensor", None),
            P(),
            P(),
            P(),
            P(("batch", "tensor"), None),
            P(("batch", "tensor"), None),
        ),
        out_specs=(
            P(("batch", "tensor"), None),
            P(("batch", "tensor"), None),
            P(("batch", "tensor"), None),
            P(None, "tensor"),
            P("tensor"),
            P(None, "tensor"),
            P(None, "tensor"),
            P("tensor"),
            P("tensor", None),
            P(),
            P(),
            P(),
            P(None, "tensor"),
            P("tensor"),
            P("tensor", None),
            P(),
            P(),
            P(),
        ),
        check_vma=False,
    )
```
